32 devices in a mesh: dp: 4 (over y, x), seq: 8 (over z, core).
Axes of the slice: x: 2, y: 2, z: 4, core: 2. Of those that a mesh axis runs over, the one named last changes fastest.
Arguments:
- tokens: bfloat16 [4, 2560, 2304], P('dp', 'seq'), may hold values from -6 to 6
- pre_attention: float32 [2304], replicated, may hold values from 0.25 to 1.75
- post_attention: float32 [2304], replicated, may hold values from 0.25 to 1.75
- pre_feedforward: float32 [2304], replicated, may hold values from 0.25 to 1.75
- post_feedforward: float32 [2304], replicated, may hold values from 0.25 to 1.75
- w_query: bfloat16 [2304, 2048], P(('dp', 'seq')), may hold values from -0.125 to 0.125
- key_weight: bfloat16 [2304, 1024], P(('dp', 'seq')), may hold values from -0.125 to 0.125
- value_weight: bfloat16 [2304, 1024], P(('dp', 'seq')), may hold values from -0.125 to 0.125
- w_output: bfloat16 [2048, 2304], P(('dp', 'seq')), may hold values from -0.125 to 0.125
- w_gate: bfloat16 [2304, 9216], P(('dp', 'seq')), may hold values from -0.125 to 0.125
- w_up: bfloat16 [2304, 9216], P(('dp', 'seq')), may hold values from -0.125 to 0.125
- w_down: bfloat16 [9216, 2304], P(('dp', 'seq')), may hold values from -0.0625 to 0.0625
- document_index: int32 [2, 5120], replicated, may hold values from 0 to 5, as said below
- token_padding_mask: int32 [2, 5120], replicated, may hold values 0 or 1
- cotangent: bfloat16 [4, 2560, 2304], P('dp', 'seq'), may hold values from -6 to 6
Outputs:
- output: float32 [4, 2560, 2304], P('dp', 'seq')
- tokens_grad: float32 [4, 2560, 2304], P('dp', 'seq')
- w_query_grad: float32 [2304, 2048], P(('dp', 'seq'))
- w_key_grad: float32 [2304, 1024], P(('dp', 'seq'))
- w_value_grad: float32 [2304, 1024], P(('dp', 'seq'))
- w_output_grad: float32 [2048, 2304], P(('dp', 'seq'))
- w_gate_grad: float32 [2304, 9216], P(('dp', 'seq'))
- w_up_grad: float32 [2304, 9216], P(('dp', 'seq'))
- w_down_grad: float32 [9216, 2304], P(('dp', 'seq'))
- pre_attention_grad: float32 [2304], P(('dp', 'seq'))
- post_attention_grad: float32 [2304], P(('dp', 'seq'))
- pre_feedforward_grad: float32 [2304], P(('dp', 'seq'))
- post_feedforward_grad: float32 [2304], P(('dp', 'seq'))
The draws below stay inside these ranges and needn't reach their ends.
Inputs may be any that keep to these rules, and one draw needn't show every extreme that they name: `document_index`: along each sequence the segment numbers start at 0, never fall, and end at 5.
All inputs are finite; a program needn't handle non-finite values.
Results may differ from the reference program's by a relative error of at most 0.018.
Values may be sent and summed in bfloat16 or wider, within the bound.
No kernel may reach another device: no remote copies, remote signals or barrier semaphores. Data moves between devices by JAX's collectives and lax.ppermute only.
A program may use at most 768 MiB of HBM per device.

```python
import math
import jax
import jax.numpy as jnp
from jax import lax

MODEL_DIM = 2304
FF = 9216
QUERY_HEADS = 8
KEY_VALUE_HEADS = 4
HEAD_DIM = 256
WINDOW = 4096
SEQUENCE_TOKENS = 5120
HALF = 2560
SPAN = 320
ROWS = 4
PACKED_COUNT = 2


def draw_document_index(key, part):
    key = jax.random.fold_in(key, 11)
    key_start, key_stop, key_cuts = jax.random.split(key, 3)
    position = jnp.arange(SEQUENCE_TOKENS, dtype=jnp.int32)[None, :]
    long_start = jax.random.randint(key_start, (PACKED_COUNT, 1), 4, SPAN)
    long_stop = jax.random.randint(key_stop, (PACKED_COUNT, 1), SEQUENCE_TOKENS - SPAN + 1, SEQUENCE_TOKENS)
    eligible = (position >= 1) & (position < long_start)
    scores = jax.random.randint(key_cuts, (PACKED_COUNT, SEQUENCE_TOKENS), 0, 1024) * SEQUENCE_TOKENS + position
    scores = jnp.where(eligible, scores, -1).astype(jnp.int32)
    top_scores, top_index = lax.top_k(scores, 3)
    third = top_scores[:, 2:3]
    cuts = eligible & (scores >= third)
    boundary = cuts | (position == long_start) | (position == long_stop)
    return jnp.cumsum(boundary.astype(jnp.int32), axis=1).astype(jnp.int32)


def with_ends(values, own_key, smallest, top_value):
    place = [jax.random.randint(jax.random.fold_in(own_key, axis), (), 0, length) for axis, length in enumerate(values.shape)]
    longest = values.shape.index(max(values.shape))
    neighbour = place[:longest] + [(place[longest] + 1) % values.shape[longest]] + place[longest + 1:]
    return values.at[tuple(place)].set(smallest).at[tuple(neighbour)].set(top_value)


def steps_of(stream_key, shape, shards, smallest, top_value):
    def one(axis_at, blocks):
        draws = jax.random.uniform(jax.random.fold_in(jax.random.fold_in(stream_key, 6), axis_at), (blocks,), jnp.float32, smallest / len(shards), top_value / len(shards))
        return jnp.repeat(jnp.exp(draws), shape[axis_at] // blocks).reshape((-1,) + (1,) * (len(shape) - axis_at - 1))

    factor_of = one(*shards[0])
    for cut in shards[1:]:
        factor_of = factor_of * one(*cut)
    return factor_of


def bell_draw(stream_key, extent, scale, limit, cuts=(), kind=jnp.bfloat16):
    entries = scale * jax.random.normal(stream_key, extent, jnp.float32)
    if cuts:
        entries = entries * steps_of(stream_key, extent, cuts, -0.22, 0.18)
    return jnp.clip(entries, -limit, limit).astype(kind)


def setup_inputs(seed: int = 0) -> dict:
    seeds = jax.random.split(jax.random.key(seed), 16)
    tokens = bell_draw(seeds[0], (ROWS, HALF, MODEL_DIM), 1.0, 6.0, ((0, 4), (1, 8)))
    pre_attention = jnp.clip(1.0 + 0.15 * jax.random.normal(seeds[1], (MODEL_DIM,), jnp.float32), 0.25, 1.75)
    post_attention = jnp.clip(1.0 + 0.15 * jax.random.normal(seeds[2], (MODEL_DIM,), jnp.float32), 0.25, 1.75)
    pre_feedforward = jnp.clip(1.0 + 0.15 * jax.random.normal(seeds[3], (MODEL_DIM,), jnp.float32), 0.25, 1.75)
    post_feedforward = jnp.clip(1.0 + 0.15 * jax.random.normal(seeds[4], (MODEL_DIM,), jnp.float32), 0.25, 1.75)
    w_query = bell_draw(seeds[5], (MODEL_DIM, QUERY_HEADS * HEAD_DIM), MODEL_DIM ** -0.5, 0.125, ((0, 32),))
    key_weight = bell_draw(seeds[6], (MODEL_DIM, KEY_VALUE_HEADS * HEAD_DIM), MODEL_DIM ** -0.5, 0.125, ((0, 32),))
    value_weight = bell_draw(seeds[7], (MODEL_DIM, KEY_VALUE_HEADS * HEAD_DIM), MODEL_DIM ** -0.5, 0.125, ((0, 32),))
    w_output = bell_draw(seeds[8], (QUERY_HEADS * HEAD_DIM, MODEL_DIM), (QUERY_HEADS * HEAD_DIM) ** -0.5, 0.125, ((0, 32),))
    w_gate = bell_draw(seeds[9], (MODEL_DIM, FF), MODEL_DIM ** -0.5, 0.125, ((0, 32),))
    w_up = bell_draw(seeds[10], (MODEL_DIM, FF), MODEL_DIM ** -0.5, 0.125, ((0, 32),))
    w_down = bell_draw(seeds[11], (FF, MODEL_DIM), FF ** -0.5, 0.0625, ((0, 32),))
    document_index = draw_document_index(jax.random.fold_in(seeds[15], 71), 0)
    token_padding_mask = with_ends((jax.random.randint(seeds[13], (PACKED_COUNT, SEQUENCE_TOKENS), 0, 8) < 7).astype(jnp.int32), jax.random.fold_in(seeds[13], 1), 0, 1)
    cotangent = bell_draw(seeds[14], (ROWS, HALF, MODEL_DIM), 1.0, 6.0, ((0, 4), (1, 8)))
    return dict(tokens=tokens, pre_attention=pre_attention, post_attention=post_attention, pre_feedforward=pre_feedforward, post_feedforward=post_feedforward, w_query=w_query, key_weight=key_weight, value_weight=value_weight, w_output=w_output, w_gate=w_gate, w_up=w_up, w_down=w_down, document_index=document_index, token_padding_mask=token_padding_mask, cotangent=cotangent)


@jax.custom_vjp
def low(v):
    return lax.optimization_barrier(v.astype(jnp.bfloat16)).astype(jnp.float32)

@jax.custom_vjp
def low_back(v):
    return v

def low_keep(v):
    return (low(v), None)

def low_pass(kept, grad):
    return (grad,)

def back_keep(v):
    return (v, None)

def back_low(kept, grad):
    return (low(grad),)
low.defvjp(low_keep, low_pass)
low_back.defvjp(back_keep, back_low)
epsilon = 1e-06
softcap = 50.0
big_negative = -1e+30
highest = lax.Precision.HIGHEST

def normed(values, gain_vec):
    inv_rms = lax.rsqrt(lax.optimization_barrier(jnp.mean(values * values, axis=-1, keepdims=True)) + epsilon)
    return values * inv_rms * gain_vec

def matmul(operand, other_operand):
    return jnp.dot(operand, other_operand, precision=highest, preferred_element_type=jnp.float32)

def attend_single_row(mapped):
    queries_row, single_key_row, single_value_row, segment_row, padding_row = mapped
    current_block = math.gcd(SEQUENCE_TOKENS, 512)
    block_count = SEQUENCE_TOKENS // current_block
    heads_of_key = single_key_row.reshape(SEQUENCE_TOKENS, KEY_VALUE_HEADS, HEAD_DIM)
    heads_of_value = single_value_row.reshape(SEQUENCE_TOKENS, KEY_VALUE_HEADS, HEAD_DIM)
    key_pos = jnp.arange(SEQUENCE_TOKENS)

    def attend_block(inner):
        block_of_query, query_segments, block_index = inner
        query_pos = block_index * current_block + jnp.arange(current_block)
        heads_of_query = block_of_query.reshape(current_block, KEY_VALUE_HEADS, QUERY_HEADS // KEY_VALUE_HEADS, HEAD_DIM)
        raw_scores = low_back(jnp.einsum('qhgd,khd->hgqk', heads_of_query, heads_of_key, precision=highest))
        capped = softcap * jnp.tanh(raw_scores * HEAD_DIM ** (-0.5) / softcap)
        allowed = segment_row[None, :] == query_segments[:, None]
        allowed = allowed & (key_pos[None, :] <= query_pos[:, None])
        allowed = allowed & (query_pos[:, None] - key_pos[None, :] < WINDOW)
        allowed = allowed & ((padding_row[None, :] == 1) | (key_pos[None, :] == query_pos[:, None]))
        allowed = allowed[None, None]
        masked = jnp.where(allowed, capped, big_negative)
        row_max = lax.optimization_barrier(jnp.max(masked, axis=-1, keepdims=True))
        weights = jnp.where(allowed, jnp.exp(masked - row_max), 0.0)
        row_total = lax.optimization_barrier(jnp.sum(weights, axis=-1, keepdims=True))
        probabilities = low(weights / row_total)
        result = jnp.einsum('hgqk,khd->qhgd', probabilities, heads_of_value, precision=highest)
        return result.reshape(current_block, QUERY_HEADS * HEAD_DIM)
    attended_rows = lax.map(jax.checkpoint(attend_block), (queries_row.reshape(block_count, current_block, QUERY_HEADS * HEAD_DIM), segment_row.reshape(block_count, current_block), jnp.arange(block_count)))
    return attended_rows.reshape(SEQUENCE_TOKENS, QUERY_HEADS * HEAD_DIM)

def layer(tokens, pre_attention, post_attention, pre_feedforward, post_feedforward, w_query, key_weight, value_weight, w_output, w_gate, w_up, w_down, document_index, token_padding_mask):
    inputs = tokens.reshape(-1, MODEL_DIM)
    normed_in = low(normed(inputs, pre_attention))
    query_rows_all = low(low_back(matmul(normed_in, w_query)))
    key_row_block = low(low_back(matmul(normed_in, key_weight)))
    value_row_block = low(low_back(matmul(normed_in, value_weight)))
    attended_output = lax.map(attend_single_row, (query_rows_all.reshape(PACKED_COUNT, SEQUENCE_TOKENS, QUERY_HEADS * HEAD_DIM), key_row_block.reshape(PACKED_COUNT, SEQUENCE_TOKENS, KEY_VALUE_HEADS * HEAD_DIM), value_row_block.reshape(PACKED_COUNT, SEQUENCE_TOKENS, KEY_VALUE_HEADS * HEAD_DIM), document_index, token_padding_mask))
    attended_output = low(low_back(attended_output.reshape(-1, QUERY_HEADS * HEAD_DIM)))
    attn_out = low_back(matmul(attended_output, w_output))
    residual = inputs + normed(attn_out, post_attention)
    normed_mid = low(normed(residual, pre_feedforward))
    gate_value = low_back(matmul(normed_mid, w_gate))
    up_value = low_back(matmul(normed_mid, w_up))
    hidden = low(jax.nn.gelu(gate_value, approximate=True) * up_value)
    down_out = low_back(matmul(hidden, w_down))
    result = residual + normed(down_out, post_feedforward)
    return result.reshape(tokens.shape)

def reference(tokens, pre_attention, post_attention, pre_feedforward, post_feedforward, w_query, key_weight, value_weight, w_output, w_gate, w_up, w_down, document_index, token_padding_mask, cotangent):
    as_floats = [item.astype(jnp.float32) for item in (tokens, pre_attention, post_attention, pre_feedforward, post_feedforward, w_query, key_weight, value_weight, w_output, w_gate, w_up, w_down)]

    def layer_fn(*floats_in):
        return layer(*floats_in, document_index, token_padding_mask)
    result, pullback = jax.vjp(layer_fn, *as_floats)
    gradients = pullback(cotangent.astype(jnp.float32))
    return (result, gradients[0], gradients[5], gradients[6], gradients[7], gradients[8], gradients[9], gradients[10], gradients[11], gradients[1], gradients[2], gradients[3], gradients[4])
```

```python
import functools

import jax
import jax.numpy as jnp
from jax import lax
from jax.experimental import pallas as pl
from jax.experimental.pallas import tpu as pltpu
from jax.sharding import PartitionSpec as P

KEY_VALUE_HEADS = 4
HEAD_DIM = 256
GROUP = 2
WINDOW = 4096
CHUNKS = 2

epsilon = 1e-06
softcap = 50.0
score_scale = HEAD_DIM ** (-0.5) / softcap
log2_scale = softcap * 1.4426950408889634
VMEM_LIMIT = 56 * 1024 * 1024
ANYWHERE = pl.BlockSpec(memory_space=pl.ANY)


def normed(values, gain_vec):
    inv_rms = lax.rsqrt(jnp.mean(values * values, axis=-1, keepdims=True) + epsilon)
    return values * inv_rms * gain_vec


def matmul(a, b):
    return jnp.dot(a, b, preferred_element_type=jnp.float32)


def matmul_t(a, b):
    return lax.dot_general(a, b, (((1,), (1,)), ((), ())), preferred_element_type=jnp.float32)


def inner_t(a, b):
    return lax.dot_general(a, b, (((0,), (0,)), ((), ())), preferred_element_type=jnp.float32)


def across(x, bits):
    return lax.ppermute(x, "dp", [(i, i ^ bits) for i in range(lax.axis_size("dp"))])


def swap_core(x):
    return lax.ppermute(x, "seq", [(i, i ^ 1) for i in range(lax.axis_size("seq"))])


def line_groups():
    count = lax.axis_size("seq")
    return [list(range(core, count, 2)) for core in (0, 1)]


def gather_line(x):
    return lax.all_gather(x, "seq", axis=0, axis_index_groups=line_groups())


def exchange_line(x, place):
    line = x.shape[0]
    parts = x
    for k in range(1, line):
        route = [
            (2 * i + core, 2 * ((i + k) % line) + core) for i in range(line) for core in (0, 1)
        ]
        moved = lax.ppermute(pick(x, 0, (place + k) % line), "seq", route)
        parts = put(parts, moved, (place + line - k) % line)
    return parts


def scatter_line(x):
    return lax.psum_scatter(x, "seq", scatter_dimension=0, axis_index_groups=line_groups())


def gather_quad_near(x):
    return across(x, 1), across(x, 2)


def gather_quad_far(one, two):
    half = one.shape[0] // 2
    return jnp.concatenate([across(two[:half], 1), across(one[half:], 2)], axis=0)


def gather_quad(x):
    one, two = gather_quad_near(x)
    return [x, one, two, gather_quad_far(one, two)]


def scatter_quad(parts):
    half = parts[0].shape[0] // 2
    low, high = [p[:half] for p in parts], [p[half:] for p in parts]
    from_one = across(jnp.stack([low[1], low[3]]), 1)
    from_two = across(jnp.stack([high[2], high[3]]), 2)
    low_rest = across(low[2] + from_one[1], 2)
    high_rest = across(high[1] + from_two[1], 1)
    f32 = jnp.float32
    return jnp.concatenate(
        [
            low[0].astype(f32) + from_one[0].astype(f32) + low_rest.astype(f32),
            high[0].astype(f32) + from_two[0].astype(f32) + high_rest.astype(f32),
        ],
        axis=0,
    )


def flip_order(x, bits):
    pairs = x.reshape((2, 2) + x.shape[1:])
    pairs = jnp.where(bits % 2 == 1, pairs[:, ::-1], pairs)
    pairs = jnp.where(bits // 2 == 1, pairs[::-1], pairs)
    return pairs.reshape(x.shape)


def exchange_quad(x, place):
    parts = flip_order(x, place)
    return exchange_quad_end([parts[0]] + [across(parts[k], k) for k in (1, 2, 3)], place)


def exchange_quad_end(parts, place):
    return flip_order(jnp.stack(parts), place)


def pick(x, axis, index):
    return lax.dynamic_index_in_dim(x, index, axis, keepdims=False)


def put(x, part, *index):
    for _ in index:
        part = part[None]
    return lax.dynamic_update_slice(x, part, index + (0,) * (x.ndim - len(index)))


def after(x, *others):
    def kernel(x_ref, *rest):
        rest[-1][...] = x_ref[...]

    return pl.pallas_call(
        kernel,
        in_specs=[pl.BlockSpec(memory_space=pltpu.VMEM)] + [ANYWHERE] * len(others),
        out_specs=pl.BlockSpec(memory_space=pltpu.VMEM),
        out_shape=jax.ShapeDtypeStruct(x.shape, x.dtype),
    )(x, *others)


def empty(shape, dtype):
    return pl.pallas_call(
        lambda out_ref: None, out_specs=ANYWHERE, out_shape=jax.ShapeDtypeStruct(shape, dtype)
    )()


class Order:
    def __init__(self):
        self.token = jnp.zeros((8, 128), jnp.float32)

    def __call__(self, *trees):
        leaves, tree = jax.tree.flatten(trees)
        held = pl.pallas_call(
            lambda *refs: None,
            in_specs=[ANYWHERE] * (1 + len(leaves)),
            out_specs=[ANYWHERE] * (1 + len(leaves)),
            out_shape=[jax.ShapeDtypeStruct(x.shape, x.dtype) for x in [self.token, *leaves]],
            input_output_aliases={i: i for i in range(1 + len(leaves))},
        )(self.token, *leaves)
        self.token = held[0]
        out = jax.tree.unflatten(tree, held[1:])
        return out[0] if len(trees) == 1 else out


def split_columns(gate, up, dp, line):
    rows, ff = gate.shape
    rest = ff // (dp * line)

    def kernel(gate_ref, up_ref, out_ref):
        for which, ref in enumerate((gate_ref, up_ref)):
            for i in range(dp):
                for j in range(line):
                    first = (i * line + j) * rest
                    out_ref[j, which, :, i * rest : (i + 1) * rest] = ref[:, first : first + rest]

    return pl.pallas_call(
        kernel,
        out_shape=jax.ShapeDtypeStruct((line, 2, rows, dp * rest), gate.dtype),
        compiler_params=pltpu.CompilerParams(vmem_limit_bytes=VMEM_LIMIT),
    )(gate, up)


def join_columns(parts, dp):
    line, _, rows, part = parts.shape
    rest = part // dp

    def kernel(parts_ref, gate_ref, up_ref):
        for which, ref in enumerate((gate_ref, up_ref)):
            for i in range(dp):
                for j in range(line):
                    first = (i * line + j) * rest
                    ref[:, first : first + rest] = parts_ref[
                        j, which, :, i * rest : (i + 1) * rest
                    ].astype(jnp.float32)

    return pl.pallas_call(
        kernel,
        out_shape=[jax.ShapeDtypeStruct((rows, line * part), jnp.float32)] * 2,
        compiler_params=pltpu.CompilerParams(vmem_limit_bytes=VMEM_LIMIT),
    )(parts)


def tile_facts(place, span, tile):
    line = pl.num_programs(0) // 2
    row_tokens = line * 2 * span
    half = tile // line
    key_first = half * row_tokens + (tile % line) * 2 * span
    query_first = [(place[2] ^ j) * row_tokens + (2 * place[0] + place[1]) * span for j in (0, 1)]
    return key_first, query_first


def reach(key_first, keys, query_first, queries):
    key_last, query_last = key_first + keys - 1, query_first + queries - 1
    live = (key_first <= query_last) & (query_first - key_last < WINDOW)
    plain = (key_last < query_first) & (query_last - key_first < WINDOW)
    return live & plain, live & jnp.logical_not(plain)


def forward_kernel(place, query_ref, own_ref, other_ref, code_ref, segment_ref, *rest):
    out_ref, log_ref, acc, total = rest[-4:]
    tile = pl.program_id(0)
    span = query_ref.shape[1]
    key_first, query_first = tile_facts(place, span, tile)

    @pl.when(tile == 0)
    def _():
        acc[...] = jnp.zeros_like(acc)
        total[...] = jnp.zeros_like(total)

    def step(j, masked):
        keys = jnp.concatenate([own_ref[0, 0, :, :HEAD_DIM], other_ref[0, 0, :, :HEAD_DIM]], axis=0)
        values = jnp.concatenate(
            [own_ref[0, 0, :, HEAD_DIM:], other_ref[0, 0, :, HEAD_DIM:]], axis=0
        )
        allowed = code_ref[0, 0] == segment_ref[j]
        if masked:
            lane = lax.broadcasted_iota(jnp.int32, (1, 2 * span), 1)
            key_pos = key_first + lane + jnp.where(lane < span, place[1], -place[1]) * span
            query_pos = query_first[j] + lax.broadcasted_iota(jnp.int32, (span, 1), 0)
            back = query_pos - key_pos
            allowed = (allowed & (back > 0) & (back < WINDOW)) | (back == 0)
        for h in range(GROUP):
            query = query_ref[j, :, h * HEAD_DIM : (h + 1) * HEAD_DIM]
            scores = matmul_t(query, keys)
            weights = jnp.exp2(log2_scale * jnp.tanh(scores * score_scale))
            weights = jnp.where(allowed, weights, 0.0)
            total[j, h] += jnp.sum(weights, axis=-1, keepdims=True)
            acc[j, h] += matmul(weights.astype(jnp.bfloat16), values)

    for j in (0, 1):
        plain, masked = reach(key_first, 2 * span, query_first[j], span)
        pl.when(plain)(functools.partial(step, j, False))
        pl.when(masked)(functools.partial(step, j, True))

    @pl.when(tile == pl.num_programs(0) - 1)
    def _():
        for j in (0, 1):
            for h in range(GROUP):
                out_ref[j, :, h * HEAD_DIM : (h + 1) * HEAD_DIM] = (
                    acc[j, h] / total[j, h]
                ).astype(jnp.bfloat16)
        log_ref[...] = jnp.log2(total[...])


def backward_kernel(
    place, query_ref, grad_ref, own_ref, other_ref, code_ref, stats_ref, segment_ref, *rest
):
    query_grad_ref, own_grad_ref, other_grad_ref = rest[-8:-5]
    queries, grads, query_acc, key_acc, value_acc = rest[-5:]
    tile = pl.program_id(0)
    span = query_ref.shape[1]
    key_first, query_first = tile_facts(place, span, tile)

    @pl.when(tile == 0)
    def _():
        query_acc[...] = jnp.zeros_like(query_acc)
        for j in (0, 1):
            for h in range(GROUP):
                rows, columns = pl.ds(h * span, span), slice(h * HEAD_DIM, (h + 1) * HEAD_DIM)
                queries[j, rows, :] = query_ref[j, :, columns]
                grads[j, rows, :] = grad_ref[j, :, columns]

    def step(j, side, side_first, keys, values, masked):
        allowed = code_ref[0, 0, pl.ds(side * span, span), :] == segment_ref[j, 0:1, :]
        if masked:
            lane = lax.broadcasted_iota(jnp.int32, (1, GROUP * span), 1)
            query_pos = query_first[j] + jnp.where(lane < span, lane, lane - span)
            key_pos = side_first + lax.broadcasted_iota(jnp.int32, (span, 1), 0)
            back = query_pos - key_pos
            allowed = (allowed & (back > 0) & (back < WINDOW)) | (back == 0)
        squashed = jnp.tanh(matmul_t(keys, queries[j]) * score_scale)
        weights = jnp.exp2(log2_scale * squashed - stats_ref[j, 0:1, :])
        weights = jnp.where(allowed, weights, 0.0)
        grad_weights = matmul_t(values, grads[j])
        value_acc[side] += matmul(weights.astype(jnp.bfloat16), grads[j])
        grad_scores = weights * (grad_weights - stats_ref[j, 1:2, :]) * (1.0 - squashed * squashed)
        grad_scores = grad_scores.astype(jnp.bfloat16)
        key_acc[side] += matmul(grad_scores, queries[j])
        query_acc[j] += inner_t(grad_scores, keys)

    key_acc[...] = jnp.zeros_like(key_acc)
    value_acc[...] = jnp.zeros_like(value_acc)
    scale = HEAD_DIM ** (-0.5)
    for side, key_ref, grad_out in ((0, own_ref, own_grad_ref), (1, other_ref, other_grad_ref)):
        side_first = key_first + (place[1] if side == 0 else 1 - place[1]) * span

        def on_side(j, masked, side=side, side_first=side_first, key_ref=key_ref):
            keys, values = key_ref[0, 0, :, :HEAD_DIM], key_ref[0, 0, :, HEAD_DIM:]
            step(j, side, side_first, keys, values, masked)

        for j in (0, 1):
            plain, masked = reach(side_first, span, query_first[j], span)
            pl.when(plain)(functools.partial(on_side, j, False))
            pl.when(masked)(functools.partial(on_side, j, True))
        grad_out[0, 0, :, :HEAD_DIM] = (key_acc[side] * scale).astype(jnp.bfloat16)
        grad_out[0, 0, :, HEAD_DIM:] = value_acc[side].astype(jnp.bfloat16)

    @pl.when(tile == pl.num_programs(0) - 1)
    def _():
        for j in (0, 1):
            for h in range(GROUP):
                query_grad_ref[j, :, h * HEAD_DIM : (h + 1) * HEAD_DIM] = (
                    query_acc[j, h * span : (h + 1) * span, :] * scale
                ).astype(jnp.bfloat16)


def whole(*shape):
    return pl.BlockSpec(shape, lambda tile, place: (0,) * len(shape))


def tile_specs(line, span):
    def key_place(tile, place):
        return (tile % line, (tile // line) ^ place[2], 0, 0)

    def code_place(tile, place):
        return ((tile // line) ^ place[2], tile % line, 0, 0)

    return pl.BlockSpec((1, 1, span, 2 * HEAD_DIM), key_place), code_place


def attention_forward(place, queries, own, other, codes, segments, *first):
    line, _, span, width = own.shape
    tile_spec, code_place = tile_specs(line, span)
    pairs = 2 * span * line * 2 * span * GROUP
    return pl.pallas_call(
        forward_kernel,
        grid_spec=pltpu.PrefetchScalarGridSpec(
            num_scalar_prefetch=1,
            grid=(2 * line,),
            in_specs=[
                whole(2, span, width),
                tile_spec,
                tile_spec,
                pl.BlockSpec((1, 1, 1, 2 * span), code_place),
                whole(2, span, 1),
            ]
            + [ANYWHERE] * len(first),
            out_specs=[whole(2, span, width), whole(2, GROUP, span, 1)],
            scratch_shapes=[
                pltpu.VMEM((2, GROUP, span, HEAD_DIM), jnp.float32),
                pltpu.VMEM((2, GROUP, span, 1), jnp.float32),
            ],
        ),
        out_shape=[
            jax.ShapeDtypeStruct((2, span, width), jnp.bfloat16),
            jax.ShapeDtypeStruct((2, GROUP, span, 1), jnp.float32),
        ],
        compiler_params=pltpu.CompilerParams(vmem_limit_bytes=VMEM_LIMIT),
        cost_estimate=pl.CostEstimate(
            flops=4 * HEAD_DIM * pairs, bytes_accessed=12 << 20, transcendentals=2 * pairs
        ),
    )(place, queries, own, other, codes, segments, *first)


def attention_backward(place, queries, grads, own, other, codes, stats, segments, *first):
    line, _, span, width = own.shape
    tile_spec, code_place = tile_specs(line, span)
    pairs = 2 * span * line * 2 * span * GROUP
    return pl.pallas_call(
        backward_kernel,
        grid_spec=pltpu.PrefetchScalarGridSpec(
            num_scalar_prefetch=1,
            grid=(2 * line,),
            in_specs=[
                whole(2, span, width),
                whole(2, span, width),
                tile_spec,
                tile_spec,
                pl.BlockSpec((1, 1, 2 * span, 1), code_place),
                whole(2, 8, GROUP * span),
                whole(2, 8, GROUP * span),
            ]
            + [ANYWHERE] * len(first),
            out_specs=[whole(2, span, width), tile_spec, tile_spec],
            scratch_shapes=[
                pltpu.VMEM((2, GROUP * span, HEAD_DIM), jnp.bfloat16),
                pltpu.VMEM((2, GROUP * span, HEAD_DIM), jnp.bfloat16),
                pltpu.VMEM((2, GROUP * span, HEAD_DIM), jnp.float32),
                pltpu.VMEM((2, span, HEAD_DIM), jnp.float32),
                pltpu.VMEM((2, span, HEAD_DIM), jnp.float32),
            ],
        ),
        out_shape=[
            jax.ShapeDtypeStruct((2, span, width), jnp.bfloat16),
            jax.ShapeDtypeStruct(own.shape, jnp.bfloat16),
            jax.ShapeDtypeStruct(own.shape, jnp.bfloat16),
        ],
        compiler_params=pltpu.CompilerParams(vmem_limit_bytes=VMEM_LIMIT),
        cost_estimate=pl.CostEstimate(
            flops=10 * HEAD_DIM * pairs, bytes_accessed=20 << 20, transcendentals=2 * pairs
        ),
    )(place, queries, grads, own, other, codes, stats, segments, *first)


def body(
    tokens, pre_attention, post_attention, pre_feedforward, post_feedforward, w_query, key_weight,
    value_weight, w_output, w_gate, w_up, w_down, document_index, token_padding_mask, cotangent,
):
    bf16, f32 = jnp.bfloat16, jnp.float32
    dp, seq = lax.axis_size("dp"), lax.axis_size("seq")
    line, groups = seq // 2, dp // KEY_VALUE_HEADS
    dp_at, seq_at = lax.axis_index("dp"), lax.axis_index("seq")
    line_at, core = seq_at // 2, seq_at % 2
    head = dp_at % KEY_VALUE_HEADS
    half_bit = dp_at % 2
    _, span, model = tokens.shape
    rows = w_query.shape[0]
    ff = w_gate.shape[1]
    ff_rows = w_down.shape[0]
    ff_part = ff // line
    width = GROUP * HEAD_DIM

    order = Order()

    def attention_codes():
        sequence = dp_at // 2

        def by_pair(table):
            both = jnp.stack([pick(table, 0, sequence), pick(table, 0, sequence ^ 1)])
            both = both.reshape(2, 2, line, 2, span)
            both = jnp.where(half_bit == 1, both[:, ::-1], both)
            return jnp.where(core == 1, both[:, :, :, ::-1], both)

        segments = by_pair(document_index)
        codes = jnp.where(by_pair(token_padding_mask) == 1, segments, -1)
        return codes.reshape(2, 2, line, 2 * span), pick(segments[:, :, :, 0], 2, line_at)

    inputs = tokens[0].astype(f32)
    normed_in = normed(inputs, pre_attention).astype(bf16)
    blocks = jnp.concatenate(
        [
            w_query.reshape(rows, KEY_VALUE_HEADS, width),
            key_weight.reshape(rows, KEY_VALUE_HEADS, HEAD_DIM),
            value_weight.reshape(rows, KEY_VALUE_HEADS, HEAD_DIM),
        ],
        axis=2,
    ).transpose(1, 0, 2)

    if groups == 1:
        flipped = flip_order(blocks, head)
        normed_in, flipped = order(normed_in, flipped)
        near_normed = gather_quad_near(normed_in)
        mixed = [flipped[0]] + [across(flipped[k], k) for k in (1, 2, 3)]
        split = split_columns(w_gate, w_up, dp, line)
        mixed = exchange_quad_end(mixed, head)
        mixed, split = order(mixed, split)
        in_weight = lax.all_gather(mixed, "seq", axis=1).reshape(model, 2 * width)
    else:
        near_normed = gather_quad_near(normed_in)
        split = split_columns(w_gate, w_up, dp, line)
        in_weight = pick(lax.all_gather(blocks, ("dp", "seq"), axis=1, tiled=True), 0, head)

    per_device = line * rows
    gate_up = exchange_line(split.reshape(line, 2 * rows, ff_part), line_at)
    gate_up = gate_up.reshape(line, 2, rows, ff_part).transpose(1, 0, 2, 3)
    gate_up = gate_up.reshape(2 * per_device, ff_part)

    def near_blocks(own):
        return gather_quad_near(own) if groups == 1 else (lax.all_gather(own, "dp", axis=0),)

    def far_blocks(near):
        return (gather_quad_far(*near),) if groups == 1 else ()

    def swap_all(blocks):
        return [swap_core(block) for block in blocks]

    down_weight = empty((dp, 2, ff_rows, model), bf16)
    gate_weight = empty((dp, line, 2, rows, ff_part), bf16)
    up_weight = empty((dp, line, 2, rows, ff_part), bf16)

    def fill_down(weight, numbers, mine, swapped):
        for k, *sides in zip(numbers, mine, swapped):
            for block, side in zip(sides, (core, 1 - core)):
                at = head ^ k if groups == 1 else 0
                weight = lax.dynamic_update_slice(
                    weight, block.reshape(-1, 1, ff_rows, model), (at, side, 0, 0)
                )
        return weight

    def fill_in(gate, up, numbers, mine, swapped):
        for k, *sides in zip(numbers, mine, swapped):
            for block, side in zip(sides, (core, 1 - core)):
                at = head ^ k if groups == 1 else 0
                block = block.reshape(-1, 2, line, 1, rows, ff_part)
                gate = lax.dynamic_update_slice(gate, block[:, 0], (at, 0, side, 0, 0))
                up = lax.dynamic_update_slice(up, block[:, 1], (at, 0, side, 0, 0))
        return gate, up

    near_normed = order(near_normed)
    far_normed = gather_quad_far(*near_normed)
    first_rows = jnp.concatenate([normed_in, near_normed[0]], axis=0)
    far_normed, near_two, first_rows = order(far_normed, near_normed[1], first_rows)
    own_down = after(w_down, far_normed)
    near_down = near_blocks(own_down)
    second_rows = jnp.concatenate([near_two, far_normed], axis=0)
    second_rows, in_weight, first_rows = order(second_rows, in_weight, first_rows)

    def project(pair_rows):
        projected = matmul(pair_rows, in_weight).astype(bf16).reshape(2, span, 2 * width)
        return projected[..., :width], projected[..., width:]

    first_queries, first_keys = project(first_rows)
    first_queries, first_keys, second_rows, first_rows = order(
        first_queries, first_keys, second_rows, first_rows
    )
    first_own = gather_line(first_keys)
    second_queries, second_keys = project(second_rows)
    near_down, second_queries, second_keys = order(near_down, second_queries, second_keys)
    far_down = far_blocks(near_down)
    second_own = gather_line(second_keys)
    if groups == 1:
        out_weight = lax.all_gather(
            after(w_output, second_keys), "seq", axis=0, tiled=True
        )
    else:
        out_weight = lax.dynamic_slice_in_dim(
            lax.all_gather(w_output, ("dp", "seq"), axis=0, tiled=True), head * width, width
        )
    normed_rows = [first_rows, second_rows]

    gate_up, own_down, far_down = order(gate_up, own_down, far_down)
    near_in = near_blocks(gate_up)
    mine_down = ([own_down] if groups == 1 else []) + list(near_down) + list(far_down)
    swapped = swap_all(mine_down[:2])
    down_weight = fill_down(down_weight, (0, 1), mine_down[:2], swapped)
    first_own, down_weight = order(first_own, down_weight)
    first_other = swap_core(first_own)
    codes, own_segments = attention_codes()
    place = jnp.stack([line_at, core, half_bit]).astype(jnp.int32)
    row_codes = codes[:, :, :, None, :]
    column_segments = own_segments[..., None]
    first_other, place, row_codes, column_segments = order(
        first_other, place, row_codes, column_segments
    )
    swapped = swap_all(mine_down[2:])
    attended, log_total = [None, None], [None, None]
    attended[0], log_total[0] = attention_forward(
        place, first_queries, first_own, first_other, row_codes[0], column_segments[0]
    )
    attended[0], swapped = order(attended[0], swapped)
    down_weight = fill_down(down_weight, (2, 3), mine_down[2:], swapped)
    if groups == 1:
        swapped = swap_all([gate_up])
        gate_weight, up_weight = fill_in(gate_weight, up_weight, (0,), [gate_up], swapped)
    near_in, second_own, down_weight, gate_weight, up_weight = order(
        near_in, second_own, down_weight, gate_weight, up_weight
    )
    second_other = swap_core(second_own)
    far_in = far_blocks(near_in)
    second_other = order(second_other)
    swapped = swap_all(near_in)
    attended[1], log_total[1] = attention_forward(
        place, second_queries, second_own, second_other, row_codes[1], column_segments[1]
    )
    queries = [first_queries, second_queries]
    own_keys, other_keys = [first_own, second_own], [first_other, second_other]
    attended, log_total, out_weight, swapped, far_in = order(
        attended, log_total, out_weight, swapped, far_in
    )
    numbers = (1, 2, 3) if groups == 1 else (0,)

    def activation(gate_in, up_in):
        return jax.nn.gelu(gate_in, approximate=True) * up_in

    step = span // CHUNKS
    chunks = [slice(c * step, (c + 1) * step) for c in range(CHUNKS)]
    grad_output = cotangent[0].astype(f32)
    attn_outs, residuals, mids = [], [], []
    for c, part in enumerate(chunks):
        parts = []
        for pair in (0, 1):
            rows_of = attended[pair][:, part].reshape(2 * step, width)
            parts += list(matmul(rows_of, out_weight).astype(bf16).reshape(2, step, model))
        if c == 0:
            parts = order(parts)
        attn_outs.append(scatter_quad(parts))
        residuals.append(inputs[part] + normed(attn_outs[-1], post_attention))
        mids.append(normed(residuals[-1], pre_feedforward).astype(bf16))
        if c == 0:
            gate_weight, up_weight = fill_in(
                gate_weight, up_weight, numbers[:2], near_in, swapped
            )
            swapped = swap_all(far_in)
            mids[0], swapped, gate_weight, up_weight = order(
                mids[0], swapped, gate_weight, up_weight
            )
        if c == 1:
            gate_weight, up_weight = fill_in(gate_weight, up_weight, numbers[2:], far_in, swapped)
    down_weight = down_weight.reshape(ff_part, model)
    gate_weight = gate_weight.reshape(model, ff_part)
    up_weight = up_weight.reshape(model, ff_part)

    results, kept, grad_mids = [], [], []
    grad_post_ff = grad_pre_ff = grad_post_attn = 0.0
    for c, part in enumerate(chunks):
        mid_rows = gather_line(mids[c]).reshape(line * step, model)
        gate_value, up_value = matmul(mid_rows, gate_weight), matmul(mid_rows, up_weight)
        hidden = activation(gate_value, up_value).astype(bf16)
        down_part = matmul(hidden, down_weight).astype(bf16).reshape(line, step, model)
        down_out = scatter_line(down_part).astype(f32)
        normed_down, down_back = jax.vjp(normed, down_out, post_feedforward)
        results.append(residuals[c] + normed_down)
        grad_down, gain_part = down_back(grad_output[part])
        grad_post_ff += gain_part
        down_rows = gather_line(grad_down.astype(bf16)).reshape(line * step, model)
        grad_hidden = matmul_t(down_rows, down_weight)
        _, act_back = jax.vjp(activation, gate_value, up_value)
        grad_gate, grad_up = act_back(grad_hidden)
        grad_gate, grad_up = grad_gate.astype(bf16), grad_up.astype(bf16)
        mid_part = matmul_t(grad_gate, gate_weight) + matmul_t(grad_up, up_weight)
        mid_part = mid_part.astype(bf16).reshape(line, step, model)
        kept.append((mid_rows, hidden, down_rows, grad_gate, grad_up))
        if c == CHUNKS - 1:
            mid_part, kept = order(mid_part, kept)
        grad_mids.append(scatter_line(mid_part).astype(f32))
    result = jnp.concatenate(results, axis=0)

    mid_rows, hidden, down_rows, grad_gate, grad_up = (
        jnp.concatenate(parts, axis=0) for parts in zip(*kept)
    )
    down_term = inner_t(hidden, down_rows).astype(bf16).reshape(dp, 2, ff_rows, model)
    in_terms = [
        inner_t(mid_rows, grad).astype(bf16).reshape(dp, line, 2, rows, ff_part)
        for grad in (grad_gate, grad_up)
    ]
    *in_terms, down_term, grad_mids = order(*in_terms, down_term, grad_mids)
    in_swapped = [swap_core(pick(term, 2, 1 - core)) for term in in_terms]
    down_swapped = swap_core(pick(down_term, 1, 1 - core))

    grad_residuals, outputs_quad = [], []
    for c, part in enumerate(chunks):
        _, mid_back = jax.vjp(normed, residuals[c], pre_feedforward)
        grad_residual, gain_part = mid_back(grad_mids[c])
        grad_pre_ff += gain_part
        grad_residuals.append(grad_output[part] + grad_residual)
        _, attn_back = jax.vjp(normed, attn_outs[c], post_attention)
        grad_attn, gain_part = attn_back(grad_residuals[-1])
        grad_post_attn += gain_part
        outputs_quad.append(gather_quad(grad_attn.astype(bf16)))
    grad_residual = jnp.concatenate(grad_residuals, axis=0)

    def owned_gains(terms):
        terms = jnp.stack(terms, axis=1)
        count = terms.shape[1]
        if groups > 1:
            return lax.psum_scatter(terms, ("dp", "seq"), scatter_dimension=0, tiled=True)
        terms = terms.reshape(dp, line, 2, rows * count)
        terms = sum(
            (across(pick(terms, 0, head ^ k), k) for k in (1, 2, 3)), pick(terms, 0, head)
        )
        terms = pick(terms, 1, core) + swap_core(pick(terms, 1, 1 - core))
        return jnp.sum(exchange_line(terms, line_at), axis=0).reshape(rows, count)

    outputs_quad, in_swapped, down_swapped, in_terms, down_term = order(
        outputs_quad, in_swapped, down_swapped, in_terms, down_term
    )
    early_gains = owned_gains([grad_post_attn, grad_pre_ff, grad_post_ff])

    grad_attended, stats, output_term = [], [], 0.0
    for pair in (0, 1):
        attn_rows = jnp.concatenate(
            [quad[2 * pair + j] for j in (0, 1) for quad in outputs_quad], axis=0
        )
        output_term += inner_t(attended[pair].reshape(2 * span, width), attn_rows)
        grad_attended.append(matmul_t(attn_rows, out_weight).astype(bf16).reshape(2, span, width))
        delta = (grad_attended[pair].astype(f32) * attended[pair].astype(f32)).reshape(
            2, span, GROUP, HEAD_DIM
        )
        delta = jnp.sum(delta, axis=-1).transpose(0, 2, 1)
        stat = jnp.stack(
            [log_total[pair].reshape(2, GROUP * span), delta.reshape(2, GROUP * span)], axis=1
        )
        stats.append(jnp.pad(stat, ((0, 0), (0, 6), (0, 0))))
    output_term = output_term.astype(bf16)
    lane_segments = jnp.broadcast_to(
        own_segments[:, :, None, None, :], (2, 2, 8, GROUP, span)
    ).reshape(2, 2, 8, GROUP * span)
    column_codes = codes[..., None]
    output_term, early_gains, grad_attended, stats, lane_segments, column_codes = order(
        output_term, early_gains, grad_attended, stats, lane_segments, column_codes
    )
    if groups == 1:
        output_shard = lax.psum_scatter(output_term, "seq", scatter_dimension=0, tiled=True)
    else:
        spread = jnp.zeros((KEY_VALUE_HEADS, width, model), bf16).at[head].set(output_term)
        output_shard = lax.psum_scatter(
            spread.reshape(KEY_VALUE_HEADS * width, model),
            ("dp", "seq"),
            scatter_dimension=0,
            tiled=True,
        )

    def scatter_near(parts):
        half = parts[0].shape[0] // 2
        low, high = [p[:half] for p in parts], [p[half:] for p in parts]
        return across(jnp.stack([low[1], low[3]]), 1), across(jnp.stack([high[2], high[3]]), 2)

    def scatter_far(parts, from_one, from_two):
        half = parts[0].shape[0] // 2
        return across(parts[2][:half] + from_one[1], 2), across(parts[1][half:] + from_two[1], 1)

    def scatter_end(parts, from_one, from_two, low_rest, high_rest):
        half = parts[0].shape[0] // 2
        low = parts[0][:half].astype(f32) + from_one[0].astype(f32) + low_rest.astype(f32)
        high = parts[0][half:].astype(f32) + from_two[0].astype(f32) + high_rest.astype(f32)
        return jnp.concatenate([low, high], axis=0)

    def attend_back(pair):
        return attention_backward(
            place, queries[pair], grad_attended[pair], own_keys[pair], other_keys[pair],
            column_codes[pair], stats[pair], lane_segments[pair],
        )

    down_mine = pick(down_term, 1, core) + down_swapped
    in_mine = [
        (pick(term, 2, core) + swapped).reshape(dp, per_device, ff_part)
        for term, swapped in zip(in_terms, in_swapped)
    ]
    in_mine = jnp.concatenate(in_mine, axis=1)
    grad_queries, key_grads = [None, None], [None, None]
    if groups == 1:
        down_parts = [pick(down_mine, 0, head ^ k) for k in range(4)]
        in_parts = [pick(in_mine, 0, head ^ k) for k in range(4)]
        down_near = scatter_near(down_parts)
    grad_queries[0], own_grad, other_grad = attend_back(0)
    grad_queries[0], own_grad, other_grad = order(grad_queries[0], own_grad, other_grad)
    swapped = swap_core(other_grad)
    if groups == 1:
        in_near = scatter_near(in_parts)
    swapped = order(swapped)
    key_grads[0] = scatter_line(own_grad + swapped)
    grad_queries[1], own_grad, other_grad = attend_back(1)
    if groups == 1:
        down_near, grad_queries[1], own_grad, other_grad = order(
            down_near, grad_queries[1], own_grad, other_grad
        )
        down_far = scatter_far(down_parts, *down_near)
    swapped = order(swap_core(other_grad))
    key_grads[1] = scatter_line(own_grad + swapped)
    if groups == 1:
        in_near, down_far = order(in_near, down_far)
        down_shard = scatter_end(down_parts, *down_near, *down_far)
        in_far = scatter_far(in_parts, *in_near)
    else:
        down_shard = lax.psum_scatter(down_mine, "dp", scatter_dimension=0).astype(f32)
        in_shard = lax.psum_scatter(in_mine, "dp", scatter_dimension=0)

    def project_back(pair):
        grad_projected = jnp.concatenate([grad_queries[pair], key_grads[pair]], axis=2)
        grad_projected = grad_projected.reshape(2 * span, 2 * width)
        part = matmul_t(grad_projected, in_weight).astype(bf16).reshape(2, span, model)
        return grad_projected, list(part)

    key_grads[0] = order(key_grads[0])
    first_grad, first_parts = project_back(0)
    in_term = inner_t(normed_rows[0], first_grad)
    if groups == 1:
        in_far, first_grad, first_parts, in_term = order(in_far, first_grad, first_parts, in_term)
        in_shard = scatter_end(in_parts, *in_near, *in_far).astype(bf16)
    key_grads[1], in_shard, in_term = order(key_grads[1], in_shard, in_term)
    second_grad, second_parts = project_back(1)
    parts = order(first_parts + second_parts)
    in_near = scatter_near(parts)
    in_term = (in_term + inner_t(normed_rows[1], second_grad)).astype(bf16)
    in_shard = in_shard.reshape(2, line, rows, ff_part).transpose(1, 0, 2, 3)
    if groups == 1:
        in_part = lax.psum_scatter(
            in_term.reshape(KEY_VALUE_HEADS, seq, rows, 2 * width).transpose(1, 0, 2, 3), "seq"
        )
    in_shard = exchange_line(in_shard, line_at)
    in_near = order(in_near)
    in_far = scatter_far(parts, *in_near)
    grad_in = scatter_end(parts, *in_near, *in_far)
    _, in_back = jax.vjp(normed, inputs, pre_attention)
    grad_inputs, grad_pre_attn = in_back(grad_in)
    tokens_grad = grad_residual + grad_inputs
    late_gains = owned_gains([grad_pre_attn])
    gate_shard, up_shard = join_columns(in_shard, dp)
    if groups == 1:
        part_shard = exchange_quad(in_part, head)
    else:
        spread = jnp.zeros((KEY_VALUE_HEADS, model, 2 * width), bf16).at[head].set(in_term)
        part_shard = lax.psum_scatter(spread, ("dp", "seq"), scatter_dimension=1, tiled=True)
    part_shard = part_shard.astype(f32).transpose(1, 0, 2)
    query_shard = part_shard[..., :width].reshape(rows, KEY_VALUE_HEADS * width)
    key_shard = part_shard[..., width : width + HEAD_DIM].reshape(rows, KEY_VALUE_HEADS * HEAD_DIM)
    value_shard = part_shard[..., width + HEAD_DIM :].reshape(rows, KEY_VALUE_HEADS * HEAD_DIM)
    return (
        result[None],
        tokens_grad[None],
        query_shard,
        key_shard,
        value_shard,
        output_shard.astype(f32),
        gate_shard,
        up_shard,
        down_shard,
        late_gains[:, 0],
        early_gains[:, 0],
        early_gains[:, 1],
        early_gains[:, 2],
    )


def solution(mesh):
    tokens, weights, whole_copy = P("dp", "seq", None), P(("dp", "seq"), None), P()
    gains = P(("dp", "seq"))
    return jax.shard_map(
        body,
        mesh=mesh,
        in_specs=(tokens,) + (whole_copy,) * 4 + (weights,) * 7 + (whole_copy,) * 2 + (tokens,),
        out_specs=(tokens,) * 2 + (weights,) * 7 + (gains,) * 4,
        check_vma=False,
    )
```

```python
import functools
import math

import jax
import jax.numpy as jnp
from jax import lax
from jax.experimental import pallas as pl
from jax.experimental.pallas import tpu as pltpu
from jax.sharding import PartitionSpec as P

KEY_VALUE_HEADS = 4
HEAD_DIM = 256
GROUP = 2
WINDOW = 4096

epsilon = 1e-06
softcap = 50.0
score_scale = HEAD_DIM ** (-0.5) / softcap
log2_scale = softcap * 1.4426950408889634
VMEM_LIMIT = 56 * 1024 * 1024
ANYWHERE = pl.BlockSpec(memory_space=pl.ANY)


def normed(values, gain_vec):
    inv_rms = lax.rsqrt(jnp.mean(values * values, axis=-1, keepdims=True) + epsilon)
    return values * inv_rms * gain_vec


def matmul(a, b):
    return jnp.dot(a, b, preferred_element_type=jnp.float32)


def matmul_t(a, b):
    return lax.dot_general(a, b, (((1,), (1,)), ((), ())), preferred_element_type=jnp.float32)


def inner_t(a, b):
    return lax.dot_general(a, b, (((0,), (0,)), ((), ())), preferred_element_type=jnp.float32)


def across(x, bits):
    return lax.ppermute(x, "dp", [(i, i ^ bits) for i in range(lax.axis_size("dp"))])


def swap_core(x):
    return lax.ppermute(x, "seq", [(i, i ^ 1) for i in range(lax.axis_size("seq"))])


def line_groups():
    count = lax.axis_size("seq")
    return [list(range(core, count, 2)) for core in (0, 1)]


def gather_line(x):
    return lax.all_gather(x, "seq", axis=0, axis_index_groups=line_groups())


def line_route(line, distance):
    return [
        (2 * i + core, 2 * ((i + distance) % line) + core) for i in range(line) for core in (0, 1)
    ]


def exchange_line_parts(parts):
    line = len(parts)
    return [parts[0]] + [lax.ppermute(parts[k], "seq", line_route(line, k)) for k in range(1, line)]


def exchange_line(x, place):
    line = x.shape[0]
    parts = exchange_line_parts([pick(x, 0, (place + k) % line) for k in range(line)])
    for k in range(1, line):
        x = put(x, parts[k], (place + line - k) % line)
    return x


def scatter_line(x):
    return lax.psum_scatter(x, "seq", scatter_dimension=0, axis_index_groups=line_groups())


def scatter_line_steps(x, place):
    line = x.shape[0]
    right = left = None
    for step in range(1, line):
        going = pick(x, 0, jnp.clip(line - step + place, 0, line - 1))
        coming = pick(x, 0, jnp.clip(step - line + place, 0, line - 1))
        right = going if right is None else going + right
        left = coming if left is None else coming + left
        right_route = [(2 * i + c, 2 * i + 2 + c) for i in range(step) for c in (0, 1)]
        left_route = [
            (2 * (line - 1 - i) + c, 2 * (line - 2 - i) + c) for i in range(step) for c in (0, 1)
        ]
        right = lax.ppermute(right, "seq", right_route)
        left = lax.ppermute(left, "seq", left_route)
    f32 = jnp.float32
    return pick(x, 0, place).astype(f32) + right.astype(f32) + left.astype(f32)


def gather_quad_near(x):
    return across(x, 1), across(x, 2)


def gather_quad_far_parts(one, two):
    half = one.shape[0] // 2
    return across(two[:half], 1), across(one[half:], 2)


def gather_quad_far(one, two):
    return jnp.concatenate(gather_quad_far_parts(one, two), axis=0)


def gather_quad(x):
    one, two = gather_quad_near(x)
    return [x, one, two, gather_quad_far(one, two)]


def scatter_quad_near(sent):
    return across(sent[0], 1), across(sent[1], 2)


def scatter_quad_far(kept, near):
    return across(kept[1] + near[0][1], 2), across(kept[2] + near[1][1], 1)


def scatter_quad_end(kept, near, far):
    half = kept[0].shape[0] // 2
    f32 = jnp.float32
    low = kept[0][:half].astype(f32) + near[0][0].astype(f32) + far[0].astype(f32)
    high = kept[0][half:].astype(f32) + near[1][0].astype(f32) + far[1].astype(f32)
    return jnp.concatenate([low, high], axis=0)


def flip_order(x, bits):
    pairs = x.reshape((2, 2) + x.shape[1:])
    pairs = jnp.where(bits % 2 == 1, pairs[:, ::-1], pairs)
    pairs = jnp.where(bits // 2 == 1, pairs[::-1], pairs)
    return pairs.reshape(x.shape)


def exchange_quad(x, place):
    parts = flip_order(x, place)
    return exchange_quad_end([parts[0]] + [across(parts[k], k) for k in (1, 2, 3)], place)


def exchange_quad_end(parts, place):
    return flip_order(jnp.stack(parts), place)


def pick(x, axis, index):
    return lax.dynamic_index_in_dim(x, index, axis, keepdims=False)


def put(x, part, *index):
    for _ in index:
        part = part[None]
    return lax.dynamic_update_slice(x, part, index + (0,) * (x.ndim - len(index)))


def after(x, *others):
    def kernel(x_ref, *rest):
        rest[-1][...] = x_ref[...]

    return pl.pallas_call(
        kernel,
        in_specs=[pl.BlockSpec(memory_space=pltpu.VMEM)] + [ANYWHERE] * len(others),
        out_specs=pl.BlockSpec(memory_space=pltpu.VMEM),
        out_shape=jax.ShapeDtypeStruct(x.shape, x.dtype),
    )(x, *others)


def empty(shape, dtype):
    return pl.pallas_call(
        lambda out_ref: None, out_specs=ANYWHERE, out_shape=jax.ShapeDtypeStruct(shape, dtype)
    )()


class Order:
    def __init__(self):
        self.token = jnp.zeros((8, 128), jnp.float32)

    def __call__(self, *trees):
        leaves, tree = jax.tree.flatten(trees)
        held = pl.pallas_call(
            lambda *refs: None,
            in_specs=[ANYWHERE] * (1 + len(leaves)),
            out_specs=[ANYWHERE] * (1 + len(leaves)),
            out_shape=[jax.ShapeDtypeStruct(x.shape, x.dtype) for x in [self.token, *leaves]],
            input_output_aliases={i: i for i in range(1 + len(leaves))},
        )(self.token, *leaves)
        self.token = held[0]
        out = jax.tree.unflatten(tree, held[1:])
        return out[0] if len(trees) == 1 else out


FREE = pl.CostEstimate(flops=0, bytes_accessed=0, transcendentals=0)


def cost(us):
    return pl.CostEstimate(flops=0, bytes_accessed=int(us * 3.5e6), transcendentals=0)


def deposit(place, targets, sources, moves):
    count = len(targets)

    def kernel(place_ref, *refs):
        source_refs = refs[count : count + len(sources)]
        target_refs, sems = refs[count + len(sources) : -1], refs[-1]
        copies = []
        for n, (source, source_at, target, target_at) in enumerate(moves):
            source_ref, target_ref = source_refs[source], target_refs[target]
            if source_at is not None:
                source_ref = source_ref.at[source_at(place_ref)]
            copies.append(
                pltpu.make_async_copy(source_ref, target_ref.at[target_at(place_ref)], sems.at[n])
            )
            copies[-1].start()
        for copy in copies:
            copy.wait()

    return pl.pallas_call(
        kernel,
        in_specs=[pl.BlockSpec(memory_space=pltpu.SMEM)]
        + [ANYWHERE] * count
        + [pl.BlockSpec(memory_space=pltpu.VMEM)] * len(sources),
        out_specs=[ANYWHERE] * count,
        out_shape=[jax.ShapeDtypeStruct(x.shape, x.dtype) for x in targets],
        scratch_shapes=[pltpu.SemaphoreType.DMA((len(moves),))],
        input_output_aliases={1 + i: i for i in range(count)},
        compiler_params=pltpu.CompilerParams(vmem_limit_bytes=VMEM_LIMIT),
        cost_estimate=FREE,
    )(place, *targets, *sources)


LINE_AT, CORE_AT, HALF_AT, HEAD_AT = range(4)


def pack_heads(place, query, key, value):
    rows, width = query.shape[0], GROUP * HEAD_DIM

    def kernel(place_ref, query_ref, key_ref, value_ref, *out_refs):
        for k, out_ref in enumerate(out_refs):
            head = place_ref[HEAD_AT] ^ k
            first = pl.multiple_of(head * width, width)
            out_ref[:, :width] = query_ref[:, pl.ds(first, width)]
            first = pl.multiple_of(head * HEAD_DIM, HEAD_DIM)
            out_ref[:, width : width + HEAD_DIM] = key_ref[:, pl.ds(first, HEAD_DIM)]
            out_ref[:, width + HEAD_DIM :] = value_ref[:, pl.ds(first, HEAD_DIM)]

    return pl.pallas_call(
        kernel,
        in_specs=[pl.BlockSpec(memory_space=pltpu.SMEM)]
        + [pl.BlockSpec(memory_space=pltpu.VMEM)] * 3,
        out_shape=[jax.ShapeDtypeStruct((rows, 2 * width), query.dtype)] * KEY_VALUE_HEADS,
        compiler_params=pltpu.CompilerParams(vmem_limit_bytes=VMEM_LIMIT),
        cost_estimate=FREE,
    )(place, query, key, value)


def order_heads(place, parts):
    def kernel(place_ref, *refs):
        for k in range(KEY_VALUE_HEADS):
            refs[-1][place_ref[HEAD_AT] ^ k] = refs[k][...]

    return pl.pallas_call(
        kernel,
        in_specs=[pl.BlockSpec(memory_space=pltpu.SMEM)]
        + [pl.BlockSpec(memory_space=pltpu.VMEM)] * KEY_VALUE_HEADS,
        out_shape=jax.ShapeDtypeStruct((KEY_VALUE_HEADS,) + parts[0].shape, parts[0].dtype),
        compiler_params=pltpu.CompilerParams(vmem_limit_bytes=VMEM_LIMIT),
        cost_estimate=FREE,
    )(place, *parts)


def weight_halves(place, lefts, rights, inner):
    rows, model = lefts[0].shape
    columns = rights[0].shape[1]
    block, strip = math.gcd(model, 1152), math.gcd(columns, 256)
    groups = block // (2 * inner)

    def kernel(place_ref, left_a, left_b, right_a, right_b, own_ref, other_ref, turned):
        turned[:, :rows] = left_a[...].T
        turned[:, rows:] = left_b[...].T
        core_here = place_ref[CORE_AT]

        def body(n, carry):
            at = pl.ds(pl.multiple_of(n * strip, strip), strip)
            term = matmul(turned[:, :rows], right_a[:, at])
            term = (term + matmul(turned[:, rows:], right_b[:, at])).astype(jnp.bfloat16)
            term = term.reshape(groups, 2, inner, strip)
            own_ref[:, :, at] = jnp.where(core_here == 0, term[:, 0], term[:, 1])
            other_ref[:, :, at] = jnp.where(core_here == 0, term[:, 1], term[:, 0])
            return carry

        lax.fori_loop(0, columns // strip, body, 0)

    half = pl.BlockSpec((groups, inner, columns), lambda i: (i, 0, 0))
    shape = jax.ShapeDtypeStruct((model // (2 * inner), inner, columns), jnp.bfloat16)
    left_spec = pl.BlockSpec((rows, block), lambda i: (0, i))
    right_spec = pl.BlockSpec((rows, columns), lambda i: (0, 0))
    return pl.pallas_call(
        kernel,
        grid=(model // block,),
        in_specs=[pl.BlockSpec(memory_space=pltpu.SMEM)] + [left_spec] * 2 + [right_spec] * 2,
        out_specs=[half, half],
        out_shape=[shape, shape],
        scratch_shapes=[pltpu.VMEM((block, 2 * rows), jnp.bfloat16)],
        compiler_params=pltpu.CompilerParams(vmem_limit_bytes=VMEM_LIMIT),
        cost_estimate=FREE,
    )(place, *lefts, *rights)


def quad_terms(lefts, weight, part, turned):
    first, count = part.start, part.stop - part.start
    half = count // 2
    model = weight.shape[0] if turned else weight.shape[1]

    def kernel(a_ref, b_ref, weight_ref, one_ref, two_ref, own_ref, low_ref, high_ref):
        for k in range(4):
            ref = (a_ref, b_ref)[k // 2]
            rows = ref[k % 2, first : first + count, :]
            product = matmul_t if turned else matmul
            term = product(rows, weight_ref[...]).astype(jnp.bfloat16)
            if k == 0:
                own_ref[...] = term
            if k % 2 == 1:
                one_ref[k // 2] = term[:half]
            if k == 2:
                low_ref[...] = term[:half]
            if k >= 2:
                two_ref[k - 2] = term[half:]
            if k == 1:
                high_ref[...] = term[half:]

    def shape(*lead):
        return jax.ShapeDtypeStruct(lead + (model,), jnp.bfloat16)

    one, two, own, low, high = pl.pallas_call(
        kernel,
        out_shape=[shape(2, half), shape(2, half), shape(count), shape(half), shape(half)],
        compiler_params=pltpu.CompilerParams(vmem_limit_bytes=VMEM_LIMIT),
        cost_estimate=FREE,
    )(*lefts, weight)
    return (one, two), (own, low, high)


def split_columns(place, gate, up, dp, line):
    rows, ff = gate.shape
    rest = ff // (dp * line)

    def kernel(place_ref, gate_ref, up_ref, *out_refs):
        def fill(j, k):
            for which, ref in enumerate((gate_ref, up_ref)):
                for i in range(dp):
                    first = (i * line + j) * rest
                    out_refs[k][which, :, i * rest : (i + 1) * rest] = ref[:, first : first + rest]

        for j in range(line):
            for k in range(line):
                there = lax.rem(place_ref[LINE_AT] + k, line) == j
                pl.when(there)(functools.partial(fill, j, k))

    return pl.pallas_call(
        kernel,
        in_specs=[pl.BlockSpec(memory_space=pltpu.SMEM)]
        + [pl.BlockSpec(memory_space=pltpu.VMEM)] * 2,
        out_shape=[jax.ShapeDtypeStruct((2, rows, dp * rest), gate.dtype)] * line,
        compiler_params=pltpu.CompilerParams(vmem_limit_bytes=VMEM_LIMIT),
        cost_estimate=FREE,
    )(place, gate, up)


def join_columns(place, parts, dp):
    line = len(parts)
    rows, part = parts[0].shape
    rest = part // dp

    def kernel(place_ref, *refs):
        def fill(j, k):
            for i in range(dp):
                first = (i * line + j) * rest
                refs[line][:, first : first + rest] = refs[k][
                    :, i * rest : (i + 1) * rest
                ].astype(jnp.float32)

        for j in range(line):
            for k in range(line):
                there = lax.rem(place_ref[LINE_AT] + line - k, line) == j
                pl.when(there)(functools.partial(fill, j, k))

    return pl.pallas_call(
        kernel,
        in_specs=[pl.BlockSpec(memory_space=pltpu.SMEM)]
        + [pl.BlockSpec(memory_space=pltpu.VMEM)] * line,
        out_shape=jax.ShapeDtypeStruct((rows, line * part), jnp.float32),
        compiler_params=pltpu.CompilerParams(vmem_limit_bytes=VMEM_LIMIT),
        cost_estimate=FREE,
    )(place, *parts)


def add_second(term, pair):
    rows, columns = term.shape

    def kernel(term_ref, pair_ref, out_ref):
        total = term_ref[...].astype(jnp.float32) + pair_ref[0].astype(jnp.float32)
        out_ref[...] = total.astype(jnp.bfloat16)

    return pl.pallas_call(
        kernel,
        grid=(1,),
        in_specs=[
            pl.BlockSpec((rows, columns), lambda i: (0, 0)),
            pl.BlockSpec((1, rows, columns), lambda i: (1, 0, 0)),
        ],
        out_specs=pl.BlockSpec((rows, columns), lambda i: (0, 0)),
        out_shape=jax.ShapeDtypeStruct((rows, columns), jnp.bfloat16),
        compiler_params=pltpu.CompilerParams(vmem_limit_bytes=VMEM_LIMIT),
        cost_estimate=FREE,
    )(term, pair)


def combine_quad(place, own, other, shapes, plan):
    _, inner, columns = own.shape
    spec = pl.BlockSpec((1, inner, columns), lambda k, place: (place[HEAD_AT] ^ k, 0, 0))

    def kernel(place_ref, own_ref, other_ref, *out_refs):
        total = own_ref[0].astype(jnp.float32) + other_ref[0].astype(jnp.float32)
        total = total.astype(jnp.bfloat16)

        def write(k):
            for out, at, taken in plan[k]:
                if at is None:
                    out_refs[out][...] = total[taken]
                else:
                    out_refs[out][at] = total[taken]

        for k in range(4):
            pl.when(pl.program_id(0) == k)(functools.partial(write, k))

    return pl.pallas_call(
        kernel,
        grid_spec=pltpu.PrefetchScalarGridSpec(
            num_scalar_prefetch=1,
            grid=(4,),
            in_specs=[spec, spec],
            out_specs=[
                pl.BlockSpec(shape, lambda k, place, rank=len(shape): (0,) * rank)
                for shape in shapes
            ],
        ),
        out_shape=[jax.ShapeDtypeStruct(shape, jnp.bfloat16) for shape in shapes],
        compiler_params=pltpu.CompilerParams(vmem_limit_bytes=VMEM_LIMIT),
        cost_estimate=cost(4),
    )(place, own, other)


def to_line(place, kept, near, far, line):
    count, columns = kept.shape
    rows, half = count // line, count // 2
    alone = pl.BlockSpec((count, columns), lambda i, place: (0, 0))
    first = pl.BlockSpec((1, half, columns), lambda i, place: (0, 0, 0))
    last = pl.BlockSpec((half, columns), lambda i, place: (0, 0))
    part = pl.BlockSpec((rows, columns), lambda i, place: (0, 0))

    def kernel(place_ref, kept_ref, near_one, near_two, far_one, far_two, *out_refs):
        def fill(j, k):
            start = j * rows % half
            near_ref, far_ref = ((near_one, far_one), (near_two, far_two))[j * rows // half]
            total = kept_ref[j * rows : (j + 1) * rows].astype(jnp.float32)
            total = total + near_ref[0, start : start + rows].astype(jnp.float32)
            total = total + far_ref[start : start + rows].astype(jnp.float32)
            out_refs[k][...] = total.astype(jnp.bfloat16)

        for j in range(line):
            for k in range(line):
                there = lax.rem(place_ref[LINE_AT] + k, line) == j
                pl.when(there)(functools.partial(fill, j, k))

    return pl.pallas_call(
        kernel,
        grid_spec=pltpu.PrefetchScalarGridSpec(
            num_scalar_prefetch=1,
            grid=(1,),
            in_specs=[alone, first, first, last, last],
            out_specs=[part] * line,
        ),
        out_shape=[jax.ShapeDtypeStruct((rows, columns), jnp.bfloat16)] * line,
        compiler_params=pltpu.CompilerParams(vmem_limit_bytes=VMEM_LIMIT),
        cost_estimate=FREE,
    )(place, kept, *near, *far)


def input_terms(lefts, rights, dp, seq):
    count, model = lefts[0].shape
    columns = rights[0].shape[1]
    rest = model // (dp * seq)
    block, strip = model // 2, math.gcd(columns, 256)
    halves = dp // 2

    def kernel(left_a, left_b, right_a, right_b, out_ref, turned):
        turned[:, :count] = left_a[...].T
        turned[:, count:] = left_b[...].T

        def body(n, carry):
            at = pl.ds(pl.multiple_of(n * strip, strip), strip)
            term = matmul(turned[:, :count], right_a[:, at])
            term = (term + matmul(turned[:, count:], right_b[:, at])).astype(jnp.bfloat16)
            term = term.reshape(halves, seq, rest, strip)
            for i in range(halves):
                out_ref[:, i, :, at] = term[i]
            return carry

        lax.fori_loop(0, columns // strip, body, 0)

    left_spec = pl.BlockSpec((count, block), lambda i: (0, i))
    right_spec = pl.BlockSpec((count, columns), lambda i: (0, 0))
    return pl.pallas_call(
        kernel,
        grid=(2,),
        in_specs=[left_spec] * 2 + [right_spec] * 2,
        out_specs=pl.BlockSpec((seq, halves, rest, columns), lambda i: (0, i, 0, 0)),
        out_shape=jax.ShapeDtypeStruct((seq, dp, rest, columns), jnp.bfloat16),
        scratch_shapes=[pltpu.VMEM((block, 2 * count), jnp.bfloat16)],
        compiler_params=pltpu.CompilerParams(vmem_limit_bytes=VMEM_LIMIT),
        cost_estimate=cost(6),
    )(*lefts, *rights)


def tile_facts(place, span, tile):
    line = pl.num_programs(0) // 2
    row_tokens = line * 2 * span
    half = tile // line
    key_first = half * row_tokens + (tile % line) * 2 * span
    query_first = [(place[2] ^ j) * row_tokens + (2 * place[0] + place[1]) * span for j in (0, 1)]
    return key_first, query_first


def reach(key_first, keys, query_first, queries):
    key_last, query_last = key_first + keys - 1, query_first + queries - 1
    live = (key_first <= query_last) & (query_first - key_last < WINDOW)
    plain = (key_last < query_first) & (query_last - key_first < WINDOW)
    return live & plain, live & jnp.logical_not(plain)


def row_of(columns, scale):
    ones = jnp.full((8, columns.shape[1]), scale, jnp.float32)
    return lax.dot_general(
        ones,
        columns,
        (((1,), (1,)), ((), ())),
        precision=lax.Precision.HIGHEST,
        preferred_element_type=jnp.float32,
    )


def forward_kernel(
    place, query_ref, own_ref, other_ref, code_ref, segment_ref, out_ref, log_ref, acc, total
):
    tile = pl.program_id(0)
    span = query_ref.shape[1]
    key_first, query_first = tile_facts(place, span, tile)

    @pl.when(tile == 0)
    def _():
        acc[...] = jnp.zeros_like(acc)
        total[...] = jnp.zeros_like(total)

    def step(j, masked):
        keys = jnp.concatenate([own_ref[0, 0, :, :HEAD_DIM], other_ref[0, 0, :, :HEAD_DIM]], axis=0)
        values = jnp.concatenate(
            [own_ref[0, 0, :, HEAD_DIM:], other_ref[0, 0, :, HEAD_DIM:]], axis=0
        )
        allowed = code_ref[0, 0] == segment_ref[j]
        if masked:
            lane = lax.broadcasted_iota(jnp.int32, (1, 2 * span), 1)
            key_pos = key_first + lane + jnp.where(lane < span, place[1], -place[1]) * span
            query_pos = query_first[j] + lax.broadcasted_iota(jnp.int32, (span, 1), 0)
            back = query_pos - key_pos
            allowed = (allowed & (back > 0) & (back < WINDOW)) | (back == 0)
        for h in range(GROUP):
            query = query_ref[j, :, h * HEAD_DIM : (h + 1) * HEAD_DIM]
            scores = matmul_t(query, keys)
            weights = jnp.exp2(log2_scale * jnp.tanh(scores * score_scale))
            weights = jnp.where(allowed, weights, 0.0)
            total[j, h] += jnp.sum(weights, axis=-1, keepdims=True)
            acc[j, h] += matmul(weights.astype(jnp.bfloat16), values)

    for j in (0, 1):
        plain, masked = reach(key_first, 2 * span, query_first[j], span)
        pl.when(plain)(functools.partial(step, j, False))
        pl.when(masked)(functools.partial(step, j, True))

    @pl.when(tile == pl.num_programs(0) - 1)
    def _():
        for j in (0, 1):
            for h in range(GROUP):
                out_ref[j, :, h * HEAD_DIM : (h + 1) * HEAD_DIM] = (
                    acc[j, h] / total[j, h]
                ).astype(jnp.bfloat16)
                column = jnp.broadcast_to(jnp.log2(total[j, h]), (span, 128))
                log_ref[j, :, h * span : (h + 1) * span] = row_of(column, 1.0 / 128)


def backward_kernel(
    place, query_ref, grad_ref, attended_ref, own_ref, other_ref, code_ref, log_ref, segment_ref,
    query_grad_ref, own_grad_ref, other_grad_ref,
    queries, grads, query_acc, key_acc, value_acc, delta,
):
    tile = pl.program_id(0)
    span = query_ref.shape[1]
    key_first, query_first = tile_facts(place, span, tile)

    @pl.when(tile == 0)
    def _():
        query_acc[...] = jnp.zeros_like(query_acc)
        for j in (0, 1):
            for h in range(GROUP):
                rows, columns = pl.ds(h * span, span), slice(h * HEAD_DIM, (h + 1) * HEAD_DIM)
                queries[j, rows, :] = query_ref[j, :, columns]
                grads[j, rows, :] = grad_ref[j, :, columns]
                products = grad_ref[j, :, columns].astype(jnp.float32) * attended_ref[
                    j, :, columns
                ].astype(jnp.float32)
                delta[j, :, h * span : (h + 1) * span] = row_of(products, 1.0)

    def step(j, side, side_first, keys, values, masked):
        allowed = code_ref[0, 0, pl.ds(side * span, span), :] == segment_ref[j, 0:1, :]
        if masked:
            lane = lax.broadcasted_iota(jnp.int32, (1, GROUP * span), 1)
            query_pos = query_first[j] + jnp.where(lane < span, lane, lane - span)
            key_pos = side_first + lax.broadcasted_iota(jnp.int32, (span, 1), 0)
            back = query_pos - key_pos
            allowed = (allowed & (back > 0) & (back < WINDOW)) | (back == 0)
        squashed = jnp.tanh(matmul_t(keys, queries[j]) * score_scale)
        weights = jnp.exp2(log2_scale * squashed - log_ref[j, 0:1, :])
        weights = jnp.where(allowed, weights, 0.0)
        grad_weights = matmul_t(values, grads[j])
        value_acc[side] += matmul(weights.astype(jnp.bfloat16), grads[j])
        grad_scores = weights * (grad_weights - delta[j, 0:1, :]) * (1.0 - squashed * squashed)
        grad_scores = grad_scores.astype(jnp.bfloat16)
        key_acc[side] += matmul(grad_scores, queries[j])
        query_acc[j] += inner_t(grad_scores, keys)

    key_acc[...] = jnp.zeros_like(key_acc)
    value_acc[...] = jnp.zeros_like(value_acc)
    scale = HEAD_DIM ** (-0.5)
    for side, key_ref, grad_out in ((0, own_ref, own_grad_ref), (1, other_ref, other_grad_ref)):
        side_first = key_first + (place[1] if side == 0 else 1 - place[1]) * span

        def on_side(j, masked, side=side, side_first=side_first, key_ref=key_ref):
            keys, values = key_ref[0, 0, :, :HEAD_DIM], key_ref[0, 0, :, HEAD_DIM:]
            step(j, side, side_first, keys, values, masked)

        for j in (0, 1):
            plain, masked = reach(side_first, span, query_first[j], span)
            pl.when(plain)(functools.partial(on_side, j, False))
            pl.when(masked)(functools.partial(on_side, j, True))
        grad_out[0, 0, :, :HEAD_DIM] = (key_acc[side] * scale).astype(jnp.bfloat16)
        grad_out[0, 0, :, HEAD_DIM:] = value_acc[side].astype(jnp.bfloat16)

    @pl.when(tile == pl.num_programs(0) - 1)
    def _():
        for j in (0, 1):
            for h in range(GROUP):
                query_grad_ref[j, :, h * HEAD_DIM : (h + 1) * HEAD_DIM] = (
                    query_acc[j, h * span : (h + 1) * span, :] * scale
                ).astype(jnp.bfloat16)


def whole(*shape):
    return pl.BlockSpec(shape, lambda tile, place: (0,) * len(shape))


def tile_specs(line, span):
    def key_place(tile, place):
        return (tile % line, (tile // line) ^ place[2], 0, 0)

    def code_place(tile, place):
        return ((tile // line) ^ place[2], tile % line, 0, 0)

    return pl.BlockSpec((1, 1, span, 2 * HEAD_DIM), key_place), code_place


def attention_forward(place, queries, own, other, codes, segments):
    line, _, span, width = own.shape
    tile_spec, code_place = tile_specs(line, span)
    return pl.pallas_call(
        forward_kernel,
        grid_spec=pltpu.PrefetchScalarGridSpec(
            num_scalar_prefetch=1,
            grid=(2 * line,),
            in_specs=[
                whole(2, span, width),
                tile_spec,
                tile_spec,
                pl.BlockSpec((1, 1, 1, 2 * span), code_place),
                whole(2, span, 1),
            ],
            out_specs=[whole(2, span, width), whole(2, 8, GROUP * span)],
            scratch_shapes=[
                pltpu.VMEM((2, GROUP, span, HEAD_DIM), jnp.float32),
                pltpu.VMEM((2, GROUP, span, 1), jnp.float32),
            ],
        ),
        out_shape=[
            jax.ShapeDtypeStruct((2, span, width), jnp.bfloat16),
            jax.ShapeDtypeStruct((2, 8, GROUP * span), jnp.float32),
        ],
        compiler_params=pltpu.CompilerParams(vmem_limit_bytes=VMEM_LIMIT),
        cost_estimate=cost(6),
    )(place, queries, own, other, codes, segments)


def attention_backward(place, queries, grads, attended, own, other, codes, logs, segments):
    line, _, span, width = own.shape
    tile_spec, code_place = tile_specs(line, span)
    return pl.pallas_call(
        backward_kernel,
        grid_spec=pltpu.PrefetchScalarGridSpec(
            num_scalar_prefetch=1,
            grid=(2 * line,),
            in_specs=[
                whole(2, span, width),
                whole(2, span, width),
                whole(2, span, width),
                tile_spec,
                tile_spec,
                pl.BlockSpec((1, 1, 2 * span, 1), code_place),
                whole(2, 8, GROUP * span),
                whole(2, 8, GROUP * span),
            ],
            out_specs=[whole(2, span, width), tile_spec, tile_spec],
            scratch_shapes=[
                pltpu.VMEM((2, GROUP * span, HEAD_DIM), jnp.bfloat16),
                pltpu.VMEM((2, GROUP * span, HEAD_DIM), jnp.bfloat16),
                pltpu.VMEM((2, GROUP * span, HEAD_DIM), jnp.float32),
                pltpu.VMEM((2, span, HEAD_DIM), jnp.float32),
                pltpu.VMEM((2, span, HEAD_DIM), jnp.float32),
                pltpu.VMEM((2, 8, GROUP * span), jnp.float32),
            ],
        ),
        out_shape=[
            jax.ShapeDtypeStruct((2, span, width), jnp.bfloat16),
            jax.ShapeDtypeStruct(own.shape, jnp.bfloat16),
            jax.ShapeDtypeStruct(own.shape, jnp.bfloat16),
        ],
        compiler_params=pltpu.CompilerParams(vmem_limit_bytes=VMEM_LIMIT),
        cost_estimate=cost(12),
    )(place, queries, grads, attended, own, other, codes, logs, segments)


def body(
    tokens, pre_attention, post_attention, pre_feedforward, post_feedforward, w_query, key_weight,
    value_weight, w_output, w_gate, w_up, w_down, document_index, token_padding_mask, cotangent,
):
    bf16, f32 = jnp.bfloat16, jnp.float32
    dp, seq = lax.axis_size("dp"), lax.axis_size("seq")
    line, groups = seq // 2, dp // KEY_VALUE_HEADS
    dp_at, seq_at = lax.axis_index("dp"), lax.axis_index("seq")
    line_at, core = seq_at // 2, seq_at % 2
    head = dp_at % KEY_VALUE_HEADS
    half_bit = dp_at % 2
    _, span, model = tokens.shape
    rows = w_query.shape[0]
    ff = w_gate.shape[1]
    ff_rows = w_down.shape[0]
    ff_part = ff // line
    width = GROUP * HEAD_DIM

    order = Order()

    def attention_codes():
        sequence = dp_at // 2

        def by_pair(table):
            both = jnp.stack([pick(table, 0, sequence), pick(table, 0, sequence ^ 1)])
            both = both.reshape(2, 2, line, 2, span)
            both = jnp.where(half_bit == 1, both[:, ::-1], both)
            return jnp.where(core == 1, both[:, :, :, ::-1], both)

        segments = by_pair(document_index)
        codes = jnp.where(by_pair(token_padding_mask) == 1, segments, -1)
        return codes.reshape(2, 2, line, 2 * span), pick(segments[:, :, :, 0], 2, line_at)

    quad = groups == 1
    place = jnp.stack([line_at, core, half_bit, head]).astype(jnp.int32)
    inputs = tokens[0].astype(f32)
    flipped = pack_heads(place, w_query, key_weight, value_weight)
    split = split_columns(place, w_gate, w_up, dp, line)
    if quad:
        flipped, split, place = order(flipped, split, place)
        mixed = [flipped[0]] + [across(flipped[k], k) for k in (1, 2, 3)]
        normed_in = normed(inputs, pre_attention).astype(bf16)
        mixed, normed_in, split = order(order_heads(place, mixed), normed_in, split)
        near_normed = gather_quad_near(normed_in)
        in_weight = lax.all_gather(mixed, "seq", axis=1).reshape(model, 2 * width)
    else:
        normed_in = normed(inputs, pre_attention).astype(bf16)
        near_normed = gather_quad_near(normed_in)
        blocks = lax.all_gather(order_heads(place, flipped), ("dp", "seq"), axis=1, tiled=True)
        in_weight = pick(blocks, 0, head)

    per_device = line * rows
    split = exchange_line_parts(split)

    def ordered_split(split):
        (whole,) = deposit(
            place,
            [empty((2, line, rows, ff_part), bf16)],
            split,
            [
                (k, lambda at, w=w: (w,), 0, lambda at, w=w, k=k: (w, (at[LINE_AT] + line - k) % line))
                for k in range(line)
                for w in (0, 1)
            ],
        )
        return whole.reshape(2 * per_device, ff_part)

    def near_blocks(own):
        return gather_quad_near(own) if quad else (lax.all_gather(own, "dp", axis=0),)

    def far_blocks(near):
        return (gather_quad_far(*near),) if quad else ()

    def swap_all(blocks):
        return [swap_core(block) for block in blocks]

    down_weight = empty((dp, 2, ff_rows, model), bf16)
    gate_weight = empty((dp, line, 2, rows, ff_part), bf16)
    up_weight = empty((dp, line, 2, rows, ff_part), bf16)

    def sides(numbers, mine, swapped):
        for k, *blocks in zip(numbers, mine, swapped):
            for other, block in enumerate(blocks):
                yield k, other, block

    def at_dp(at, k):
        return at[HEAD_AT] ^ k if quad else pl.ds(0, dp)

    def fill_down(weight, numbers, mine, swapped):
        sources, moves = [], []
        for k, other, block in sides(numbers, mine, swapped):
            target = lambda at, k=k, other=other: (at_dp(at, k), at[CORE_AT] ^ other)
            moves.append((len(sources), None, 0, target))
            sources.append(block)
        return deposit(place, [weight], sources, moves)[0] if sources else weight

    def fill_in(gate, up, numbers, mine, swapped):
        sources, moves = [], []
        for k, other, block in sides(numbers, mine, swapped):
            for which in (0, 1):
                source = lambda at, which=which: (slice(None),) * (not quad) + (which,)
                target = lambda at, k=k, other=other: (
                    at_dp(at, k), slice(None), at[CORE_AT] ^ other
                )
                moves.append((len(sources), source, which, target))
            lead = () if quad else (dp,)
            sources.append(block.reshape(lead + (2, line, rows, ff_part)))
        return deposit(place, [gate, up], sources, moves) if sources else (gate, up)

    def project(pair_rows):
        projected = matmul(pair_rows, in_weight).astype(bf16).reshape(2, span, 2 * width)
        return projected[..., :width], projected[..., width:]

    codes, own_segments = attention_codes()
    row_codes = codes[:, :, :, None, :]
    column_segments = own_segments[..., None]
    near_normed, in_weight, split, row_codes, column_segments = order(
        near_normed, in_weight, split, row_codes, column_segments
    )
    far_normed = gather_quad_far_parts(*near_normed)
    first_rows = jnp.concatenate([normed_in, near_normed[0]], axis=0)
    first_queries, first_keys = project(first_rows)
    first_queries, first_keys, first_rows, far_normed = order(
        first_queries, first_keys, first_rows, far_normed
    )
    first_own = gather_line(first_keys)
    gate_up = ordered_split(split)
    second_rows = jnp.concatenate([near_normed[1], *far_normed], axis=0)
    second_queries, second_keys = project(second_rows)
    second_queries, second_keys, second_rows, gate_up = order(
        second_queries, second_keys, second_rows, gate_up
    )
    second_own = gather_line(second_keys)
    normed_rows = [first_rows, second_rows]
    near_in = near_blocks(gate_up)
    swapped = swap_all([gate_up] if quad else [])
    column_codes = [codes[pair][..., None] for pair in (0, 1)]
    lane_segments = jnp.broadcast_to(
        own_segments[:, :, None, None, :], (2, 2, 8, GROUP, span)
    ).reshape(2, 2, 8, GROUP * span)
    lane_segments = [lane_segments[0], lane_segments[1]]
    swapped, first_own, column_codes, lane_segments = order(
        swapped, first_own, column_codes, lane_segments
    )
    first_other = order(swap_core(first_own))
    attended, log_total = [None, None], [None, None]
    attended[0], log_total[0] = attention_forward(
        place, first_queries, first_own, first_other, row_codes[0], column_segments[0]
    )
    if quad:
        gate_weight, up_weight = fill_in(gate_weight, up_weight, (0,), [gate_up], swapped)
    attended[0], log_total[0], gate_weight, up_weight, near_in = order(
        attended[0], log_total[0], gate_weight, up_weight, near_in
    )
    far_in = far_blocks(near_in)
    swapped = swap_all(near_in)
    second_own, swapped, far_in = order(second_own, swapped, far_in)
    second_other = swap_core(second_own)
    if quad:
        out_weight = lax.all_gather(after(w_output, second_own), "seq", axis=0, tiled=True)
    else:
        out_weight = lax.dynamic_slice_in_dim(
            lax.all_gather(w_output, ("dp", "seq"), axis=0, tiled=True), head * width, width
        )
    numbers = (1, 2, 3) if quad else (0,)
    near_swapped = swapped
    second_other = order(second_other)
    swapped = swap_all(far_in)
    attended[1], log_total[1] = attention_forward(
        place, second_queries, second_own, second_other, row_codes[1], column_segments[1]
    )
    attended, log_total, out_weight, swapped = order(attended, log_total, out_weight, swapped)
    in_blocks, swapped = list(near_in) + list(far_in), near_swapped + swapped
    queries = [first_queries, second_queries]
    own_keys, other_keys = [first_own, second_own], [first_other, second_other]

    def activation(gate_in, up_in):
        return jax.nn.gelu(gate_in, approximate=True) * up_in

    step = span // 2
    chunks = [slice(0, step), slice(step, 2 * step)]
    grad_output = cotangent[0].astype(f32)

    def into_feedforward(part, kept, near, far):
        attn_out = scatter_quad_end(kept, near, far)
        residual = inputs[part] + normed(attn_out, post_attention)
        return attn_out, residual, normed(residual, pre_feedforward).astype(bf16)

    sent_a, kept_a = order(quad_terms(attended, out_weight, chunks[0], False))
    near_a = scatter_quad_near(sent_a)
    sent_b, kept_b = quad_terms(attended, out_weight, chunks[1], False)
    near_a, sent_b, kept_b = order(near_a, sent_b, kept_b)
    far_a = scatter_quad_far(kept_a, near_a)
    far_a, sent_b = order(far_a, sent_b)
    near_b = scatter_quad_near(sent_b)
    attn_out_a, residual_a, mid_a = order(into_feedforward(chunks[0], kept_a, near_a, far_a))
    mid_rows_a = gather_line(mid_a).reshape(line * step, model)
    near_b = order(near_b)
    far_b = order(scatter_quad_far(kept_b, near_b))
    attn_out_b, residual_b, mid_b = order(into_feedforward(chunks[1], kept_b, near_b, far_b))
    mid_rows_b = gather_line(mid_b).reshape(line * step, model)
    own_down = after(w_down, far_b[0])
    near_down = near_blocks(own_down)
    gate_weight, up_weight = fill_in(gate_weight, up_weight, numbers, in_blocks, swapped)
    mid_rows_a, gate_weight, up_weight = order(mid_rows_a, gate_weight, up_weight)
    gate_weight = gate_weight.reshape(model, ff_part)
    up_weight = up_weight.reshape(model, ff_part)
    gate_a = matmul(mid_rows_a, gate_weight)
    gate_a, mid_rows_a, near_down = order(gate_a, mid_rows_a, near_down)
    far_down = far_blocks(near_down)
    down_blocks = ([own_down] if quad else []) + list(near_down)
    swapped = swap_all(down_blocks)
    up_a = matmul(mid_rows_a, up_weight)
    gate_a, up_a, far_down, swapped = order(gate_a, up_a, far_down, swapped)
    down_weight = fill_down(down_weight, range(3), down_blocks, swapped)
    swapped = swap_all(far_down)
    down_weight, swapped = order(down_weight, swapped)
    down_weight = fill_down(down_weight, (3,), far_down, swapped)
    down_weight = down_weight.reshape(ff_part, model)

    def feedforward(gate_value, up_value):
        hidden = activation(gate_value, up_value).astype(bf16)
        down_part = matmul(hidden, down_weight).astype(bf16).reshape(line, step, model)
        return gate_value, up_value, hidden, down_part

    def output_of(part, residual, down_out):
        down_out = down_out.astype(f32)
        normed_down, down_back = jax.vjp(normed, down_out, post_feedforward)
        grad_down, gain_part = down_back(grad_output[part])
        return residual + normed_down, grad_down.astype(bf16), gain_part

    def feedforward_back(down_rows, gate_value, up_value):
        grad_hidden = matmul_t(down_rows, down_weight)
        _, act_back = jax.vjp(activation, gate_value, up_value)
        grad_gate, grad_up = act_back(grad_hidden)
        grad_gate, grad_up = grad_gate.astype(bf16), grad_up.astype(bf16)
        mid_part = matmul_t(grad_gate, gate_weight) + matmul_t(grad_up, up_weight)
        return grad_gate, grad_up, mid_part.astype(bf16).reshape(line, step, model)

    def attention_grad(part, residual, attn_out, grad_mid):
        _, mid_back = jax.vjp(normed, residual, pre_feedforward)
        grad_residual, grad_pre = mid_back(grad_mid.astype(f32))
        grad_residual = grad_output[part] + grad_residual
        _, attn_back = jax.vjp(normed, attn_out, post_attention)
        grad_attn, grad_post = attn_back(grad_residual)
        return grad_residual, grad_attn.astype(bf16), grad_pre, grad_post

    gate_a, up_a, hidden_a, down_a = order(feedforward(gate_a, up_a))
    down_a = scatter_line(down_a)
    mid_rows_b = order(mid_rows_b)
    gate_b, up_b, hidden_b, down_b = order(
        feedforward(matmul(mid_rows_b, gate_weight), matmul(mid_rows_b, up_weight))
    )
    down_b = scatter_line(down_b)
    down_a = order(down_a)
    result_a, grad_down_a, post_ff_a = order(output_of(chunks[0], residual_a, down_a))
    down_rows_a = gather_line(grad_down_a).reshape(line * step, model)
    down_b = order(down_b)
    result_b, grad_down_b, post_ff_b = order(output_of(chunks[1], residual_b, down_b))
    down_rows_b = gather_line(grad_down_b).reshape(line * step, model)
    down_rows_a = order(down_rows_a)
    grad_gate_a, grad_up_a, mid_part = order(feedforward_back(down_rows_a, gate_a, up_a))
    grad_mid_a = scatter_line(mid_part)
    down_rows_b = order(down_rows_b)
    grad_gate_b, grad_up_b, mid_part = order(feedforward_back(down_rows_b, gate_b, up_b))
    grad_mid_b = scatter_line(mid_part)
    result = jnp.concatenate([result_a, result_b], axis=0)

    def halves(lefts, rights, inner):
        if inner % 8 == 0:
            return weight_halves(place, lefts, rights, inner)
        term = sum(inner_t(left, right) for left, right in zip(lefts, rights))
        term = term.astype(bf16).reshape(-1, 2, inner, rights[0].shape[1])
        return pick(term, 1, core), pick(term, 1, 1 - core)

    def from_cores(own, moved, inner, plan, *shapes):
        own, moved = own.reshape(dp, inner, -1), moved.reshape(dp, inner, -1)
        if not quad:
            return own + moved
        shapes = [tuple(shape) + (own.shape[-1],) for shape in shapes]
        return combine_quad(place, own, moved, shapes, plan)

    def quad_plan(inner):
        low, high = slice(0, inner // 2), slice(inner // 2, inner)
        plan = [
            [(2, None, slice(0, inner))],
            [(0, 0, low), (4, None, high)],
            [(1, 0, high), (3, None, low)],
            [(0, 1, low), (1, 1, high)],
        ]
        half = inner // 2
        return plan, (2, half), (2, half), (inner,), (half,), (half,)

    def combine(own, moved, inner):
        parts = from_cores(own, moved, inner, *quad_plan(inner))
        return (parts[:2], parts[2:]) if quad else (parts, ())

    def near_sums(sent):
        return scatter_quad_near(sent) if quad else ()

    def far_sums(kept, near):
        if not quad:
            return ()
        return across(add_second(kept[1], near[0]), 2), across(add_second(kept[2], near[1]), 1)

    def line_parts(sent, kept, near, far):
        if quad:
            return to_line(place, kept[0], near, far, line)
        total = lax.psum_scatter(sent, "dp", scatter_dimension=0).reshape(line, rows, ff_part)
        return [pick(total, 0, (line_at + k) % line) for k in range(line)]

    mid_rows, hiddens, down_rows = (mid_rows_a, mid_rows_b), (hidden_a, hidden_b), (
        down_rows_a, down_rows_b
    )
    grad_gates, grad_ups = (grad_gate_a, grad_gate_b), (grad_up_a, grad_up_b)
    gate_own, gate_other = halves(mid_rows, grad_gates, rows)
    grad_mid_a, gate_own, gate_other = order(grad_mid_a, gate_own, gate_other)
    gate_other = swap_core(gate_other)
    grad_residual_a, grad_attn, pre_ff_a, post_attn_a = attention_grad(
        chunks[0], residual_a, attn_out_a, grad_mid_a
    )
    grad_residual_a, grad_attn, pre_ff_a, post_attn_a, gate_other = order(
        grad_residual_a, grad_attn, pre_ff_a, post_attn_a, gate_other
    )
    near_a = gather_quad_near(grad_attn)
    gate_sent, gate_kept = combine(gate_own, gate_other, per_device)
    near_a, gate_sent, gate_kept, mid_rows, grad_ups = order(
        near_a, gate_sent, gate_kept, mid_rows, grad_ups
    )
    far_a = gather_quad_far_parts(*near_a)
    gate_near = near_sums(gate_sent)
    up_own, up_other = halves(mid_rows, grad_ups, rows)
    far_a, gate_near, up_own, up_other = order(far_a, gate_near, up_own, up_other)
    quad_a = [grad_attn, *near_a, jnp.concatenate(far_a, axis=0)]
    gate_far = far_sums(gate_kept, gate_near)
    up_other = swap_core(up_other)
    grad_mid_b = order(grad_mid_b)
    grad_residual_b, grad_attn, pre_ff_b, post_attn_b = order(
        attention_grad(chunks[1], residual_b, attn_out_b, grad_mid_b)
    )
    near_b = gather_quad_near(grad_attn)
    up_sent, up_kept = combine(up_own, up_other, per_device)
    near_b, up_sent, up_kept, gate_far, quad_a = order(near_b, up_sent, up_kept, gate_far, quad_a)
    far_b = gather_quad_far_parts(*near_b)
    grad_residual = jnp.concatenate([grad_residual_a, grad_residual_b], axis=0)

    def attention_rows(blocks_a, blocks_b):
        return jnp.concatenate(
            [block for pair in zip(blocks_a, blocks_b) for block in pair], axis=0
        )

    def attended_grad(attn_rows):
        return matmul_t(attn_rows, out_weight).astype(bf16).reshape(2, span, width)

    def attend_back(pair, grad_attended):
        return attention_backward(
            place, queries[pair], grad_attended, attended[pair], own_keys[pair], other_keys[pair],
            column_codes[pair], log_total[pair], lane_segments[pair],
        )

    def owned_gains(terms):
        terms = jnp.stack(terms, axis=1)
        count = terms.shape[1]
        if not quad:
            return lax.psum_scatter(terms, ("dp", "seq"), scatter_dimension=0, tiled=True)
        terms = terms.reshape(dp, line, 2, rows * count)
        terms = sum(
            (across(pick(terms, 0, head ^ k), k) for k in (1, 2, 3)), pick(terms, 0, head)
        )
        terms = pick(terms, 1, core) + swap_core(pick(terms, 1, 1 - core))
        return jnp.sum(exchange_line(terms, line_at), axis=0).reshape(rows, count)

    def project_back(grad_queries, key_grads):
        grad_projected = jnp.concatenate([grad_queries, key_grads], axis=2)
        return grad_projected, grad_projected.reshape(2 * span, 2 * width)

    first_attn = attention_rows(quad_a[:2], [grad_attn, near_b[0]])
    gate_line = line_parts(gate_sent, gate_kept, gate_near, gate_far)
    far_b, grad_attended, gate_line = order(far_b, attended_grad(first_attn), gate_line)
    gate_line = exchange_line_parts(gate_line)
    up_near = near_sums(up_sent)
    first_grads, own_grad, other_grad, far_b, gate_line = order(
        *attend_back(0, grad_attended), far_b, gate_line
    )
    swapped = swap_core(other_grad)
    second_attn = attention_rows(quad_a[2:], [near_b[1], jnp.concatenate(far_b, axis=0)])
    grad_attended = attended_grad(second_attn)
    swapped, grad_attended = order(swapped, grad_attended)
    first_key_grads, up_near = order(own_grad + swapped, up_near)
    first_key_grads = scatter_line(first_key_grads)
    up_far = far_sums(up_kept, up_near)
    second_grads, own_grad, other_grad, up_far = order(*attend_back(1, grad_attended), up_far)
    swapped = swap_core(other_grad)
    up_line = line_parts(up_sent, up_kept, up_near, up_far)
    swapped, up_line = order(swapped, up_line)
    second_key_grads, first_key_grads, hiddens, down_rows = order(
        own_grad + swapped, first_key_grads, hiddens, down_rows
    )
    second_key_grads = scatter_line(second_key_grads)

    down_own, down_other = halves(hiddens, down_rows, ff_rows)
    output_term = inner_t(attended[0].reshape(2 * span, width), first_attn)
    output_term += inner_t(attended[1].reshape(2 * span, width), second_attn)
    output_term = output_term.astype(bf16)
    second_key_grads, up_line, down_own, down_other, output_term = order(
        second_key_grads, up_line, down_own, down_other, output_term
    )

    first_grad, first_rows = project_back(first_grads, first_key_grads)
    second_grad, second_rows = project_back(second_grads, second_key_grads)
    sent, kept = quad_terms((first_grad, second_grad), in_weight, slice(0, span), True)
    sent, kept, first_rows, second_rows = order(sent, kept, first_rows, second_rows)
    near = scatter_quad_near(sent)
    if quad:
        output_shard = lax.psum_scatter(output_term, "seq", scatter_dimension=0, tiled=True)
    else:
        spread = jnp.zeros((KEY_VALUE_HEADS, width, model), bf16).at[head].set(output_term)
        output_shard = lax.psum_scatter(
            spread.reshape(KEY_VALUE_HEADS * width, model),
            ("dp", "seq"),
            scatter_dimension=0,
            tiled=True,
        )
    up_line = exchange_line_parts(up_line)
    down_other = swap_core(down_other)
    if quad:
        in_term = order(input_terms(normed_rows, (first_rows, second_rows), dp, seq))
        in_part = lax.psum_scatter(
            in_term.reshape(model, 2 * width), "seq", scatter_dimension=0, tiled=True
        )
        near, up_line = order(near, up_line)
        far = scatter_quad_far(kept, near)
        down_sent, down_kept = combine(down_own, down_other, ff_rows)
        far, down_sent, down_kept = order(far, down_sent, down_kept)
        down_near = scatter_quad_near(down_sent)
    else:
        in_term = inner_t(normed_rows[0], first_rows) + inner_t(normed_rows[1], second_rows)
        near, in_term = order(near, in_term.astype(bf16))
        far = order(scatter_quad_far(kept, near))
        down_mine, _ = combine(down_own, down_other, ff_rows)
        down_shard = lax.psum_scatter(down_mine, "dp", scatter_dimension=0).astype(f32)
    grad_in = scatter_quad_end(kept, near, far)
    _, in_back = jax.vjp(normed, inputs, pre_attention)
    grad_inputs, grad_pre_attn = in_back(grad_in)
    grad_pre_attn, grad_inputs = order(grad_pre_attn, grad_inputs)
    gains = owned_gains(
        [grad_pre_attn, post_attn_a + post_attn_b, pre_ff_a + pre_ff_b, post_ff_a + post_ff_b]
    )
    tokens_grad = grad_residual + grad_inputs
    if quad:
        gains, down_near, in_part = order(gains, down_near, in_part)
        down_far = scatter_quad_far(down_kept, down_near)
        down_shard = scatter_quad_end(down_kept, down_near, down_far)
    gate_shard, up_shard = join_columns(place, gate_line, dp), join_columns(place, up_line, dp)
    if quad:
        part_shard = exchange_quad(in_part.reshape(dp, rows, 2 * width), head)
    else:
        spread = jnp.zeros((KEY_VALUE_HEADS, model, 2 * width), bf16).at[head].set(in_term)
        part_shard = lax.psum_scatter(spread, ("dp", "seq"), scatter_dimension=1, tiled=True)
    part_shard = part_shard.astype(f32).transpose(1, 0, 2)
    query_shard = part_shard[..., :width].reshape(rows, KEY_VALUE_HEADS * width)
    key_shard = part_shard[..., width : width + HEAD_DIM].reshape(rows, KEY_VALUE_HEADS * HEAD_DIM)
    value_shard = part_shard[..., width + HEAD_DIM :].reshape(rows, KEY_VALUE_HEADS * HEAD_DIM)
    return (
        result[None],
        tokens_grad[None],
        query_shard,
        key_shard,
        value_shard,
        output_shard.astype(f32),
        gate_shard,
        up_shard,
        down_shard,
        gains[:, 0],
        gains[:, 1],
        gains[:, 2],
        gains[:, 3],
    )


def solution(mesh):
    tokens, weights, whole_copy = P("dp", "seq", None), P(("dp", "seq"), None), P()
    gains = P(("dp", "seq"))
    return jax.shard_map(
        body,
        mesh=mesh,
        in_specs=(tokens,) + (whole_copy,) * 4 + (weights,) * 7 + (whole_copy,) * 2 + (tokens,),
        out_specs=(tokens,) * 2 + (weights,) * 7 + (gains,) * 4,
        check_vma=False,
    )
```

```python
import functools
import math

import jax
import jax.numpy as jnp
from jax import lax
from jax.experimental import pallas as pl
from jax.experimental.pallas import tpu as pltpu
from jax.sharding import PartitionSpec as P

KEY_VALUE_HEADS = 4
HEAD_DIM = 256
GROUP = 2
WINDOW = 4096

epsilon = 1e-06
softcap = 50.0
score_scale = HEAD_DIM ** (-0.5) / softcap
log2_scale = softcap * 1.4426950408889634
VMEM_LIMIT = 56 * 1024 * 1024
ANYWHERE = pl.BlockSpec(memory_space=pl.ANY)


def normed(values, gain_vec):
    inv_rms = lax.rsqrt(jnp.mean(values * values, axis=-1, keepdims=True) + epsilon)
    return values * inv_rms * gain_vec


def matmul(a, b):
    return jnp.dot(a, b, preferred_element_type=jnp.float32)


def matmul_t(a, b):
    return lax.dot_general(a, b, (((1,), (1,)), ((), ())), preferred_element_type=jnp.float32)


def inner_t(a, b):
    return lax.dot_general(a, b, (((0,), (0,)), ((), ())), preferred_element_type=jnp.float32)


def across(x, bits):
    return lax.ppermute(x, "dp", [(i, i ^ bits) for i in range(lax.axis_size("dp"))])


def swap_core(x):
    return lax.ppermute(x, "seq", [(i, i ^ 1) for i in range(lax.axis_size("seq"))])


def line_groups():
    count = lax.axis_size("seq")
    return [list(range(core, count, 2)) for core in (0, 1)]


def gather_line(x):
    return lax.all_gather(x, "seq", axis=0, axis_index_groups=line_groups())


def line_route(line, distance):
    return [
        (2 * i + core, 2 * ((i + distance) % line) + core) for i in range(line) for core in (0, 1)
    ]


def exchange_line_parts(parts):
    line = len(parts)
    return [parts[0]] + [lax.ppermute(parts[k], "seq", line_route(line, k)) for k in range(1, line)]


def exchange_line(x, place):
    line = x.shape[0]
    parts = exchange_line_parts([pick(x, 0, (place + k) % line) for k in range(line)])
    for k in range(1, line):
        x = put(x, parts[k], (place + line - k) % line)
    return x


def scatter_line(x):
    return lax.psum_scatter(x, "seq", scatter_dimension=0, axis_index_groups=line_groups())


def scatter_line_steps(x, place):
    line = x.shape[0]
    right = left = None
    for step in range(1, line):
        going = pick(x, 0, jnp.clip(line - step + place, 0, line - 1))
        coming = pick(x, 0, jnp.clip(step - line + place, 0, line - 1))
        right = going if right is None else going + right
        left = coming if left is None else coming + left
        right_route = [(2 * i + c, 2 * i + 2 + c) for i in range(step) for c in (0, 1)]
        left_route = [
            (2 * (line - 1 - i) + c, 2 * (line - 2 - i) + c) for i in range(step) for c in (0, 1)
        ]
        right = lax.ppermute(right, "seq", right_route)
        left = lax.ppermute(left, "seq", left_route)
    f32 = jnp.float32
    return pick(x, 0, place).astype(f32) + right.astype(f32) + left.astype(f32)


def gather_quad_near(x):
    return across(x, 1), across(x, 2)


def gather_quad_far_parts(one, two):
    half = one.shape[0] // 2
    return across(two[:half], 1), across(one[half:], 2)


def gather_quad_far(one, two):
    return jnp.concatenate(gather_quad_far_parts(one, two), axis=0)


def gather_quad(x):
    one, two = gather_quad_near(x)
    return [x, one, two, gather_quad_far(one, two)]


def scatter_quad_near(sent):
    return across(sent[0], 1), across(sent[1], 2)


def scatter_quad_far(kept, near):
    return across(kept[1] + near[0][1], 2), across(kept[2] + near[1][1], 1)


def scatter_quad_end(kept, near, far):
    half = kept[0].shape[0] // 2
    f32 = jnp.float32
    low = kept[0][:half].astype(f32) + near[0][0].astype(f32) + far[0].astype(f32)
    high = kept[0][half:].astype(f32) + near[1][0].astype(f32) + far[1].astype(f32)
    return jnp.concatenate([low, high], axis=0)


def flip_order(x, bits):
    pairs = x.reshape((2, 2) + x.shape[1:])
    pairs = jnp.where(bits % 2 == 1, pairs[:, ::-1], pairs)
    pairs = jnp.where(bits // 2 == 1, pairs[::-1], pairs)
    return pairs.reshape(x.shape)


def exchange_quad(x, place):
    parts = flip_order(x, place)
    return exchange_quad_end([parts[0]] + [across(parts[k], k) for k in (1, 2, 3)], place)


def exchange_quad_end(parts, place):
    return flip_order(jnp.stack(parts), place)


def pick(x, axis, index):
    return lax.dynamic_index_in_dim(x, index, axis, keepdims=False)


def put(x, part, *index):
    for _ in index:
        part = part[None]
    return lax.dynamic_update_slice(x, part, index + (0,) * (x.ndim - len(index)))


def after(x, *others):
    def kernel(x_ref, *rest):
        rest[-1][...] = x_ref[...]

    return pl.pallas_call(
        kernel,
        in_specs=[pl.BlockSpec(memory_space=pltpu.VMEM)] + [ANYWHERE] * len(others),
        out_specs=pl.BlockSpec(memory_space=pltpu.VMEM),
        out_shape=jax.ShapeDtypeStruct(x.shape, x.dtype),
    )(x, *others)


def empty(shape, dtype):
    return pl.pallas_call(
        lambda out_ref: None, out_specs=ANYWHERE, out_shape=jax.ShapeDtypeStruct(shape, dtype)
    )()


class Order:
    def __init__(self):
        self.token = jnp.zeros((8, 128), jnp.float32)

    def __call__(self, *trees):
        leaves, tree = jax.tree.flatten(trees)
        held = pl.pallas_call(
            lambda *refs: None,
            in_specs=[ANYWHERE] * (1 + len(leaves)),
            out_specs=[ANYWHERE] * (1 + len(leaves)),
            out_shape=[jax.ShapeDtypeStruct(x.shape, x.dtype) for x in [self.token, *leaves]],
            input_output_aliases={i: i for i in range(1 + len(leaves))},
        )(self.token, *leaves)
        self.token = held[0]
        out = jax.tree.unflatten(tree, held[1:])
        return out[0] if len(trees) == 1 else out


FREE = pl.CostEstimate(flops=0, bytes_accessed=0, transcendentals=0)


def cost(us):
    return pl.CostEstimate(flops=0, bytes_accessed=int(us * 3.5e6), transcendentals=0)


def deposit(place, targets, sources, moves):
    count = len(targets)

    def kernel(place_ref, *refs):
        source_refs = refs[count : count + len(sources)]
        target_refs, sems = refs[count + len(sources) : -1], refs[-1]
        copies = []
        for n, (source, source_at, target, target_at) in enumerate(moves):
            source_ref, target_ref = source_refs[source], target_refs[target]
            if source_at is not None:
                source_ref = source_ref.at[source_at(place_ref)]
            copies.append(
                pltpu.make_async_copy(source_ref, target_ref.at[target_at(place_ref)], sems.at[n])
            )
            copies[-1].start()
        for copy in copies:
            copy.wait()

    return pl.pallas_call(
        kernel,
        in_specs=[pl.BlockSpec(memory_space=pltpu.SMEM)]
        + [ANYWHERE] * count
        + [pl.BlockSpec(memory_space=pltpu.VMEM)] * len(sources),
        out_specs=[ANYWHERE] * count,
        out_shape=[jax.ShapeDtypeStruct(x.shape, x.dtype) for x in targets],
        scratch_shapes=[pltpu.SemaphoreType.DMA((len(moves),))],
        input_output_aliases={1 + i: i for i in range(count)},
        compiler_params=pltpu.CompilerParams(vmem_limit_bytes=VMEM_LIMIT),
        cost_estimate=FREE,
    )(place, *targets, *sources)


LINE_AT, CORE_AT, HALF_AT, HEAD_AT = range(4)


def pack_heads(place, query, key, value):
    rows, width = query.shape[0], GROUP * HEAD_DIM

    def kernel(place_ref, query_ref, key_ref, value_ref, *out_refs):
        for k, out_ref in enumerate(out_refs):
            head = place_ref[HEAD_AT] ^ k
            first = pl.multiple_of(head * width, width)
            out_ref[:, :width] = query_ref[:, pl.ds(first, width)]
            first = pl.multiple_of(head * HEAD_DIM, HEAD_DIM)
            out_ref[:, width : width + HEAD_DIM] = key_ref[:, pl.ds(first, HEAD_DIM)]
            out_ref[:, width + HEAD_DIM :] = value_ref[:, pl.ds(first, HEAD_DIM)]

    return pl.pallas_call(
        kernel,
        in_specs=[pl.BlockSpec(memory_space=pltpu.SMEM)]
        + [pl.BlockSpec(memory_space=pltpu.VMEM)] * 3,
        out_shape=[jax.ShapeDtypeStruct((rows, 2 * width), query.dtype)] * KEY_VALUE_HEADS,
        compiler_params=pltpu.CompilerParams(vmem_limit_bytes=VMEM_LIMIT),
        cost_estimate=FREE,
    )(place, query, key, value)


def order_heads(place, parts):
    def kernel(place_ref, *refs):
        for k in range(KEY_VALUE_HEADS):
            refs[-1][place_ref[HEAD_AT] ^ k] = refs[k][...]

    return pl.pallas_call(
        kernel,
        in_specs=[pl.BlockSpec(memory_space=pltpu.SMEM)]
        + [pl.BlockSpec(memory_space=pltpu.VMEM)] * KEY_VALUE_HEADS,
        out_shape=jax.ShapeDtypeStruct((KEY_VALUE_HEADS,) + parts[0].shape, parts[0].dtype),
        compiler_params=pltpu.CompilerParams(vmem_limit_bytes=VMEM_LIMIT),
        cost_estimate=FREE,
    )(place, *parts)


def weight_halves(place, lefts, rights, inner):
    rows, model = lefts[0].shape
    columns = rights[0].shape[1]
    block, strip = math.gcd(model, 1152), math.gcd(columns, 256)
    groups = block // (2 * inner)

    def kernel(place_ref, left_a, left_b, right_a, right_b, own_ref, other_ref, turned):
        turned[:, :rows] = left_a[...].T
        turned[:, rows:] = left_b[...].T
        core_here = place_ref[CORE_AT]

        def body(n, carry):
            at = pl.ds(pl.multiple_of(n * strip, strip), strip)
            term = matmul(turned[:, :rows], right_a[:, at])
            term = (term + matmul(turned[:, rows:], right_b[:, at])).astype(jnp.bfloat16)
            term = term.reshape(groups, 2, inner, strip)
            own_ref[:, :, at] = jnp.where(core_here == 0, term[:, 0], term[:, 1])
            other_ref[:, :, at] = jnp.where(core_here == 0, term[:, 1], term[:, 0])
            return carry

        lax.fori_loop(0, columns // strip, body, 0)

    half = pl.BlockSpec((groups, inner, columns), lambda i: (i, 0, 0))
    shape = jax.ShapeDtypeStruct((model // (2 * inner), inner, columns), jnp.bfloat16)
    left_spec = pl.BlockSpec((rows, block), lambda i: (0, i))
    right_spec = pl.BlockSpec((rows, columns), lambda i: (0, 0))
    return pl.pallas_call(
        kernel,
        grid=(model // block,),
        in_specs=[pl.BlockSpec(memory_space=pltpu.SMEM)] + [left_spec] * 2 + [right_spec] * 2,
        out_specs=[half, half],
        out_shape=[shape, shape],
        scratch_shapes=[pltpu.VMEM((block, 2 * rows), jnp.bfloat16)],
        compiler_params=pltpu.CompilerParams(vmem_limit_bytes=VMEM_LIMIT),
        cost_estimate=FREE,
    )(place, *lefts, *rights)


def quad_terms(lefts, weight, part, turned, sent):
    first, count = part.start, part.stop - part.start
    half = count // 2
    model = weight.shape[0] if turned else weight.shape[1]
    if sent:
        plan = [(1, 0, half, 0, 0), (3, 0, half, 0, 1), (2, half, half, 1, 0), (3, half, half, 1, 1)]
        shapes = [(2, half, model), (2, half, model)]
    else:
        plan = [(0, 0, count, 0, None), (2, 0, half, 1, None), (1, half, half, 2, None)]
        shapes = [(count, model), (half, model), (half, model)]
    widths = [pair[0].shape[2] for pair in lefts]

    def kernel(*refs):
        weight_ref, scratch = refs[2 * len(lefts)], refs[-1]
        out_refs = refs[2 * len(lefts) + 1 : -1]
        row = 0
        for k, start, size, _, _ in plan:
            column = 0
            for n, width in enumerate(widths):
                ref = refs[2 * n + k // 2]
                scratch[row : row + size, column : column + width] = ref[
                    k % 2, first + start : first + start + size, :
                ]
                column += width
            row += size
        product = matmul_t if turned else matmul
        term = product(scratch[...], weight_ref[...]).astype(jnp.bfloat16)
        row = 0
        for _, _, size, out, at in plan:
            if at is None:
                out_refs[out][...] = term[row : row + size]
            else:
                out_refs[out][at] = term[row : row + size]
            row += size

    return pl.pallas_call(
        kernel,
        out_shape=[jax.ShapeDtypeStruct(shape, jnp.bfloat16) for shape in shapes],
        scratch_shapes=[pltpu.VMEM((2 * count, sum(widths)), jnp.bfloat16)],
        compiler_params=pltpu.CompilerParams(vmem_limit_bytes=VMEM_LIMIT),
        cost_estimate=cost(1),
    )(*[x for pair in lefts for x in pair], weight)


def split_columns(place, gate, up, dp, line):
    rows, ff = gate.shape
    rest = ff // (dp * line)

    def kernel(place_ref, gate_ref, up_ref, *out_refs):
        def fill(j, k):
            for which, ref in enumerate((gate_ref, up_ref)):
                for i in range(dp):
                    first = (i * line + j) * rest
                    out_refs[k][which, :, i * rest : (i + 1) * rest] = ref[:, first : first + rest]

        for j in range(line):
            for k in range(line):
                there = lax.rem(place_ref[LINE_AT] + k, line) == j
                pl.when(there)(functools.partial(fill, j, k))

    return pl.pallas_call(
        kernel,
        in_specs=[pl.BlockSpec(memory_space=pltpu.SMEM)]
        + [pl.BlockSpec(memory_space=pltpu.VMEM)] * 2,
        out_shape=[jax.ShapeDtypeStruct((2, rows, dp * rest), gate.dtype)] * line,
        compiler_params=pltpu.CompilerParams(vmem_limit_bytes=VMEM_LIMIT),
        cost_estimate=FREE,
    )(place, gate, up)


def join_columns(place, parts, which, dp):
    line = len(parts)
    _, rows, part = parts[0].shape
    rest = part // dp

    def kernel(place_ref, *refs):
        def fill(j, k):
            for i in range(dp):
                first = (i * line + j) * rest
                refs[line][:, first : first + rest] = refs[k][
                    0, :, i * rest : (i + 1) * rest
                ].astype(jnp.float32)

        for j in range(line):
            for k in range(line):
                there = lax.rem(place_ref[LINE_AT] + line - k, line) == j
                pl.when(there)(functools.partial(fill, j, k))

    return pl.pallas_call(
        kernel,
        grid_spec=pltpu.PrefetchScalarGridSpec(
            num_scalar_prefetch=1,
            grid=(1,),
            in_specs=[pl.BlockSpec((1, rows, part), lambda i, place: (which, 0, 0))] * line,
            out_specs=pl.BlockSpec((rows, line * part), lambda i, place: (0, 0)),
        ),
        out_shape=jax.ShapeDtypeStruct((rows, line * part), jnp.float32),
        compiler_params=pltpu.CompilerParams(vmem_limit_bytes=VMEM_LIMIT),
        cost_estimate=FREE,
    )(place, *parts)


def add_second(term, pair):
    rows, columns = term.shape

    def kernel(term_ref, pair_ref, out_ref):
        total = term_ref[...].astype(jnp.float32) + pair_ref[0].astype(jnp.float32)
        out_ref[...] = total.astype(jnp.bfloat16)

    return pl.pallas_call(
        kernel,
        grid=(1,),
        in_specs=[
            pl.BlockSpec((rows, columns), lambda i: (0, 0)),
            pl.BlockSpec((1, rows, columns), lambda i: (1, 0, 0)),
        ],
        out_specs=pl.BlockSpec((rows, columns), lambda i: (0, 0)),
        out_shape=jax.ShapeDtypeStruct((rows, columns), jnp.bfloat16),
        compiler_params=pltpu.CompilerParams(vmem_limit_bytes=VMEM_LIMIT),
        cost_estimate=FREE,
    )(term, pair)


def combine_quad(place, own, other, shapes, plan):
    _, inner, columns = own.shape
    spec = pl.BlockSpec((1, inner, columns), lambda k, place: (place[HEAD_AT] ^ k, 0, 0))

    def kernel(place_ref, own_ref, other_ref, *out_refs):
        total = own_ref[0].astype(jnp.float32) + other_ref[0].astype(jnp.float32)
        total = total.astype(jnp.bfloat16)

        def write(k):
            for out, at, taken in plan[k]:
                if at is None:
                    out_refs[out][...] = total[taken]
                else:
                    out_refs[out][at] = total[taken]

        for k in range(4):
            pl.when(pl.program_id(0) == k)(functools.partial(write, k))

    return pl.pallas_call(
        kernel,
        grid_spec=pltpu.PrefetchScalarGridSpec(
            num_scalar_prefetch=1,
            grid=(4,),
            in_specs=[spec, spec],
            out_specs=[
                pl.BlockSpec(shape, lambda k, place, rank=len(shape): (0,) * rank)
                for shape in shapes
            ],
        ),
        out_shape=[jax.ShapeDtypeStruct(shape, jnp.bfloat16) for shape in shapes],
        compiler_params=pltpu.CompilerParams(vmem_limit_bytes=VMEM_LIMIT),
        cost_estimate=FREE,
    )(place, own, other)


def to_line(place, terms, line):
    count, columns = terms[0][0].shape
    rows, half = count // line, count // 2
    alone = pl.BlockSpec((count, columns), lambda i, place: (0, 0))
    first = pl.BlockSpec((1, half, columns), lambda i, place: (0, 0, 0))
    last = pl.BlockSpec((half, columns), lambda i, place: (0, 0))
    part = pl.BlockSpec((len(terms), rows, columns), lambda i, place: (0, 0, 0))

    def kernel(place_ref, *refs):
        def fill(j, k):
            start, high = j * rows % half, j * rows // half
            for which in range(len(terms)):
                kept_ref, *near_refs = refs[5 * which : 5 * which + 3]
                far_ref = refs[5 * which + 3 + high]
                total = kept_ref[j * rows : (j + 1) * rows].astype(jnp.float32)
                total = total + near_refs[high][0, start : start + rows].astype(jnp.float32)
                total = total + far_ref[start : start + rows].astype(jnp.float32)
                refs[5 * len(terms) + k][which] = total.astype(jnp.bfloat16)

        for j in range(line):
            for k in range(line):
                there = lax.rem(place_ref[LINE_AT] + k, line) == j
                pl.when(there)(functools.partial(fill, j, k))

    return pl.pallas_call(
        kernel,
        grid_spec=pltpu.PrefetchScalarGridSpec(
            num_scalar_prefetch=1,
            grid=(1,),
            in_specs=[alone, first, first, last, last] * len(terms),
            out_specs=[part] * line,
        ),
        out_shape=[jax.ShapeDtypeStruct((len(terms), rows, columns), jnp.bfloat16)] * line,
        compiler_params=pltpu.CompilerParams(vmem_limit_bytes=VMEM_LIMIT),
        cost_estimate=FREE,
    )(place, *[x for kept, near, far in terms for x in (kept, *near, *far)])


def input_terms(lefts, rights, dp, seq):
    count, model = lefts[0].shape
    widths = [pair[0].shape[1] for pair in rights]
    rest = model // (dp * seq)
    block, strip = model // 2, math.gcd(*widths, 256)
    halves = dp // 2

    def kernel(left_a, left_b, *refs):
        out_ref, turned = refs[-2:]
        turned[:, :count] = left_a[...].T
        turned[:, count:] = left_b[...].T
        column = 0
        for n, width in enumerate(widths):

            def body(m, carry, right_a=refs[2 * n], right_b=refs[2 * n + 1], column=column):
                at = pl.ds(pl.multiple_of(m * strip, strip), strip)
                to = pl.ds(pl.multiple_of(column + m * strip, strip), strip)
                term = matmul(turned[:, :count], right_a[:, at])
                term = (term + matmul(turned[:, count:], right_b[:, at])).astype(jnp.bfloat16)
                term = term.reshape(halves, seq, rest, strip)
                for i in range(halves):
                    out_ref[:, i, :, to] = term[i]
                return carry

            lax.fori_loop(0, width // strip, body, 0)
            column += width

    left_spec = pl.BlockSpec((count, block), lambda i: (0, i))
    columns = sum(widths)
    return pl.pallas_call(
        kernel,
        grid=(2,),
        in_specs=[left_spec] * 2
        + [pl.BlockSpec((count, width), lambda i: (0, 0)) for width in widths for _ in (0, 1)],
        out_specs=pl.BlockSpec((seq, halves, rest, columns), lambda i: (0, i, 0, 0)),
        out_shape=jax.ShapeDtypeStruct((seq, dp, rest, columns), jnp.bfloat16),
        scratch_shapes=[pltpu.VMEM((block, 2 * count), jnp.bfloat16)],
        compiler_params=pltpu.CompilerParams(vmem_limit_bytes=VMEM_LIMIT),
        cost_estimate=cost(6),
    )(*lefts, *[x for pair in rights for x in pair])


def tile_facts(place, span, tile):
    line = pl.num_programs(0) // 2
    row_tokens = line * 2 * span
    half = tile // line
    key_first = half * row_tokens + (tile % line) * 2 * span
    query_first = [(place[2] ^ j) * row_tokens + (2 * place[0] + place[1]) * span for j in (0, 1)]
    return key_first, query_first


def reach(key_first, keys, query_first, queries):
    key_last, query_last = key_first + keys - 1, query_first + queries - 1
    live = (key_first <= query_last) & (query_first - key_last < WINDOW)
    plain = (key_last < query_first) & (query_last - key_first < WINDOW)
    return live & plain, live & jnp.logical_not(plain)


def row_of(columns, scale):
    ones = jnp.full((8, columns.shape[1]), scale, jnp.float32)
    return lax.dot_general(
        ones,
        columns,
        (((1,), (1,)), ((), ())),
        precision=lax.Precision.HIGHEST,
        preferred_element_type=jnp.float32,
    )


def forward_kernel(
    place, query_ref, own_ref, other_ref, code_ref, segment_ref, out_ref, log_ref, acc, total
):
    tile = pl.program_id(0)
    span = query_ref.shape[1]
    key_first, query_first = tile_facts(place, span, tile)

    @pl.when(tile == 0)
    def _():
        acc[...] = jnp.zeros_like(acc)
        total[...] = jnp.zeros_like(total)

    def step(j, masked):
        keys = jnp.concatenate([own_ref[0, 0, :, :HEAD_DIM], other_ref[0, 0, :, :HEAD_DIM]], axis=0)
        values = jnp.concatenate(
            [own_ref[0, 0, :, HEAD_DIM:], other_ref[0, 0, :, HEAD_DIM:]], axis=0
        )
        allowed = code_ref[0, 0] == segment_ref[j]
        if masked:
            lane = lax.broadcasted_iota(jnp.int32, (1, 2 * span), 1)
            key_pos = key_first + lane + jnp.where(lane < span, place[1], -place[1]) * span
            query_pos = query_first[j] + lax.broadcasted_iota(jnp.int32, (span, 1), 0)
            back = query_pos - key_pos
            allowed = (allowed & (back > 0) & (back < WINDOW)) | (back == 0)
        for h in range(GROUP):
            query = query_ref[j, :, h * HEAD_DIM : (h + 1) * HEAD_DIM]
            scores = matmul_t(query, keys)
            weights = jnp.exp2(log2_scale * jnp.tanh(scores * score_scale))
            weights = jnp.where(allowed, weights, 0.0)
            total[j, h] += jnp.sum(weights, axis=-1, keepdims=True)
            acc[j, h] += matmul(weights.astype(jnp.bfloat16), values)

    for j in (0, 1):
        plain, masked = reach(key_first, 2 * span, query_first[j], span)
        pl.when(plain)(functools.partial(step, j, False))
        pl.when(masked)(functools.partial(step, j, True))

    @pl.when(tile == pl.num_programs(0) - 1)
    def _():
        for j in (0, 1):
            for h in range(GROUP):
                out_ref[j, :, h * HEAD_DIM : (h + 1) * HEAD_DIM] = (
                    acc[j, h] / total[j, h]
                ).astype(jnp.bfloat16)
                column = jnp.broadcast_to(jnp.log2(total[j, h]), (span, 128))
                log_ref[j, :, h * span : (h + 1) * span] = row_of(column, 1.0 / 128)


def backward_kernel(
    place, query_ref, grad_ref, attended_ref, own_ref, other_ref, code_ref, log_ref, segment_ref,
    query_grad_ref, own_grad_ref, other_grad_ref,
    queries, grads, query_acc, key_acc, value_acc, delta,
):
    tile = pl.program_id(0)
    span = query_ref.shape[1]
    key_first, query_first = tile_facts(place, span, tile)

    @pl.when(tile == 0)
    def _():
        query_acc[...] = jnp.zeros_like(query_acc)
        for j in (0, 1):
            for h in range(GROUP):
                rows, columns = pl.ds(h * span, span), slice(h * HEAD_DIM, (h + 1) * HEAD_DIM)
                queries[j, rows, :] = query_ref[j, :, columns]
                grads[j, rows, :] = grad_ref[j, :, columns]
                products = grad_ref[j, :, columns].astype(jnp.float32) * attended_ref[
                    j, :, columns
                ].astype(jnp.float32)
                delta[j, :, h * span : (h + 1) * span] = row_of(products, 1.0)

    def step(j, side, side_first, keys, values, masked):
        allowed = code_ref[0, 0, pl.ds(side * span, span), :] == segment_ref[j, 0:1, :]
        if masked:
            lane = lax.broadcasted_iota(jnp.int32, (1, GROUP * span), 1)
            query_pos = query_first[j] + jnp.where(lane < span, lane, lane - span)
            key_pos = side_first + lax.broadcasted_iota(jnp.int32, (span, 1), 0)
            back = query_pos - key_pos
            allowed = (allowed & (back > 0) & (back < WINDOW)) | (back == 0)
        squashed = jnp.tanh(matmul_t(keys, queries[j]) * score_scale)
        weights = jnp.exp2(log2_scale * squashed - log_ref[j, 0:1, :])
        weights = jnp.where(allowed, weights, 0.0)
        grad_weights = matmul_t(values, grads[j])
        value_acc[side] += matmul(weights.astype(jnp.bfloat16), grads[j])
        grad_scores = weights * (grad_weights - delta[j, 0:1, :]) * (1.0 - squashed * squashed)
        grad_scores = grad_scores.astype(jnp.bfloat16)
        key_acc[side] += matmul(grad_scores, queries[j])
        query_acc[j] += inner_t(grad_scores, keys)

    key_acc[...] = jnp.zeros_like(key_acc)
    value_acc[...] = jnp.zeros_like(value_acc)
    scale = HEAD_DIM ** (-0.5)
    for side, key_ref, grad_out in ((0, own_ref, own_grad_ref), (1, other_ref, other_grad_ref)):
        side_first = key_first + (place[1] if side == 0 else 1 - place[1]) * span

        def on_side(j, masked, side=side, side_first=side_first, key_ref=key_ref):
            keys, values = key_ref[0, 0, :, :HEAD_DIM], key_ref[0, 0, :, HEAD_DIM:]
            step(j, side, side_first, keys, values, masked)

        for j in (0, 1):
            plain, masked = reach(side_first, span, query_first[j], span)
            pl.when(plain)(functools.partial(on_side, j, False))
            pl.when(masked)(functools.partial(on_side, j, True))
        grad_out[0, 0, :, :HEAD_DIM] = (key_acc[side] * scale).astype(jnp.bfloat16)
        grad_out[0, 0, :, HEAD_DIM:] = value_acc[side].astype(jnp.bfloat16)

    @pl.when(tile == pl.num_programs(0) - 1)
    def _():
        for j in (0, 1):
            for h in range(GROUP):
                query_grad_ref[j, :, h * HEAD_DIM : (h + 1) * HEAD_DIM] = (
                    query_acc[j, h * span : (h + 1) * span, :] * scale
                ).astype(jnp.bfloat16)


def whole(*shape):
    return pl.BlockSpec(shape, lambda tile, place: (0,) * len(shape))


def tile_specs(line, span):
    def key_place(tile, place):
        return (tile % line, (tile // line) ^ place[2], 0, 0)

    def code_place(tile, place):
        return ((tile // line) ^ place[2], tile % line, 0, 0)

    return pl.BlockSpec((1, 1, span, 2 * HEAD_DIM), key_place), code_place


def attention_forward(place, queries, own, other, codes, segments):
    line, _, span, width = own.shape
    tile_spec, code_place = tile_specs(line, span)
    return pl.pallas_call(
        forward_kernel,
        grid_spec=pltpu.PrefetchScalarGridSpec(
            num_scalar_prefetch=1,
            grid=(2 * line,),
            in_specs=[
                whole(2, span, width),
                tile_spec,
                tile_spec,
                pl.BlockSpec((1, 1, 1, 2 * span), code_place),
                whole(2, span, 1),
            ],
            out_specs=[whole(2, span, width), whole(2, 8, GROUP * span)],
            scratch_shapes=[
                pltpu.VMEM((2, GROUP, span, HEAD_DIM), jnp.float32),
                pltpu.VMEM((2, GROUP, span, 1), jnp.float32),
            ],
        ),
        out_shape=[
            jax.ShapeDtypeStruct((2, span, width), jnp.bfloat16),
            jax.ShapeDtypeStruct((2, 8, GROUP * span), jnp.float32),
        ],
        compiler_params=pltpu.CompilerParams(vmem_limit_bytes=VMEM_LIMIT),
        cost_estimate=cost(6),
    )(place, queries, own, other, codes, segments)


def attention_backward(place, queries, grads, attended, own, other, codes, logs, segments):
    line, _, span, width = own.shape
    tile_spec, code_place = tile_specs(line, span)
    return pl.pallas_call(
        backward_kernel,
        grid_spec=pltpu.PrefetchScalarGridSpec(
            num_scalar_prefetch=1,
            grid=(2 * line,),
            in_specs=[
                whole(2, span, width),
                whole(2, span, width),
                whole(2, span, width),
                tile_spec,
                tile_spec,
                pl.BlockSpec((1, 1, 2 * span, 1), code_place),
                whole(2, 8, GROUP * span),
                whole(2, 8, GROUP * span),
            ],
            out_specs=[whole(2, span, width), tile_spec, tile_spec],
            scratch_shapes=[
                pltpu.VMEM((2, GROUP * span, HEAD_DIM), jnp.bfloat16),
                pltpu.VMEM((2, GROUP * span, HEAD_DIM), jnp.bfloat16),
                pltpu.VMEM((2, GROUP * span, HEAD_DIM), jnp.float32),
                pltpu.VMEM((2, span, HEAD_DIM), jnp.float32),
                pltpu.VMEM((2, span, HEAD_DIM), jnp.float32),
                pltpu.VMEM((2, 8, GROUP * span), jnp.float32),
            ],
        ),
        out_shape=[
            jax.ShapeDtypeStruct((2, span, width), jnp.bfloat16),
            jax.ShapeDtypeStruct(own.shape, jnp.bfloat16),
            jax.ShapeDtypeStruct(own.shape, jnp.bfloat16),
        ],
        compiler_params=pltpu.CompilerParams(vmem_limit_bytes=VMEM_LIMIT),
        cost_estimate=cost(6),
    )(place, queries, grads, attended, own, other, codes, logs, segments)


def body(
    tokens, pre_attention, post_attention, pre_feedforward, post_feedforward, w_query, key_weight,
    value_weight, w_output, w_gate, w_up, w_down, document_index, token_padding_mask, cotangent,
):
    bf16, f32 = jnp.bfloat16, jnp.float32
    dp, seq = lax.axis_size("dp"), lax.axis_size("seq")
    line, groups = seq // 2, dp // KEY_VALUE_HEADS
    dp_at, seq_at = lax.axis_index("dp"), lax.axis_index("seq")
    line_at, core = seq_at // 2, seq_at % 2
    head = dp_at % KEY_VALUE_HEADS
    half_bit = dp_at % 2
    _, span, model = tokens.shape
    rows = w_query.shape[0]
    ff = w_gate.shape[1]
    ff_rows = w_down.shape[0]
    ff_part = ff // line
    width = GROUP * HEAD_DIM

    order = Order()

    def attention_codes():
        sequence = dp_at // 2

        def by_pair(table):
            both = jnp.stack([pick(table, 0, sequence), pick(table, 0, sequence ^ 1)])
            both = both.reshape(2, 2, line, 2, span)
            both = jnp.where(half_bit == 1, both[:, ::-1], both)
            return jnp.where(core == 1, both[:, :, :, ::-1], both)

        segments = by_pair(document_index)
        codes = jnp.where(by_pair(token_padding_mask) == 1, segments, -1)
        return codes.reshape(2, 2, line, 2 * span), pick(segments[:, :, :, 0], 2, line_at)

    quad = groups == 1
    place = jnp.stack([line_at, core, half_bit, head]).astype(jnp.int32)
    inputs = tokens[0].astype(f32)
    flipped = pack_heads(place, w_query, key_weight, value_weight)
    split = split_columns(place, w_gate, w_up, dp, line)
    if quad:
        flipped, split, place = order(flipped, split, place)
        mixed = [flipped[0]] + [across(flipped[k], k) for k in (1, 2, 3)]
        normed_in = normed(inputs, pre_attention).astype(bf16)
        mixed, normed_in, split = order(order_heads(place, mixed), normed_in, split)
        near_normed = gather_quad_near(normed_in)
        in_weight = lax.all_gather(mixed, "seq", axis=1).reshape(model, 2 * width)
    else:
        normed_in = normed(inputs, pre_attention).astype(bf16)
        near_normed = gather_quad_near(normed_in)
        blocks = lax.all_gather(order_heads(place, flipped), ("dp", "seq"), axis=1, tiled=True)
        in_weight = pick(blocks, 0, head)

    per_device = line * rows
    split = exchange_line_parts(split)

    def ordered_split(split):
        (whole,) = deposit(
            place,
            [empty((2, line, rows, ff_part), bf16)],
            split,
            [
                (k, lambda at, w=w: (w,), 0, lambda at, w=w, k=k: (w, (at[LINE_AT] + line - k) % line))
                for k in range(line)
                for w in (0, 1)
            ],
        )
        return whole.reshape(2 * per_device, ff_part)

    def near_blocks(own):
        return gather_quad_near(own) if quad else (lax.all_gather(own, "dp", axis=0),)

    def far_blocks(near):
        return (gather_quad_far(*near),) if quad else ()

    def swap_all(blocks):
        return [swap_core(block) for block in blocks]

    down_weight = empty((dp, 2, ff_rows, model), bf16)
    gate_weight = empty((dp, line, 2, rows, ff_part), bf16)
    up_weight = empty((dp, line, 2, rows, ff_part), bf16)

    def sides(numbers, mine, swapped):
        for k, *blocks in zip(numbers, mine, swapped):
            for other, block in enumerate(blocks):
                yield k, other, block

    def at_dp(at, k):
        return at[HEAD_AT] ^ k if quad else pl.ds(0, dp)

    def fill_down(weight, numbers, mine, swapped):
        sources, moves = [], []
        for k, other, block in sides(numbers, mine, swapped):
            target = lambda at, k=k, other=other: (at_dp(at, k), at[CORE_AT] ^ other)
            moves.append((len(sources), None, 0, target))
            sources.append(block)
        return deposit(place, [weight], sources, moves)[0] if sources else weight

    def fill_in(gate, up, numbers, mine, swapped):
        sources, moves = [], []
        for k, other, block in sides(numbers, mine, swapped):
            for which in (0, 1):
                source = lambda at, which=which: (slice(None),) * (not quad) + (which,)
                target = lambda at, k=k, other=other: (
                    at_dp(at, k), slice(None), at[CORE_AT] ^ other
                )
                moves.append((len(sources), source, which, target))
            lead = () if quad else (dp,)
            sources.append(block.reshape(lead + (2, line, rows, ff_part)))
        return deposit(place, [gate, up], sources, moves) if sources else (gate, up)

    def project(pair_rows):
        projected = matmul(pair_rows, in_weight).astype(bf16).reshape(2, span, 2 * width)
        return projected[..., :width], projected[..., width:]

    codes, own_segments = attention_codes()
    row_codes = codes[:, :, :, None, :]
    column_segments = own_segments[..., None]
    first_rows = jnp.concatenate([normed_in, near_normed[0]], axis=0)
    halfway = span // 2
    far_normed = near_normed[1][:halfway], near_normed[0][halfway:]
    near_two, far_normed, first_rows, in_weight, split, row_codes, column_segments = order(
        near_normed[1], far_normed, first_rows, in_weight, split, row_codes, column_segments
    )
    far_normed = across(far_normed[0], 1), across(far_normed[1], 2)
    first_queries, first_keys = project(first_rows)
    first_queries, first_keys, first_rows = order(first_queries, first_keys, first_rows)
    first_own = gather_line(first_keys)
    gate_up = ordered_split(split)
    far_normed, gate_up = order(far_normed, gate_up)
    second_rows = jnp.concatenate([near_two, *far_normed], axis=0)
    second_queries, second_keys = project(second_rows)
    second_queries, second_keys, second_rows, gate_up = order(
        second_queries, second_keys, second_rows, gate_up
    )
    second_own = gather_line(second_keys)
    normed_rows = [first_rows, second_rows]
    near_in = near_blocks(gate_up)
    swapped = swap_all([gate_up] if quad else [])
    swapped, first_own = order(swapped, first_own)
    first_other = order(swap_core(first_own))
    attended, log_total = [None, None], [None, None]
    attended[0], log_total[0] = attention_forward(
        place, first_queries, first_own, first_other, row_codes[0], column_segments[0]
    )
    if quad:
        gate_weight, up_weight = fill_in(gate_weight, up_weight, (0,), [gate_up], swapped)
    attended[0], log_total[0], gate_weight, up_weight, near_in = order(
        attended[0], log_total[0], gate_weight, up_weight, near_in
    )
    far_in = far_blocks(near_in)
    swapped = swap_all(near_in)
    second_own, swapped, far_in = order(second_own, swapped, far_in)
    second_other = swap_core(second_own)
    if quad:
        out_weight = lax.all_gather(after(w_output, second_own), "seq", axis=0, tiled=True)
    else:
        out_weight = lax.dynamic_slice_in_dim(
            lax.all_gather(w_output, ("dp", "seq"), axis=0, tiled=True), head * width, width
        )
    numbers = (1, 2, 3) if quad else (0,)
    near_swapped = swapped
    second_other = order(second_other)
    swapped = swap_all(far_in)
    attended[1], log_total[1] = attention_forward(
        place, second_queries, second_own, second_other, row_codes[1], column_segments[1]
    )
    attended, log_total, out_weight, swapped = order(attended, log_total, out_weight, swapped)
    in_blocks, swapped = list(near_in) + list(far_in), near_swapped + swapped
    queries = [first_queries, second_queries]
    own_keys, other_keys = [first_own, second_own], [first_other, second_other]

    def activation(gate_in, up_in):
        return jax.nn.gelu(gate_in, approximate=True) * up_in

    step = span // 2
    chunks = [slice(0, step), slice(step, 2 * step)]
    grad_output = cotangent[0].astype(f32)

    def into_feedforward(part, kept, near, far):
        attn_out = scatter_quad_end(kept, near, far)
        residual = inputs[part] + normed(attn_out, post_attention)
        return attn_out, residual, normed(residual, pre_feedforward).astype(bf16)

    sent_a = order(quad_terms([attended], out_weight, chunks[0], False, True))
    near_a = scatter_quad_near(sent_a)
    kept_a = quad_terms([attended], out_weight, chunks[0], False, False)
    near_a, kept_a = order(near_a, kept_a)
    far_a = scatter_quad_far(kept_a, near_a)
    sent_b = quad_terms([attended], out_weight, chunks[1], False, True)
    far_a, sent_b = order(far_a, sent_b)
    near_b = scatter_quad_near(sent_b)
    attn_out_a, residual_a, mid_a = order(into_feedforward(chunks[0], kept_a, near_a, far_a))
    mid_rows_a = gather_line(mid_a).reshape(line * step, model)
    kept_b = quad_terms([attended], out_weight, chunks[1], False, False)
    near_b, kept_b = order(near_b, kept_b)
    far_b = order(scatter_quad_far(kept_b, near_b))
    attn_out_b, residual_b, mid_b = order(into_feedforward(chunks[1], kept_b, near_b, far_b))
    mid_rows_b = gather_line(mid_b).reshape(line * step, model)
    own_down = after(w_down, far_b[0])
    near_down = near_blocks(own_down)
    gate_weight, up_weight = fill_in(gate_weight, up_weight, numbers, in_blocks, swapped)
    mid_rows_a, gate_weight, up_weight = order(mid_rows_a, gate_weight, up_weight)
    gate_weight = gate_weight.reshape(model, ff_part)
    up_weight = up_weight.reshape(model, ff_part)
    gate_a = matmul(mid_rows_a, gate_weight)
    gate_a, mid_rows_a, near_down = order(gate_a, mid_rows_a, near_down)
    far_down = far_blocks(near_down)
    down_blocks = ([own_down] if quad else []) + list(near_down)
    swapped = swap_all(down_blocks)
    up_a = matmul(mid_rows_a, up_weight)
    hidden_a, far_down, swapped = order(activation(gate_a, up_a).astype(bf16), far_down, swapped)
    down_weight = fill_down(down_weight, range(3), down_blocks, swapped)
    swapped = swap_all(far_down)
    down_weight, swapped = order(down_weight, swapped)
    down_weight = fill_down(down_weight, (3,), far_down, swapped)
    down_weight = down_weight.reshape(ff_part, model)

    def feedforward_end(hidden):
        return matmul(hidden, down_weight).astype(bf16).reshape(line, step, model)

    def output_of(part, residual, down_out):
        down_out = down_out.astype(f32)
        normed_down, down_back = jax.vjp(normed, down_out, post_feedforward)
        grad_down, gain_part = down_back(grad_output[part])
        return residual + normed_down, grad_down.astype(bf16), gain_part

    def feedforward_back(down_rows, gate_value, up_value):
        grad_hidden = matmul_t(down_rows, down_weight)
        _, act_back = jax.vjp(activation, gate_value, up_value)
        grad_gate, grad_up = act_back(grad_hidden)
        grad_gate, grad_up = grad_gate.astype(bf16), grad_up.astype(bf16)
        mid_part = matmul_t(grad_gate, gate_weight) + matmul_t(grad_up, up_weight)
        return grad_gate, grad_up, mid_part.astype(bf16).reshape(line, step, model)

    def attention_grad(part, residual, attn_out, grad_mid):
        _, mid_back = jax.vjp(normed, residual, pre_feedforward)
        grad_residual, grad_pre = mid_back(grad_mid.astype(f32))
        grad_residual = grad_output[part] + grad_residual
        _, attn_back = jax.vjp(normed, attn_out, post_attention)
        grad_attn, grad_post = attn_back(grad_residual)
        return grad_residual, grad_attn.astype(bf16), grad_pre, grad_post

    down_a = scatter_line(order(feedforward_end(hidden_a)))
    mid_rows_b = order(mid_rows_b)
    gate_b, up_b = matmul(mid_rows_b, gate_weight), matmul(mid_rows_b, up_weight)
    hidden_b = activation(gate_b, up_b).astype(bf16)
    down_b = order(feedforward_end(hidden_b))
    down_b = scatter_line(down_b)
    down_a = order(down_a)
    result_a, grad_down_a, post_ff_a = order(output_of(chunks[0], residual_a, down_a))
    down_rows_a = gather_line(grad_down_a).reshape(line * step, model)
    column_codes = [codes[pair][..., None] for pair in (0, 1)]
    lane_segments = jnp.broadcast_to(
        own_segments[:, :, None, None, :], (2, 2, 8, GROUP, span)
    ).reshape(2, 2, 8, GROUP * span)
    lane_segments = [lane_segments[0], lane_segments[1]]
    down_b, column_codes, lane_segments = order(down_b, column_codes, lane_segments)
    result_b, grad_down_b, post_ff_b = order(output_of(chunks[1], residual_b, down_b))
    down_rows_b = gather_line(grad_down_b).reshape(line * step, model)
    down_rows_a = order(down_rows_a)
    grad_gate_a, grad_up_a, mid_part = order(feedforward_back(down_rows_a, gate_a, up_a))
    grad_mid_a = scatter_line(mid_part)
    down_rows_b = order(down_rows_b)
    grad_gate_b, grad_up_b, mid_part = order(feedforward_back(down_rows_b, gate_b, up_b))
    grad_mid_b = scatter_line(mid_part)
    result = jnp.concatenate([result_a, result_b], axis=0)

    def halves(lefts, rights, inner):
        if inner % 8 == 0:
            return weight_halves(place, lefts, rights, inner)
        term = sum(inner_t(left, right) for left, right in zip(lefts, rights))
        term = term.astype(bf16).reshape(-1, 2, inner, rights[0].shape[1])
        return pick(term, 1, core), pick(term, 1, 1 - core)

    def from_cores(own, moved, inner, plan, *shapes):
        own, moved = own.reshape(dp, inner, -1), moved.reshape(dp, inner, -1)
        if not quad:
            return own + moved
        shapes = [tuple(shape) + (own.shape[-1],) for shape in shapes]
        return combine_quad(place, own, moved, shapes, plan)

    def quad_plan(inner):
        low, high = slice(0, inner // 2), slice(inner // 2, inner)
        plan = [
            [(2, None, slice(0, inner))],
            [(0, 0, low), (4, None, high)],
            [(1, 0, high), (3, None, low)],
            [(0, 1, low), (1, 1, high)],
        ]
        half = inner // 2
        return plan, (2, half), (2, half), (inner,), (half,), (half,)

    def combine(own, moved, inner):
        parts = from_cores(own, moved, inner, *quad_plan(inner))
        return (parts[:2], parts[2:]) if quad else (parts, ())

    def near_sums(sent):
        return scatter_quad_near(sent) if quad else ()

    def far_terms(kept, near):
        return (add_second(kept[1], near[0]), add_second(kept[2], near[1])) if quad else ()

    def far_sums(terms):
        return (across(terms[0], 2), across(terms[1], 1)) if quad else ()

    def line_parts(*terms):
        if quad:
            return to_line(place, [(kept[0], near, far) for _, kept, near, far in terms], line)
        totals = [
            lax.psum_scatter(sent, "dp", scatter_dimension=0).reshape(line, rows, ff_part)
            for sent, _, _, _ in terms
        ]
        totals = jnp.stack(totals, axis=1)
        return [pick(totals, 0, (line_at + k) % line) for k in range(line)]

    mid_rows, hiddens, down_rows = (mid_rows_a, mid_rows_b), (hidden_a, hidden_b), (
        down_rows_a, down_rows_b
    )
    grad_gates, grad_ups = (grad_gate_a, grad_gate_b), (grad_up_a, grad_up_b)
    gate_own, gate_other = halves(mid_rows, grad_gates, rows)
    grad_mid_a, gate_own, gate_other = order(grad_mid_a, gate_own, gate_other)
    gate_other = swap_core(gate_other)
    grad_residual_a, grad_attn, pre_ff_a, post_attn_a = attention_grad(
        chunks[0], residual_a, attn_out_a, grad_mid_a
    )
    grad_residual_a, grad_attn, pre_ff_a, post_attn_a, gate_other = order(
        grad_residual_a, grad_attn, pre_ff_a, post_attn_a, gate_other
    )
    near_a = gather_quad_near(grad_attn)
    gate_sent, gate_kept, near_a, mid_rows, grad_ups = order(
        *combine(gate_own, gate_other, per_device), near_a, mid_rows, grad_ups
    )
    gate_near = near_sums(gate_sent)
    up_own, up_other = halves(mid_rows, grad_ups, rows)
    up_own, up_other, gate_near, grad_mid_b = order(up_own, up_other, gate_near, grad_mid_b)
    up_other = swap_core(up_other)
    gate_far = far_terms(gate_kept, gate_near)
    attn_grads, gate_far, up_other, up_own = order(
        attention_grad(chunks[1], residual_b, attn_out_b, grad_mid_b), gate_far, up_other, up_own
    )
    quad_a = [grad_attn, *near_a]
    grad_residual_b, grad_attn, pre_ff_b, post_attn_b = attn_grads
    near_b = gather_quad_near(grad_attn)
    gate_far = far_sums(gate_far)
    up_sent, up_kept = combine(up_own, up_other, per_device)
    near_b, up_sent, up_kept, near_a = order(near_b, up_sent, up_kept, near_a)
    far_b = gather_quad_far_parts(*near_b)
    far_a = gather_quad_far_parts(*near_a)
    grad_residual = jnp.concatenate([grad_residual_a, grad_residual_b], axis=0)

    def attention_rows(blocks_a, blocks_b):
        return jnp.concatenate(
            [block for pair in zip(blocks_a, blocks_b) for block in pair], axis=0
        )

    def attended_grad(attn_rows):
        return matmul_t(attn_rows, out_weight).astype(bf16).reshape(2, span, width)

    def attend_back(pair, grad_attended):
        return attention_backward(
            place, queries[pair], grad_attended, attended[pair], own_keys[pair], other_keys[pair],
            column_codes[pair], log_total[pair], lane_segments[pair],
        )

    def gains_over_dp(terms):
        terms = jnp.stack(terms, axis=1)
        if not quad:
            return lax.psum_scatter(terms, ("dp", "seq"), scatter_dimension=0, tiled=True)
        terms = terms.reshape(dp, line, 2, -1)
        return [pick(terms, 0, head)] + [across(pick(terms, 0, head ^ k), k) for k in (1, 2, 3)]

    def gains_over_seq(terms):
        if not quad:
            return terms
        terms = sum(terms)
        terms = pick(terms, 1, core) + swap_core(pick(terms, 1, 1 - core))
        return jnp.sum(exchange_line(terms, line_at), axis=0).reshape(rows, -1)

    first_attn = attention_rows(quad_a[:2], [grad_attn, near_b[0]])
    grad_attended, gate_far, far_a = order(attended_grad(first_attn), gate_far, far_a)
    gate_line = order(line_parts((gate_sent, gate_kept, gate_near, gate_far)))
    gate_line = exchange_line_parts(gate_line)
    first_grads, own_grad, other_grad, far_b, gate_line, up_sent = order(
        *attend_back(0, grad_attended), far_b, gate_line, up_sent
    )
    up_near = near_sums(up_sent)
    swapped = swap_core(other_grad)
    second_attn = attention_rows(
        [quad_a[2], jnp.concatenate(far_a, axis=0)], [near_b[1], jnp.concatenate(far_b, axis=0)]
    )
    grad_attended = attended_grad(second_attn)
    swapped, grad_attended = order(swapped, grad_attended)
    first_key_grads = order(own_grad + swapped)
    first_key_grads = scatter_line(first_key_grads)
    second_grads, own_grad, other_grad, up_near = order(*attend_back(1, grad_attended), up_near)
    swapped = swap_core(other_grad)
    up_far = far_terms(up_kept, up_near)
    swapped, up_far = order(swapped, up_far)
    second_key_grads, first_key_grads, hiddens, down_rows = order(
        own_grad + swapped, first_key_grads, hiddens, down_rows
    )
    second_key_grads = scatter_line(second_key_grads)

    up_far = far_sums(up_far)
    down_own, down_other = halves(hiddens, down_rows, ff_rows)
    output_term = inner_t(attended[0].reshape(2 * span, width), first_attn)
    output_term += inner_t(attended[1].reshape(2 * span, width), second_attn)
    output_term = output_term.astype(bf16)
    up_line = line_parts((up_sent, up_kept, up_near, up_far))
    second_key_grads, down_own, down_other, output_term, up_line = order(
        second_key_grads, down_own, down_other, output_term, up_line
    )

    grads = [(first_grads, second_grads), (first_key_grads, second_key_grads)]
    sent, grads = order(quad_terms(grads, in_weight, slice(0, span), True, True), grads)
    near = scatter_quad_near(sent)
    kept = quad_terms(grads, in_weight, slice(0, span), True, False)
    if quad:
        output_shard = lax.psum_scatter(output_term, "seq", scatter_dimension=0, tiled=True)
    else:
        spread = jnp.zeros((KEY_VALUE_HEADS, width, model), bf16).at[head].set(output_term)
        output_shard = lax.psum_scatter(
            spread.reshape(KEY_VALUE_HEADS * width, model),
            ("dp", "seq"),
            scatter_dimension=0,
            tiled=True,
        )
    up_line = exchange_line_parts(up_line)
    down_other = swap_core(down_other)
    if quad:
        flat = [[x.reshape(2 * span, width) for x in pair] for pair in grads]
        in_term = input_terms(normed_rows, flat, dp, seq)
        down_sent, down_kept = combine(down_own, down_other, ff_rows)
        near, kept, in_term, down_sent, down_kept, up_line = order(
            near, kept, in_term, down_sent, down_kept, up_line
        )
        far = scatter_quad_far(kept, near)
        in_part = lax.psum_scatter(
            in_term.reshape(model, 2 * width), "seq", scatter_dimension=0, tiled=True
        )
        far, down_sent = order(far, down_sent)
        down_near = scatter_quad_near(down_sent)
    else:
        in_term = sum(
            inner_t(left, jnp.concatenate(right, axis=2).reshape(2 * span, 2 * width))
            for left, right in zip(normed_rows, zip(*grads))
        )
        near, in_term = order(near, in_term.astype(bf16))
        far = order(scatter_quad_far(kept, near))
        down_mine, _ = combine(down_own, down_other, ff_rows)
        down_shard = lax.psum_scatter(down_mine, "dp", scatter_dimension=0).astype(f32)
    grad_in = scatter_quad_end(kept, near, far)
    _, in_back = jax.vjp(normed, inputs, pre_attention)
    grad_inputs, grad_pre_attn = in_back(grad_in)
    grad_pre_attn, grad_inputs = order(grad_pre_attn, grad_inputs)
    gains = gains_over_dp(
        [grad_pre_attn, post_attn_a + post_attn_b, pre_ff_a + pre_ff_b, post_ff_a + post_ff_b]
    )
    tokens_grad = grad_residual + grad_inputs
    if quad:
        gains, down_near = order(gains, down_near)
        down_far = scatter_quad_far(down_kept, down_near)
        in_part = order(in_part)
        part_shard = exchange_quad(in_part.reshape(dp, rows, 2 * width), head)
        part_shard, down_far = order(part_shard, down_far)
        down_shard = scatter_quad_end(down_kept, down_near, down_far)
    gains = gains_over_seq(gains)
    gate_shard, up_shard = (join_columns(place, x, 0, dp) for x in (gate_line, up_line))
    if not quad:
        spread = jnp.zeros((KEY_VALUE_HEADS, model, 2 * width), bf16).at[head].set(in_term)
        part_shard = lax.psum_scatter(spread, ("dp", "seq"), scatter_dimension=1, tiled=True)
    part_shard = part_shard.astype(f32).transpose(1, 0, 2)
    query_shard = part_shard[..., :width].reshape(rows, KEY_VALUE_HEADS * width)
    key_shard = part_shard[..., width : width + HEAD_DIM].reshape(rows, KEY_VALUE_HEADS * HEAD_DIM)
    value_shard = part_shard[..., width + HEAD_DIM :].reshape(rows, KEY_VALUE_HEADS * HEAD_DIM)
    return (
        result[None],
        tokens_grad[None],
        query_shard,
        key_shard,
        value_shard,
        output_shard.astype(f32),
        gate_shard,
        up_shard,
        down_shard,
        gains[:, 0],
        gains[:, 1],
        gains[:, 2],
        gains[:, 3],
    )


def solution(mesh):
    tokens, weights, whole_copy = P("dp", "seq", None), P(("dp", "seq"), None), P()
    gains = P(("dp", "seq"))
    return jax.shard_map(
        body,
        mesh=mesh,
        in_specs=(tokens,) + (whole_copy,) * 4 + (weights,) * 7 + (whole_copy,) * 2 + (tokens,),
        out_specs=(tokens,) * 2 + (weights,) * 7 + (gains,) * 4,
        check_vma=False,
    )
```

```python
import functools
import math

import jax
import jax.numpy as jnp
from jax import lax
from jax.experimental import pallas as pl
from jax.experimental.pallas import tpu as pltpu
from jax.sharding import PartitionSpec as P

KEY_VALUE_HEADS = 4
HEAD_DIM = 256
GROUP = 2
WINDOW = 4096

epsilon = 1e-06
softcap = 50.0
score_scale = HEAD_DIM ** (-0.5) / softcap
log2_scale = softcap * 1.4426950408889634
VMEM_LIMIT = 56 * 1024 * 1024
ANYWHERE = pl.BlockSpec(memory_space=pl.ANY)


def normed(values, gain_vec):
    inv_rms = lax.rsqrt(jnp.mean(values * values, axis=-1, keepdims=True) + epsilon)
    return values * inv_rms * gain_vec


def matmul(a, b):
    return jnp.dot(a, b, preferred_element_type=jnp.float32)


def matmul_t(a, b):
    return lax.dot_general(a, b, (((1,), (1,)), ((), ())), preferred_element_type=jnp.float32)


def inner_t(a, b):
    return lax.dot_general(a, b, (((0,), (0,)), ((), ())), preferred_element_type=jnp.float32)


def across(x, bits):
    return lax.ppermute(x, "dp", [(i, i ^ bits) for i in range(lax.axis_size("dp"))])


def swap_core(x):
    return lax.ppermute(x, "seq", [(i, i ^ 1) for i in range(lax.axis_size("seq"))])


def line_groups():
    count = lax.axis_size("seq")
    return [list(range(core, count, 2)) for core in (0, 1)]


def gather_line(x):
    return lax.all_gather(x, "seq", axis=0, axis_index_groups=line_groups())


def line_route(line, distance):
    return [
        (2 * i + core, 2 * ((i + distance) % line) + core) for i in range(line) for core in (0, 1)
    ]


def exchange_line_parts(parts):
    line = len(parts)
    return [parts[0]] + [lax.ppermute(parts[k], "seq", line_route(line, k)) for k in range(1, line)]


def exchange_line(x, place):
    line = x.shape[0]
    parts = exchange_line_parts([pick(x, 0, (place + k) % line) for k in range(line)])
    for k in range(1, line):
        x = put(x, parts[k], (place + line - k) % line)
    return x


def scatter_line(x):
    return lax.psum_scatter(x, "seq", scatter_dimension=0, axis_index_groups=line_groups())


def scatter_line_steps(x, place):
    line = x.shape[0]
    right = left = None
    for step in range(1, line):
        going = pick(x, 0, jnp.clip(line - step + place, 0, line - 1))
        coming = pick(x, 0, jnp.clip(step - line + place, 0, line - 1))
        right = going if right is None else going + right
        left = coming if left is None else coming + left
        right_route = [(2 * i + c, 2 * i + 2 + c) for i in range(step) for c in (0, 1)]
        left_route = [
            (2 * (line - 1 - i) + c, 2 * (line - 2 - i) + c) for i in range(step) for c in (0, 1)
        ]
        right = lax.ppermute(right, "seq", right_route)
        left = lax.ppermute(left, "seq", left_route)
    f32 = jnp.float32
    return pick(x, 0, place).astype(f32) + right.astype(f32) + left.astype(f32)


def gather_quad_near(x):
    return across(x, 1), across(x, 2)


def gather_quad_far_parts(one, two):
    half = one.shape[0] // 2
    return across(two[:half], 1), across(one[half:], 2)


def gather_quad_far(one, two):
    return jnp.concatenate(gather_quad_far_parts(one, two), axis=0)


def gather_quad(x):
    one, two = gather_quad_near(x)
    return [x, one, two, gather_quad_far(one, two)]


def scatter_quad_near(sent):
    return across(sent[0], 1), across(sent[1], 2)


def scatter_quad_far(kept, near):
    return across(kept[1] + near[0][1], 2), across(kept[2] + near[1][1], 1)


def scatter_quad_end(kept, near, far):
    half = kept[0].shape[0] // 2
    f32 = jnp.float32
    low = kept[0][:half].astype(f32) + near[0][0].astype(f32) + far[0].astype(f32)
    high = kept[0][half:].astype(f32) + near[1][0].astype(f32) + far[1].astype(f32)
    return jnp.concatenate([low, high], axis=0)


def flip_order(x, bits):
    pairs = x.reshape((2, 2) + x.shape[1:])
    pairs = jnp.where(bits % 2 == 1, pairs[:, ::-1], pairs)
    pairs = jnp.where(bits // 2 == 1, pairs[::-1], pairs)
    return pairs.reshape(x.shape)


def exchange_quad(x, place):
    parts = flip_order(x, place)
    return exchange_quad_end([parts[0]] + [across(parts[k], k) for k in (1, 2, 3)], place)


def exchange_quad_end(parts, place):
    return flip_order(jnp.stack(parts), place)


def pick(x, axis, index):
    return lax.dynamic_index_in_dim(x, index, axis, keepdims=False)


def put(x, part, *index):
    for _ in index:
        part = part[None]
    return lax.dynamic_update_slice(x, part, index + (0,) * (x.ndim - len(index)))


def after(x, *others):
    def kernel(x_ref, *rest):
        rest[-1][...] = x_ref[...]

    return pl.pallas_call(
        kernel,
        in_specs=[pl.BlockSpec(memory_space=pltpu.VMEM)] + [ANYWHERE] * len(others),
        out_specs=pl.BlockSpec(memory_space=pltpu.VMEM),
        out_shape=jax.ShapeDtypeStruct(x.shape, x.dtype),
    )(x, *others)


def empty(shape, dtype):
    return pl.pallas_call(
        lambda out_ref: None, out_specs=ANYWHERE, out_shape=jax.ShapeDtypeStruct(shape, dtype)
    )()


class Order:
    def __init__(self):
        self.token = jnp.zeros((8, 128), jnp.float32)

    def __call__(self, *trees):
        leaves, tree = jax.tree.flatten(trees)
        held = pl.pallas_call(
            lambda *refs: None,
            in_specs=[ANYWHERE] * (1 + len(leaves)),
            out_specs=[ANYWHERE] * (1 + len(leaves)),
            out_shape=[jax.ShapeDtypeStruct(x.shape, x.dtype) for x in [self.token, *leaves]],
            input_output_aliases={i: i for i in range(1 + len(leaves))},
        )(self.token, *leaves)
        self.token = held[0]
        out = jax.tree.unflatten(tree, held[1:])
        return out[0] if len(trees) == 1 else out


FREE = pl.CostEstimate(flops=0, bytes_accessed=0, transcendentals=0)


def cost(us):
    return pl.CostEstimate(flops=0, bytes_accessed=int(us * 3.5e6), transcendentals=0)


def deposit(place, targets, sources, moves):
    count = len(targets)

    def kernel(place_ref, *refs):
        source_refs = refs[count : count + len(sources)]
        target_refs, sems = refs[count + len(sources) : -1], refs[-1]
        copies = []
        for n, (source, source_at, target, target_at) in enumerate(moves):
            source_ref, target_ref = source_refs[source], target_refs[target]
            if source_at is not None:
                source_ref = source_ref.at[source_at(place_ref)]
            copies.append(
                pltpu.make_async_copy(source_ref, target_ref.at[target_at(place_ref)], sems.at[n])
            )
            copies[-1].start()
        for copy in copies:
            copy.wait()

    return pl.pallas_call(
        kernel,
        in_specs=[pl.BlockSpec(memory_space=pltpu.SMEM)]
        + [ANYWHERE] * count
        + [pl.BlockSpec(memory_space=pltpu.VMEM)] * len(sources),
        out_specs=[ANYWHERE] * count,
        out_shape=[jax.ShapeDtypeStruct(x.shape, x.dtype) for x in targets],
        scratch_shapes=[pltpu.SemaphoreType.DMA((len(moves),))],
        input_output_aliases={1 + i: i for i in range(count)},
        compiler_params=pltpu.CompilerParams(vmem_limit_bytes=VMEM_LIMIT),
        cost_estimate=FREE,
    )(place, *targets, *sources)


LINE_AT, CORE_AT, HALF_AT, HEAD_AT = range(4)


def pack_heads(place, query, key, value):
    rows, width = query.shape[0], GROUP * HEAD_DIM

    def kernel(place_ref, query_ref, key_ref, value_ref, *out_refs):
        for k, out_ref in enumerate(out_refs):
            head = place_ref[HEAD_AT] ^ k
            first = pl.multiple_of(head * width, width)
            out_ref[:, :width] = query_ref[:, pl.ds(first, width)]
            first = pl.multiple_of(head * HEAD_DIM, HEAD_DIM)
            out_ref[:, width : width + HEAD_DIM] = key_ref[:, pl.ds(first, HEAD_DIM)]
            out_ref[:, width + HEAD_DIM :] = value_ref[:, pl.ds(first, HEAD_DIM)]

    return pl.pallas_call(
        kernel,
        in_specs=[pl.BlockSpec(memory_space=pltpu.SMEM)]
        + [pl.BlockSpec(memory_space=pltpu.VMEM)] * 3,
        out_shape=[jax.ShapeDtypeStruct((rows, 2 * width), query.dtype)] * KEY_VALUE_HEADS,
        compiler_params=pltpu.CompilerParams(vmem_limit_bytes=VMEM_LIMIT),
        cost_estimate=FREE,
    )(place, query, key, value)


def order_heads(place, parts):
    def kernel(place_ref, *refs):
        for k in range(KEY_VALUE_HEADS):
            refs[-1][place_ref[HEAD_AT] ^ k] = refs[k][...]

    return pl.pallas_call(
        kernel,
        in_specs=[pl.BlockSpec(memory_space=pltpu.SMEM)]
        + [pl.BlockSpec(memory_space=pltpu.VMEM)] * KEY_VALUE_HEADS,
        out_shape=jax.ShapeDtypeStruct((KEY_VALUE_HEADS,) + parts[0].shape, parts[0].dtype),
        compiler_params=pltpu.CompilerParams(vmem_limit_bytes=VMEM_LIMIT),
        cost_estimate=FREE,
    )(place, *parts)


def weight_halves(place, lefts, rights, inner):
    rows, model = lefts[0].shape
    columns = rights[0].shape[1]
    block, strip = math.gcd(model, 1152), math.gcd(columns, 256)
    groups = block // (2 * inner)

    def kernel(place_ref, left_a, left_b, right_a, right_b, own_ref, other_ref, turned):
        turned[:, :rows] = left_a[...].T
        turned[:, rows:] = left_b[...].T
        core_here = place_ref[CORE_AT]

        def body(n, carry):
            at = pl.ds(pl.multiple_of(n * strip, strip), strip)
            term = matmul(turned[:, :rows], right_a[:, at])
            term = (term + matmul(turned[:, rows:], right_b[:, at])).astype(jnp.bfloat16)
            term = term.reshape(groups, 2, inner, strip)
            own_ref[:, :, at] = jnp.where(core_here == 0, term[:, 0], term[:, 1])
            other_ref[:, :, at] = jnp.where(core_here == 0, term[:, 1], term[:, 0])
            return carry

        lax.fori_loop(0, columns // strip, body, 0)

    half = pl.BlockSpec((groups, inner, columns), lambda i: (i, 0, 0))
    shape = jax.ShapeDtypeStruct((model // (2 * inner), inner, columns), jnp.bfloat16)
    left_spec = pl.BlockSpec((rows, block), lambda i: (0, i))
    right_spec = pl.BlockSpec((rows, columns), lambda i: (0, 0))
    return pl.pallas_call(
        kernel,
        grid=(model // block,),
        in_specs=[pl.BlockSpec(memory_space=pltpu.SMEM)] + [left_spec] * 2 + [right_spec] * 2,
        out_specs=[half, half],
        out_shape=[shape, shape],
        scratch_shapes=[pltpu.VMEM((block, 2 * rows), jnp.bfloat16)],
        compiler_params=pltpu.CompilerParams(vmem_limit_bytes=VMEM_LIMIT),
        cost_estimate=FREE,
    )(place, *lefts, *rights)


def quad_terms(lefts, weight, part, turned, sent):
    first, count = part.start, part.stop - part.start
    half = count // 2
    model = weight.shape[0] if turned else weight.shape[1]
    if sent:
        plan = [(1, 0, half, 0, 0), (3, 0, half, 0, 1), (2, half, half, 1, 0), (3, half, half, 1, 1)]
        shapes = [(2, half, model), (2, half, model)]
    else:
        plan = [(0, 0, count, 0, None), (2, 0, half, 1, None), (1, half, half, 2, None)]
        shapes = [(count, model), (half, model), (half, model)]
    widths = [pair[0].shape[2] for pair in lefts]

    def kernel(*refs):
        weight_ref, scratch = refs[2 * len(lefts)], refs[-1]
        out_refs = refs[2 * len(lefts) + 1 : -1]
        row = 0
        for k, start, size, _, _ in plan:
            column = 0
            for n, width in enumerate(widths):
                ref = refs[2 * n + k // 2]
                scratch[row : row + size, column : column + width] = ref[
                    k % 2, first + start : first + start + size, :
                ]
                column += width
            row += size
        product = matmul_t if turned else matmul
        term = product(scratch[...], weight_ref[...]).astype(jnp.bfloat16)
        row = 0
        for _, _, size, out, at in plan:
            if at is None:
                out_refs[out][...] = term[row : row + size]
            else:
                out_refs[out][at] = term[row : row + size]
            row += size

    return pl.pallas_call(
        kernel,
        out_shape=[jax.ShapeDtypeStruct(shape, jnp.bfloat16) for shape in shapes],
        scratch_shapes=[pltpu.VMEM((2 * count, sum(widths)), jnp.bfloat16)],
        compiler_params=pltpu.CompilerParams(vmem_limit_bytes=VMEM_LIMIT),
        cost_estimate=cost(1),
    )(*[x for pair in lefts for x in pair], weight)


def split_columns(place, gate, up, dp, line):
    rows, ff = gate.shape
    rest = ff // (dp * line)

    def kernel(place_ref, gate_ref, up_ref, *out_refs):
        def fill(j, k):
            for which, ref in enumerate((gate_ref, up_ref)):
                for i in range(dp):
                    first = (i * line + j) * rest
                    out_refs[k][which, :, i * rest : (i + 1) * rest] = ref[:, first : first + rest]

        for j in range(line):
            for k in range(line):
                there = lax.rem(place_ref[LINE_AT] + k, line) == j
                pl.when(there)(functools.partial(fill, j, k))

    return pl.pallas_call(
        kernel,
        in_specs=[pl.BlockSpec(memory_space=pltpu.SMEM)]
        + [pl.BlockSpec(memory_space=pltpu.VMEM)] * 2,
        out_shape=[jax.ShapeDtypeStruct((2, rows, dp * rest), gate.dtype)] * line,
        compiler_params=pltpu.CompilerParams(vmem_limit_bytes=VMEM_LIMIT),
        cost_estimate=FREE,
    )(place, gate, up)


def join_columns(place, parts, which, dp):
    line = len(parts)
    _, rows, part = parts[0].shape
    rest = part // dp

    def kernel(place_ref, *refs):
        def fill(j, k):
            for i in range(dp):
                first = (i * line + j) * rest
                refs[line][:, first : first + rest] = refs[k][
                    0, :, i * rest : (i + 1) * rest
                ].astype(jnp.float32)

        for j in range(line):
            for k in range(line):
                there = lax.rem(place_ref[LINE_AT] + line - k, line) == j
                pl.when(there)(functools.partial(fill, j, k))

    return pl.pallas_call(
        kernel,
        grid_spec=pltpu.PrefetchScalarGridSpec(
            num_scalar_prefetch=1,
            grid=(1,),
            in_specs=[pl.BlockSpec((1, rows, part), lambda i, place: (which, 0, 0))] * line,
            out_specs=pl.BlockSpec((rows, line * part), lambda i, place: (0, 0)),
        ),
        out_shape=jax.ShapeDtypeStruct((rows, line * part), jnp.float32),
        compiler_params=pltpu.CompilerParams(vmem_limit_bytes=VMEM_LIMIT),
        cost_estimate=FREE,
    )(place, *parts)


def add_second(term, pair):
    rows, columns = term.shape

    def kernel(term_ref, pair_ref, out_ref):
        total = term_ref[...].astype(jnp.float32) + pair_ref[0].astype(jnp.float32)
        out_ref[...] = total.astype(jnp.bfloat16)

    return pl.pallas_call(
        kernel,
        grid=(1,),
        in_specs=[
            pl.BlockSpec((rows, columns), lambda i: (0, 0)),
            pl.BlockSpec((1, rows, columns), lambda i: (1, 0, 0)),
        ],
        out_specs=pl.BlockSpec((rows, columns), lambda i: (0, 0)),
        out_shape=jax.ShapeDtypeStruct((rows, columns), jnp.bfloat16),
        compiler_params=pltpu.CompilerParams(vmem_limit_bytes=VMEM_LIMIT),
        cost_estimate=FREE,
    )(term, pair)


def combine_quad(place, own, other, shapes, plan):
    _, inner, columns = own.shape
    spec = pl.BlockSpec((1, inner, columns), lambda k, place: (place[HEAD_AT] ^ k, 0, 0))

    def kernel(place_ref, own_ref, other_ref, *out_refs):
        total = own_ref[0].astype(jnp.float32) + other_ref[0].astype(jnp.float32)
        total = total.astype(jnp.bfloat16)

        def write(k):
            for out, at, taken in plan[k]:
                if at is None:
                    out_refs[out][...] = total[taken]
                else:
                    out_refs[out][at] = total[taken]

        for k in range(4):
            pl.when(pl.program_id(0) == k)(functools.partial(write, k))

    return pl.pallas_call(
        kernel,
        grid_spec=pltpu.PrefetchScalarGridSpec(
            num_scalar_prefetch=1,
            grid=(4,),
            in_specs=[spec, spec],
            out_specs=[
                pl.BlockSpec(shape, lambda k, place, rank=len(shape): (0,) * rank)
                for shape in shapes
            ],
        ),
        out_shape=[jax.ShapeDtypeStruct(shape, jnp.bfloat16) for shape in shapes],
        compiler_params=pltpu.CompilerParams(vmem_limit_bytes=VMEM_LIMIT),
        cost_estimate=FREE,
    )(place, own, other)


def to_line(place, terms, line):
    count, columns = terms[0][0].shape
    rows, half = count // line, count // 2
    alone = pl.BlockSpec((count, columns), lambda i, place: (0, 0))
    first = pl.BlockSpec((1, half, columns), lambda i, place: (0, 0, 0))
    last = pl.BlockSpec((half, columns), lambda i, place: (0, 0))
    part = pl.BlockSpec((len(terms), rows, columns), lambda i, place: (0, 0, 0))

    def kernel(place_ref, *refs):
        def fill(j, k):
            start, high = j * rows % half, j * rows // half
            for which in range(len(terms)):
                kept_ref, *near_refs = refs[5 * which : 5 * which + 3]
                far_ref = refs[5 * which + 3 + high]
                total = kept_ref[j * rows : (j + 1) * rows].astype(jnp.float32)
                total = total + near_refs[high][0, start : start + rows].astype(jnp.float32)
                total = total + far_ref[start : start + rows].astype(jnp.float32)
                refs[5 * len(terms) + k][which] = total.astype(jnp.bfloat16)

        for j in range(line):
            for k in range(line):
                there = lax.rem(place_ref[LINE_AT] + k, line) == j
                pl.when(there)(functools.partial(fill, j, k))

    return pl.pallas_call(
        kernel,
        grid_spec=pltpu.PrefetchScalarGridSpec(
            num_scalar_prefetch=1,
            grid=(1,),
            in_specs=[alone, first, first, last, last] * len(terms),
            out_specs=[part] * line,
        ),
        out_shape=[jax.ShapeDtypeStruct((len(terms), rows, columns), jnp.bfloat16)] * line,
        compiler_params=pltpu.CompilerParams(vmem_limit_bytes=VMEM_LIMIT),
        cost_estimate=FREE,
    )(place, *[x for kept, near, far in terms for x in (kept, *near, *far)])


def input_terms(lefts, rights, dp, seq):
    count, model = lefts[0].shape
    widths = [pair[0].shape[1] for pair in rights]
    rest = model // (dp * seq)
    block, strip = model // 2, math.gcd(*widths, 256)
    halves = dp // 2

    def kernel(left_a, left_b, *refs):
        out_ref, turned = refs[-2:]
        turned[:, :count] = left_a[...].T
        turned[:, count:] = left_b[...].T
        column = 0
        for n, width in enumerate(widths):

            def body(m, carry, right_a=refs[2 * n], right_b=refs[2 * n + 1], column=column):
                at = pl.ds(pl.multiple_of(m * strip, strip), strip)
                to = pl.ds(pl.multiple_of(column + m * strip, strip), strip)
                term = matmul(turned[:, :count], right_a[:, at])
                term = (term + matmul(turned[:, count:], right_b[:, at])).astype(jnp.bfloat16)
                term = term.reshape(halves, seq, rest, strip)
                for i in range(halves):
                    out_ref[:, i, :, to] = term[i]
                return carry

            lax.fori_loop(0, width // strip, body, 0)
            column += width

    left_spec = pl.BlockSpec((count, block), lambda i: (0, i))
    columns = sum(widths)
    return pl.pallas_call(
        kernel,
        grid=(2,),
        in_specs=[left_spec] * 2
        + [pl.BlockSpec((count, width), lambda i: (0, 0)) for width in widths for _ in (0, 1)],
        out_specs=pl.BlockSpec((seq, halves, rest, columns), lambda i: (0, i, 0, 0)),
        out_shape=jax.ShapeDtypeStruct((seq, dp, rest, columns), jnp.bfloat16),
        scratch_shapes=[pltpu.VMEM((block, 2 * count), jnp.bfloat16)],
        compiler_params=pltpu.CompilerParams(vmem_limit_bytes=VMEM_LIMIT),
        cost_estimate=cost(6),
    )(*lefts, *[x for pair in rights for x in pair])


def tile_facts(place, span, tile):
    line = pl.num_programs(0) // 2
    row_tokens = line * 2 * span
    half = tile // line
    key_first = half * row_tokens + (tile % line) * 2 * span
    query_first = [(place[2] ^ j) * row_tokens + (2 * place[0] + place[1]) * span for j in (0, 1)]
    return key_first, query_first


def reach(key_first, keys, query_first, queries):
    key_last, query_last = key_first + keys - 1, query_first + queries - 1
    live = (key_first <= query_last) & (query_first - key_last < WINDOW)
    plain = (key_last < query_first) & (query_last - key_first < WINDOW)
    return live & plain, live & jnp.logical_not(plain)


def row_of(columns, scale):
    ones = jnp.full((8, columns.shape[1]), scale, jnp.float32)
    return lax.dot_general(
        ones,
        columns,
        (((1,), (1,)), ((), ())),
        precision=lax.Precision.HIGHEST,
        preferred_element_type=jnp.float32,
    )


def forward_kernel(
    place, query_ref, own_ref, other_ref, code_ref, segment_ref, out_ref, log_ref, acc, total
):
    tile = pl.program_id(0)
    span = query_ref.shape[1]
    key_first, query_first = tile_facts(place, span, tile)

    @pl.when(tile == 0)
    def _():
        acc[...] = jnp.zeros_like(acc)
        total[...] = jnp.zeros_like(total)

    def step(j, masked):
        keys = jnp.concatenate([own_ref[0, 0, :, :HEAD_DIM], other_ref[0, 0, :, :HEAD_DIM]], axis=0)
        values = jnp.concatenate(
            [own_ref[0, 0, :, HEAD_DIM:], other_ref[0, 0, :, HEAD_DIM:]], axis=0
        )
        allowed = code_ref[0, 0] == segment_ref[j]
        if masked:
            lane = lax.broadcasted_iota(jnp.int32, (1, 2 * span), 1)
            key_pos = key_first + lane + jnp.where(lane < span, place[1], -place[1]) * span
            query_pos = query_first[j] + lax.broadcasted_iota(jnp.int32, (span, 1), 0)
            back = query_pos - key_pos
            allowed = (allowed & (back > 0) & (back < WINDOW)) | (back == 0)
        for h in range(GROUP):
            query = query_ref[j, :, h * HEAD_DIM : (h + 1) * HEAD_DIM]
            scores = matmul_t(query, keys)
            weights = jnp.exp2(log2_scale * jnp.tanh(scores * score_scale))
            weights = jnp.where(allowed, weights, 0.0)
            total[j, h] += jnp.sum(weights, axis=-1, keepdims=True)
            acc[j, h] += matmul(weights.astype(jnp.bfloat16), values)

    for j in (0, 1):
        plain, masked = reach(key_first, 2 * span, query_first[j], span)
        pl.when(plain)(functools.partial(step, j, False))
        pl.when(masked)(functools.partial(step, j, True))

    @pl.when(tile == pl.num_programs(0) - 1)
    def _():
        for j in (0, 1):
            for h in range(GROUP):
                out_ref[j, :, h * HEAD_DIM : (h + 1) * HEAD_DIM] = (
                    acc[j, h] / total[j, h]
                ).astype(jnp.bfloat16)
                column = jnp.broadcast_to(jnp.log2(total[j, h]), (span, 128))
                log_ref[j, :, h * span : (h + 1) * span] = row_of(column, 1.0 / 128)


def backward_kernel(
    place, query_ref, grad_ref, attended_ref, own_ref, other_ref, code_ref, log_ref, segment_ref,
    query_grad_ref, own_grad_ref, other_grad_ref,
    queries, grads, query_acc, key_acc, value_acc, delta,
):
    tile = pl.program_id(0)
    span = query_ref.shape[1]
    key_first, query_first = tile_facts(place, span, tile)

    @pl.when(tile == 0)
    def _():
        query_acc[...] = jnp.zeros_like(query_acc)
        for j in (0, 1):
            for h in range(GROUP):
                rows, columns = pl.ds(h * span, span), slice(h * HEAD_DIM, (h + 1) * HEAD_DIM)
                queries[j, rows, :] = query_ref[j, :, columns]
                grads[j, rows, :] = grad_ref[j, :, columns]
                products = grad_ref[j, :, columns].astype(jnp.float32) * attended_ref[
                    j, :, columns
                ].astype(jnp.float32)
                delta[j, :, h * span : (h + 1) * span] = row_of(products, 1.0)

    def step(j, side, side_first, keys, values, masked):
        allowed = code_ref[0, 0, pl.ds(side * span, span), :] == segment_ref[j, 0:1, :]
        if masked:
            lane = lax.broadcasted_iota(jnp.int32, (1, GROUP * span), 1)
            query_pos = query_first[j] + jnp.where(lane < span, lane, lane - span)
            key_pos = side_first + lax.broadcasted_iota(jnp.int32, (span, 1), 0)
            back = query_pos - key_pos
            allowed = (allowed & (back > 0) & (back < WINDOW)) | (back == 0)
        squashed = jnp.tanh(matmul_t(keys, queries[j]) * score_scale)
        weights = jnp.exp2(log2_scale * squashed - log_ref[j, 0:1, :])
        weights = jnp.where(allowed, weights, 0.0)
        grad_weights = matmul_t(values, grads[j])
        value_acc[side] += matmul(weights.astype(jnp.bfloat16), grads[j])
        grad_scores = weights * (grad_weights - delta[j, 0:1, :]) * (1.0 - squashed * squashed)
        grad_scores = grad_scores.astype(jnp.bfloat16)
        key_acc[side] += matmul(grad_scores, queries[j])
        query_acc[j] += inner_t(grad_scores, keys)

    key_acc[...] = jnp.zeros_like(key_acc)
    value_acc[...] = jnp.zeros_like(value_acc)
    scale = HEAD_DIM ** (-0.5)
    for side, key_ref, grad_out in ((0, own_ref, own_grad_ref), (1, other_ref, other_grad_ref)):
        side_first = key_first + (place[1] if side == 0 else 1 - place[1]) * span

        def on_side(j, masked, side=side, side_first=side_first, key_ref=key_ref):
            keys, values = key_ref[0, 0, :, :HEAD_DIM], key_ref[0, 0, :, HEAD_DIM:]
            step(j, side, side_first, keys, values, masked)

        for j in (0, 1):
            plain, masked = reach(side_first, span, query_first[j], span)
            pl.when(plain)(functools.partial(on_side, j, False))
            pl.when(masked)(functools.partial(on_side, j, True))
        grad_out[0, 0, :, :HEAD_DIM] = (key_acc[side] * scale).astype(jnp.bfloat16)
        grad_out[0, 0, :, HEAD_DIM:] = value_acc[side].astype(jnp.bfloat16)

    @pl.when(tile == pl.num_programs(0) - 1)
    def _():
        for j in (0, 1):
            for h in range(GROUP):
                query_grad_ref[j, :, h * HEAD_DIM : (h + 1) * HEAD_DIM] = (
                    query_acc[j, h * span : (h + 1) * span, :] * scale
                ).astype(jnp.bfloat16)


def whole(*shape):
    return pl.BlockSpec(shape, lambda tile, place: (0,) * len(shape))


def tile_specs(line, span):
    def key_place(tile, place):
        return (tile % line, (tile // line) ^ place[2], 0, 0)

    def code_place(tile, place):
        return ((tile // line) ^ place[2], tile % line, 0, 0)

    return pl.BlockSpec((1, 1, span, 2 * HEAD_DIM), key_place), code_place


def attention_forward(place, queries, own, other, codes, segments):
    line, _, span, width = own.shape
    tile_spec, code_place = tile_specs(line, span)
    return pl.pallas_call(
        forward_kernel,
        grid_spec=pltpu.PrefetchScalarGridSpec(
            num_scalar_prefetch=1,
            grid=(2 * line,),
            in_specs=[
                whole(2, span, width),
                tile_spec,
                tile_spec,
                pl.BlockSpec((1, 1, 1, 2 * span), code_place),
                whole(2, span, 1),
            ],
            out_specs=[whole(2, span, width), whole(2, 8, GROUP * span)],
            scratch_shapes=[
                pltpu.VMEM((2, GROUP, span, HEAD_DIM), jnp.float32),
                pltpu.VMEM((2, GROUP, span, 1), jnp.float32),
            ],
        ),
        out_shape=[
            jax.ShapeDtypeStruct((2, span, width), jnp.bfloat16),
            jax.ShapeDtypeStruct((2, 8, GROUP * span), jnp.float32),
        ],
        compiler_params=pltpu.CompilerParams(vmem_limit_bytes=VMEM_LIMIT),
        cost_estimate=cost(6),
    )(place, queries, own, other, codes, segments)


def attention_backward(place, queries, grads, attended, own, other, codes, logs, segments):
    line, _, span, width = own.shape
    tile_spec, code_place = tile_specs(line, span)
    return pl.pallas_call(
        backward_kernel,
        grid_spec=pltpu.PrefetchScalarGridSpec(
            num_scalar_prefetch=1,
            grid=(2 * line,),
            in_specs=[
                whole(2, span, width),
                whole(2, span, width),
                whole(2, span, width),
                tile_spec,
                tile_spec,
                pl.BlockSpec((1, 1, 2 * span, 1), code_place),
                whole(2, 8, GROUP * span),
                whole(2, 8, GROUP * span),
            ],
            out_specs=[whole(2, span, width), tile_spec, tile_spec],
            scratch_shapes=[
                pltpu.VMEM((2, GROUP * span, HEAD_DIM), jnp.bfloat16),
                pltpu.VMEM((2, GROUP * span, HEAD_DIM), jnp.bfloat16),
                pltpu.VMEM((2, GROUP * span, HEAD_DIM), jnp.float32),
                pltpu.VMEM((2, span, HEAD_DIM), jnp.float32),
                pltpu.VMEM((2, span, HEAD_DIM), jnp.float32),
                pltpu.VMEM((2, 8, GROUP * span), jnp.float32),
            ],
        ),
        out_shape=[
            jax.ShapeDtypeStruct((2, span, width), jnp.bfloat16),
            jax.ShapeDtypeStruct(own.shape, jnp.bfloat16),
            jax.ShapeDtypeStruct(own.shape, jnp.bfloat16),
        ],
        compiler_params=pltpu.CompilerParams(vmem_limit_bytes=VMEM_LIMIT),
        cost_estimate=FREE,
    )(place, queries, grads, attended, own, other, codes, logs, segments)


def body(
    tokens, pre_attention, post_attention, pre_feedforward, post_feedforward, w_query, key_weight,
    value_weight, w_output, w_gate, w_up, w_down, document_index, token_padding_mask, cotangent,
):
    bf16, f32 = jnp.bfloat16, jnp.float32
    dp, seq = lax.axis_size("dp"), lax.axis_size("seq")
    line, groups = seq // 2, dp // KEY_VALUE_HEADS
    dp_at, seq_at = lax.axis_index("dp"), lax.axis_index("seq")
    line_at, core = seq_at // 2, seq_at % 2
    head = dp_at % KEY_VALUE_HEADS
    half_bit = dp_at % 2
    _, span, model = tokens.shape
    rows = w_query.shape[0]
    ff = w_gate.shape[1]
    ff_rows = w_down.shape[0]
    ff_part = ff // line
    width = GROUP * HEAD_DIM

    order = Order()

    def attention_codes():
        sequence = dp_at // 2

        def by_pair(table):
            both = jnp.stack([pick(table, 0, sequence), pick(table, 0, sequence ^ 1)])
            both = both.reshape(2, 2, line, 2, span)
            both = jnp.where(half_bit == 1, both[:, ::-1], both)
            return jnp.where(core == 1, both[:, :, :, ::-1], both)

        segments = by_pair(document_index)
        codes = jnp.where(by_pair(token_padding_mask) == 1, segments, -1)
        return codes.reshape(2, 2, line, 2 * span), pick(segments[:, :, :, 0], 2, line_at)

    quad = groups == 1
    place = jnp.stack([line_at, core, half_bit, head]).astype(jnp.int32)
    inputs = tokens[0].astype(f32)
    flipped = pack_heads(place, w_query, key_weight, value_weight)
    split = split_columns(place, w_gate, w_up, dp, line)
    if quad:
        flipped = order(flipped)
        mixed = [flipped[0]] + [across(flipped[k], k) for k in (1, 2, 3)]
        normed_in = normed(inputs, pre_attention).astype(bf16)
        mixed, normed_in, split, place = order(order_heads(place, mixed), normed_in, split, place)
        near_normed = gather_quad_near(normed_in)
        in_weight = lax.all_gather(mixed, "seq", axis=1).reshape(model, 2 * width)
    else:
        normed_in = normed(inputs, pre_attention).astype(bf16)
        near_normed = gather_quad_near(normed_in)
        blocks = lax.all_gather(order_heads(place, flipped), ("dp", "seq"), axis=1, tiled=True)
        in_weight = pick(blocks, 0, head)

    per_device = line * rows
    split = exchange_line_parts(split)

    def ordered_split(split):
        (whole,) = deposit(
            place,
            [empty((2, line, rows, ff_part), bf16)],
            split,
            [
                (k, lambda at, w=w: (w,), 0, lambda at, w=w, k=k: (w, (at[LINE_AT] + line - k) % line))
                for k in range(line)
                for w in (0, 1)
            ],
        )
        return whole.reshape(2 * per_device, ff_part)

    def near_blocks(own):
        return gather_quad_near(own) if quad else (lax.all_gather(own, "dp", axis=0),)

    def far_blocks(near):
        return (gather_quad_far(*near),) if quad else ()

    def far_halves(near):
        return gather_quad_far_parts(*near) if quad else ()

    def swap_all(blocks):
        return [swap_core(block) for block in blocks]

    down_weight = empty((dp, 2, ff_rows, model), bf16)
    gate_weight = empty((dp, line, 2, rows, ff_part), bf16)
    up_weight = empty((dp, line, 2, rows, ff_part), bf16)

    def sides(numbers, mine, swapped):
        for k, *blocks in zip(numbers, mine, swapped):
            for other, block in enumerate(blocks):
                yield k, other, block

    def at_dp(at, k):
        return at[HEAD_AT] ^ k if quad else pl.ds(0, dp)

    def fill_down(weight, numbers, mine, swapped):
        sources, moves = [], []
        for k, other, block in sides(numbers, mine, swapped):
            target = lambda at, k=k, other=other: (at_dp(at, k), at[CORE_AT] ^ other)
            moves.append((len(sources), None, 0, target))
            sources.append(block)
        return deposit(place, [weight], sources, moves)[0] if sources else weight

    def fill_in(gate, up, numbers, mine, swapped, halves=()):
        sources, moves = [], []
        for which, pair in enumerate(halves):
            for other, block in enumerate(pair):
                target = lambda at, other=other: (at_dp(at, 3), slice(None), at[CORE_AT] ^ other)
                moves.append((len(sources), None, which, target))
                sources.append(block.reshape(line, rows, ff_part))
        for k, other, block in sides(numbers, mine, swapped):
            for which in (0, 1):
                source = lambda at, which=which: (slice(None),) * (not quad) + (which,)
                target = lambda at, k=k, other=other: (
                    at_dp(at, k), slice(None), at[CORE_AT] ^ other
                )
                moves.append((len(sources), source, which, target))
            lead = () if quad else (dp,)
            sources.append(block.reshape(lead + (2, line, rows, ff_part)))
        return deposit(place, [gate, up], sources, moves) if sources else (gate, up)

    def project(pair_rows):
        projected = matmul(pair_rows, in_weight).astype(bf16).reshape(2, span, 2 * width)
        return projected[..., :width], projected[..., width:]

    codes, own_segments = attention_codes()
    row_codes = codes[:, :, :, None, :]
    column_segments = own_segments[..., None]
    first_rows = jnp.concatenate([normed_in, near_normed[0]], axis=0)
    halfway = span // 2
    far_normed = near_normed[1][:halfway], near_normed[0][halfway:]
    near_two, far_normed, first_rows, in_weight, split, row_codes, column_segments = order(
        near_normed[1], far_normed, first_rows, in_weight, split, row_codes, column_segments
    )
    far_normed = across(far_normed[0], 1), across(far_normed[1], 2)
    first_queries, first_keys = project(first_rows)
    first_queries, first_keys, first_rows = order(first_queries, first_keys, first_rows)
    first_own = gather_line(first_keys)
    gate_up = ordered_split(split)
    far_normed, gate_up = order(far_normed, gate_up)
    second_rows = jnp.concatenate([near_two, *far_normed], axis=0)
    second_queries, second_keys = project(second_rows)
    second_queries, second_keys, second_rows, gate_up = order(
        second_queries, second_keys, second_rows, gate_up
    )
    second_own = gather_line(second_keys)
    normed_rows = [first_rows, second_rows]
    near_in = near_blocks(gate_up)
    swapped = swap_all([gate_up] if quad else [])
    swapped, first_own = order(swapped, first_own)
    first_other = order(swap_core(first_own))
    attended, log_total = [None, None], [None, None]
    attended[0], log_total[0] = attention_forward(
        place, first_queries, first_own, first_other, row_codes[0], column_segments[0]
    )
    if quad:
        gate_weight, up_weight = fill_in(gate_weight, up_weight, (0,), [gate_up], swapped)
    attended[0], log_total[0], gate_weight, up_weight, near_in = order(
        attended[0], log_total[0], gate_weight, up_weight, near_in
    )
    far_in = far_halves(near_in)
    swapped = swap_all(near_in)
    second_own, swapped, far_in = order(second_own, swapped, far_in)
    second_other = swap_core(second_own)
    if quad:
        out_weight = lax.all_gather(after(w_output, attended[0]), "seq", axis=0, tiled=True)
    else:
        out_weight = lax.dynamic_slice_in_dim(
            lax.all_gather(w_output, ("dp", "seq"), axis=0, tiled=True), head * width, width
        )
    numbers = (1, 2, 3) if quad else (0,)
    near_swapped = swapped
    second_other = order(second_other)
    swapped = swap_all(far_in)
    attended[1], log_total[1] = attention_forward(
        place, second_queries, second_own, second_other, row_codes[1], column_segments[1]
    )
    attended, log_total, out_weight, swapped = order(attended, log_total, out_weight, swapped)
    in_halves = list(zip(far_in, swapped))
    queries = [first_queries, second_queries]
    own_keys, other_keys = [first_own, second_own], [first_other, second_other]

    def activation(gate_in, up_in):
        return jax.nn.gelu(gate_in, approximate=True) * up_in

    step = span // 2
    chunks = [slice(0, step), slice(step, 2 * step)]
    grad_output = cotangent[0].astype(f32)

    def into_feedforward(part, kept, near, far):
        attn_out = scatter_quad_end(kept, near, far)
        residual = inputs[part] + normed(attn_out, post_attention)
        return attn_out, residual, normed(residual, pre_feedforward).astype(bf16)

    sent_a = order(quad_terms([attended], out_weight, chunks[0], False, True))
    near_a = scatter_quad_near(sent_a)
    kept_a = quad_terms([attended], out_weight, chunks[0], False, False)
    near_a, kept_a = order(near_a, kept_a)
    far_a = scatter_quad_far(kept_a, near_a)
    sent_b = quad_terms([attended], out_weight, chunks[1], False, True)
    far_a, sent_b = order(far_a, sent_b)
    near_b = scatter_quad_near(sent_b)
    attn_out_a, residual_a, mid_a = order(into_feedforward(chunks[0], kept_a, near_a, far_a))
    mid_rows_a = gather_line(mid_a).reshape(line * step, model)
    kept_b = quad_terms([attended], out_weight, chunks[1], False, False)
    near_b, kept_b = order(near_b, kept_b)
    far_b = order(scatter_quad_far(kept_b, near_b))
    attn_out_b, residual_b, mid_b = order(into_feedforward(chunks[1], kept_b, near_b, far_b))
    mid_rows_b = gather_line(mid_b).reshape(line * step, model)
    own_down = after(w_down, far_b[0])
    near_down = near_blocks(own_down)
    gate_weight, up_weight = fill_in(
        gate_weight, up_weight, numbers, near_in, near_swapped, in_halves
    )
    mid_rows_a, gate_weight, up_weight = order(mid_rows_a, gate_weight, up_weight)
    gate_weight = gate_weight.reshape(model, ff_part)
    up_weight = up_weight.reshape(model, ff_part)
    gate_a = matmul(mid_rows_a, gate_weight)
    gate_a, mid_rows_a, near_down = order(gate_a, mid_rows_a, near_down)
    far_down = far_blocks(near_down)
    down_blocks = ([own_down] if quad else []) + list(near_down)
    swapped = swap_all(down_blocks)
    up_a = matmul(mid_rows_a, up_weight)
    hidden_a, far_down, swapped = order(activation(gate_a, up_a).astype(bf16), far_down, swapped)
    down_weight = fill_down(down_weight, range(3), down_blocks, swapped)
    swapped = swap_all(far_down)
    down_weight, swapped = order(down_weight, swapped)
    down_weight = fill_down(down_weight, (3,), far_down, swapped)
    down_weight = down_weight.reshape(ff_part, model)

    def feedforward_end(hidden):
        return matmul(hidden, down_weight).astype(bf16).reshape(line, step, model)

    def output_of(part, residual, down_out):
        down_out = down_out.astype(f32)
        normed_down, down_back = jax.vjp(normed, down_out, post_feedforward)
        grad_down, gain_part = down_back(grad_output[part])
        return residual + normed_down, grad_down.astype(bf16), gain_part

    def feedforward_back(down_rows, gate_value, up_value):
        grad_hidden = matmul_t(down_rows, down_weight)
        _, act_back = jax.vjp(activation, gate_value, up_value)
        grad_gate, grad_up = act_back(grad_hidden)
        grad_gate, grad_up = grad_gate.astype(bf16), grad_up.astype(bf16)
        mid_part = matmul_t(grad_gate, gate_weight) + matmul_t(grad_up, up_weight)
        return grad_gate, grad_up, mid_part.astype(bf16).reshape(line, step, model)

    def attention_grad(part, residual, attn_out, grad_mid):
        _, mid_back = jax.vjp(normed, residual, pre_feedforward)
        grad_residual, grad_pre = mid_back(grad_mid.astype(f32))
        grad_residual = grad_output[part] + grad_residual
        _, attn_back = jax.vjp(normed, attn_out, post_attention)
        grad_attn, grad_post = attn_back(grad_residual)
        return grad_residual, grad_attn.astype(bf16), grad_pre, grad_post

    down_a = scatter_line(order(feedforward_end(hidden_a)))
    mid_rows_b = order(mid_rows_b)
    gate_b, up_b = matmul(mid_rows_b, gate_weight), matmul(mid_rows_b, up_weight)
    hidden_b = activation(gate_b, up_b).astype(bf16)
    down_b = order(feedforward_end(hidden_b))
    down_b = scatter_line(down_b)
    down_a = order(down_a)
    result_a, grad_down_a, post_ff_a = order(output_of(chunks[0], residual_a, down_a))
    down_rows_a = gather_line(grad_down_a).reshape(line * step, model)
    column_codes = [codes[pair][..., None] for pair in (0, 1)]
    lane_segments = jnp.broadcast_to(
        own_segments[:, :, None, None, :], (2, 2, 8, GROUP, span)
    ).reshape(2, 2, 8, GROUP * span)
    lane_segments = [lane_segments[0], lane_segments[1]]
    down_b, column_codes, lane_segments = order(down_b, column_codes, lane_segments)
    result_b, grad_down_b, post_ff_b = order(output_of(chunks[1], residual_b, down_b))
    down_rows_b = gather_line(grad_down_b).reshape(line * step, model)
    down_rows_a = order(down_rows_a)
    grad_gate_a, grad_up_a, mid_part = order(feedforward_back(down_rows_a, gate_a, up_a))
    grad_mid_a = scatter_line(mid_part)
    down_rows_b = order(down_rows_b)
    grad_gate_b, grad_up_b, mid_part = order(feedforward_back(down_rows_b, gate_b, up_b))
    grad_mid_b = scatter_line(mid_part)
    result = jnp.concatenate([result_a, result_b], axis=0)

    def halves(lefts, rights, inner):
        if inner % 8 == 0:
            return weight_halves(place, lefts, rights, inner)
        term = sum(inner_t(left, right) for left, right in zip(lefts, rights))
        term = term.astype(bf16).reshape(-1, 2, inner, rights[0].shape[1])
        return pick(term, 1, core), pick(term, 1, 1 - core)

    def from_cores(own, moved, inner, plan, *shapes):
        own, moved = own.reshape(dp, inner, -1), moved.reshape(dp, inner, -1)
        if not quad:
            return own + moved
        shapes = [tuple(shape) + (own.shape[-1],) for shape in shapes]
        return combine_quad(place, own, moved, shapes, plan)

    def quad_plan(inner):
        low, high = slice(0, inner // 2), slice(inner // 2, inner)
        plan = [
            [(2, None, slice(0, inner))],
            [(0, 0, low), (4, None, high)],
            [(1, 0, high), (3, None, low)],
            [(0, 1, low), (1, 1, high)],
        ]
        half = inner // 2
        return plan, (2, half), (2, half), (inner,), (half,), (half,)

    def combine(own, moved, inner):
        parts = from_cores(own, moved, inner, *quad_plan(inner))
        return (parts[:2], parts[2:]) if quad else (parts, ())

    def near_sums(sent):
        return scatter_quad_near(sent) if quad else ()

    def far_terms(kept, near):
        return (add_second(kept[1], near[0]), add_second(kept[2], near[1])) if quad else ()

    def far_sums(terms):
        return (across(terms[0], 2), across(terms[1], 1)) if quad else ()

    def line_parts(*terms):
        if quad:
            return to_line(place, [(kept[0], near, far) for _, kept, near, far in terms], line)
        totals = [
            lax.psum_scatter(sent, "dp", scatter_dimension=0).reshape(line, rows, ff_part)
            for sent, _, _, _ in terms
        ]
        totals = jnp.stack(totals, axis=1)
        return [pick(totals, 0, (line_at + k) % line) for k in range(line)]

    mid_rows, hiddens, down_rows = (mid_rows_a, mid_rows_b), (hidden_a, hidden_b), (
        down_rows_a, down_rows_b
    )
    grad_gates, grad_ups = (grad_gate_a, grad_gate_b), (grad_up_a, grad_up_b)
    gate_own, gate_other = halves(mid_rows, grad_gates, rows)
    grad_mid_a, gate_own, gate_other = order(grad_mid_a, gate_own, gate_other)
    gate_other = swap_core(gate_other)
    grad_residual_a, grad_attn, pre_ff_a, post_attn_a = attention_grad(
        chunks[0], residual_a, attn_out_a, grad_mid_a
    )
    grad_residual_a, grad_attn, pre_ff_a, post_attn_a, gate_other = order(
        grad_residual_a, grad_attn, pre_ff_a, post_attn_a, gate_other
    )
    near_a = gather_quad_near(grad_attn)
    gate_sent, gate_kept, near_a, mid_rows, grad_ups = order(
        *combine(gate_own, gate_other, per_device), near_a, mid_rows, grad_ups
    )
    gate_near = near_sums(gate_sent)
    up_own, up_other = halves(mid_rows, grad_ups, rows)
    up_own, up_other, gate_near, grad_mid_b = order(up_own, up_other, gate_near, grad_mid_b)
    up_other = swap_core(up_other)
    gate_far = far_terms(gate_kept, gate_near)
    attn_grads, gate_far, up_other, up_own = order(
        attention_grad(chunks[1], residual_b, attn_out_b, grad_mid_b), gate_far, up_other, up_own
    )
    quad_a = [grad_attn, *near_a]
    grad_residual_b, grad_attn, pre_ff_b, post_attn_b = attn_grads
    near_b = gather_quad_near(grad_attn)
    gate_far = far_sums(gate_far)
    up_sent, up_kept = combine(up_own, up_other, per_device)
    near_b, up_sent, up_kept, near_a = order(near_b, up_sent, up_kept, near_a)
    far_b = gather_quad_far_parts(*near_b)
    far_a = gather_quad_far_parts(*near_a)
    grad_residual = jnp.concatenate([grad_residual_a, grad_residual_b], axis=0)

    def attention_rows(blocks_a, blocks_b):
        return jnp.concatenate(
            [block for pair in zip(blocks_a, blocks_b) for block in pair], axis=0
        )

    def attended_grad(attn_rows):
        return matmul_t(attn_rows, out_weight).astype(bf16).reshape(2, span, width)

    def attend_back(pair, grad_attended):
        return attention_backward(
            place, queries[pair], grad_attended, attended[pair], own_keys[pair], other_keys[pair],
            column_codes[pair], log_total[pair], lane_segments[pair],
        )

    def gains_over_dp(terms):
        terms = jnp.stack(terms, axis=1)
        if not quad:
            return lax.psum_scatter(terms, ("dp", "seq"), scatter_dimension=0, tiled=True)
        terms = terms.reshape(dp, line, 2, -1)
        return [pick(terms, 0, head)] + [across(pick(terms, 0, head ^ k), k) for k in (1, 2, 3)]

    def gains_over_seq(terms):
        if not quad:
            return terms
        terms = sum(terms)
        terms = pick(terms, 1, core) + swap_core(pick(terms, 1, 1 - core))
        return jnp.sum(exchange_line(terms, line_at), axis=0).reshape(rows, -1)

    first_attn = attention_rows(quad_a[:2], [grad_attn, near_b[0]])
    grad_attended, gate_far, far_a = order(attended_grad(first_attn), gate_far, far_a)
    gate_line = order(line_parts((gate_sent, gate_kept, gate_near, gate_far)))
    gate_line = exchange_line_parts(gate_line)
    first_grads, own_grad, other_grad, far_b, gate_line, up_sent = order(
        *attend_back(0, grad_attended), far_b, gate_line, up_sent
    )
    up_near = near_sums(up_sent)
    swapped = swap_core(other_grad)
    swapped, far_b, far_a = order(swapped, far_b, far_a)
    first_key_grads, far_b, far_a = order(own_grad + swapped, far_b, far_a)
    first_key_grads = scatter_line(first_key_grads)
    second_attn = attention_rows(
        [quad_a[2], jnp.concatenate(far_a, axis=0)], [near_b[1], jnp.concatenate(far_b, axis=0)]
    )
    grad_attended = attended_grad(second_attn)
    second_grads, own_grad, other_grad, up_near = order(*attend_back(1, grad_attended), up_near)
    swapped = swap_core(other_grad)
    up_far = far_terms(up_kept, up_near)
    swapped, up_far = order(swapped, up_far)
    second_key_grads, first_key_grads, hiddens, down_rows = order(
        own_grad + swapped, first_key_grads, hiddens, down_rows
    )
    second_key_grads = scatter_line(second_key_grads)

    up_far = far_sums(up_far)
    down_own, down_other = halves(hiddens, down_rows, ff_rows)
    output_term = inner_t(attended[0].reshape(2 * span, width), first_attn)
    output_term += inner_t(attended[1].reshape(2 * span, width), second_attn)
    output_term = output_term.astype(bf16)
    up_line = line_parts((up_sent, up_kept, up_near, up_far))
    second_key_grads, down_own, down_other, output_term, up_line = order(
        second_key_grads, down_own, down_other, output_term, up_line
    )

    grads = [(first_grads, second_grads), (first_key_grads, second_key_grads)]
    sent, grads = order(quad_terms(grads, in_weight, slice(0, span), True, True), grads)
    near = scatter_quad_near(sent)
    kept = quad_terms(grads, in_weight, slice(0, span), True, False)
    if quad:
        output_shard = lax.psum_scatter(output_term, "seq", scatter_dimension=0, tiled=True)
    else:
        spread = jnp.zeros((KEY_VALUE_HEADS, width, model), bf16).at[head].set(output_term)
        output_shard = lax.psum_scatter(
            spread.reshape(KEY_VALUE_HEADS * width, model),
            ("dp", "seq"),
            scatter_dimension=0,
            tiled=True,
        )
    up_line = exchange_line_parts(up_line)
    down_other = swap_core(down_other)
    if quad:
        flat = [[x.reshape(2 * span, width) for x in pair] for pair in grads]
        in_term = input_terms(normed_rows, flat, dp, seq)
        down_sent, down_kept = combine(down_own, down_other, ff_rows)
        near, kept, in_term, down_sent, down_kept, up_line = order(
            near, kept, in_term, down_sent, down_kept, up_line
        )
        far = scatter_quad_far(kept, near)
        in_part = lax.psum_scatter(
            in_term.reshape(model, 2 * width), "seq", scatter_dimension=0, tiled=True
        )
        far, down_sent = order(far, down_sent)
        down_near = scatter_quad_near(down_sent)
    else:
        in_term = sum(
            inner_t(left, jnp.concatenate(right, axis=2).reshape(2 * span, 2 * width))
            for left, right in zip(normed_rows, zip(*grads))
        )
        near, in_term = order(near, in_term.astype(bf16))
        far = order(scatter_quad_far(kept, near))
        down_mine, _ = combine(down_own, down_other, ff_rows)
        down_shard = lax.psum_scatter(down_mine, "dp", scatter_dimension=0).astype(f32)
    grad_in = scatter_quad_end(kept, near, far)
    _, in_back = jax.vjp(normed, inputs, pre_attention)
    grad_inputs, grad_pre_attn = in_back(grad_in)
    grad_pre_attn, grad_inputs = order(grad_pre_attn, grad_inputs)
    gains = gains_over_dp(
        [grad_pre_attn, post_attn_a + post_attn_b, pre_ff_a + pre_ff_b, post_ff_a + post_ff_b]
    )
    tokens_grad = grad_residual + grad_inputs
    if quad:
        gains, down_near = order(gains, down_near)
        down_far = scatter_quad_far(down_kept, down_near)
        in_part = order(in_part)
        part_shard = exchange_quad(in_part.reshape(dp, rows, 2 * width), head)
        part_shard, down_far = order(part_shard, down_far)
        down_shard = scatter_quad_end(down_kept, down_near, down_far)
    gains = gains_over_seq(gains)
    gate_shard, up_shard = (join_columns(place, x, 0, dp) for x in (gate_line, up_line))
    if not quad:
        spread = jnp.zeros((KEY_VALUE_HEADS, model, 2 * width), bf16).at[head].set(in_term)
        part_shard = lax.psum_scatter(spread, ("dp", "seq"), scatter_dimension=1, tiled=True)
    part_shard = part_shard.astype(f32).transpose(1, 0, 2)
    query_shard = part_shard[..., :width].reshape(rows, KEY_VALUE_HEADS * width)
    key_shard = part_shard[..., width : width + HEAD_DIM].reshape(rows, KEY_VALUE_HEADS * HEAD_DIM)
    value_shard = part_shard[..., width + HEAD_DIM :].reshape(rows, KEY_VALUE_HEADS * HEAD_DIM)
    return (
        result[None],
        tokens_grad[None],
        query_shard,
        key_shard,
        value_shard,
        output_shard.astype(f32),
        gate_shard,
        up_shard,
        down_shard,
        gains[:, 0],
        gains[:, 1],
        gains[:, 2],
        gains[:, 3],
    )


def solution(mesh):
    tokens, weights, whole_copy = P("dp", "seq", None), P(("dp", "seq"), None), P()
    gains = P(("dp", "seq"))
    return jax.shard_map(
        body,
        mesh=mesh,
        in_specs=(tokens,) + (whole_copy,) * 4 + (weights,) * 7 + (whole_copy,) * 2 + (tokens,),
        out_specs=(tokens,) * 2 + (weights,) * 7 + (gains,) * 4,
        check_vma=False,
    )
```

```python
import functools
import math

import jax
import jax.numpy as jnp
from jax import lax
from jax.experimental import pallas as pl
from jax.experimental.pallas import tpu as pltpu
from jax.sharding import PartitionSpec as P

KEY_VALUE_HEADS = 4
HEAD_DIM = 256
GROUP = 2
WINDOW = 4096

epsilon = 1e-06
softcap = 50.0
score_scale = HEAD_DIM ** (-0.5) / softcap
log2_scale = softcap * 1.4426950408889634
VMEM_LIMIT = 56 * 1024 * 1024
ANYWHERE = pl.BlockSpec(memory_space=pl.ANY)


def normed(values, gain_vec):
    inv_rms = lax.rsqrt(jnp.mean(values * values, axis=-1, keepdims=True) + epsilon)
    return values * inv_rms * gain_vec


def matmul(a, b):
    return jnp.dot(a, b, preferred_element_type=jnp.float32)


def matmul_t(a, b):
    return lax.dot_general(a, b, (((1,), (1,)), ((), ())), preferred_element_type=jnp.float32)


def inner_t(a, b):
    return lax.dot_general(a, b, (((0,), (0,)), ((), ())), preferred_element_type=jnp.float32)


def across(x, bits):
    return lax.ppermute(x, "dp", [(i, i ^ bits) for i in range(lax.axis_size("dp"))])


def swap_core(x):
    return lax.ppermute(x, "seq", [(i, i ^ 1) for i in range(lax.axis_size("seq"))])


def line_groups():
    count = lax.axis_size("seq")
    return [list(range(core, count, 2)) for core in (0, 1)]


def gather_line(x):
    return lax.all_gather(x, "seq", axis=0, axis_index_groups=line_groups())


def line_route(line, distance):
    return [
        (2 * i + core, 2 * ((i + distance) % line) + core) for i in range(line) for core in (0, 1)
    ]


def exchange_line_parts(parts):
    line = len(parts)
    return [parts[0]] + [lax.ppermute(parts[k], "seq", line_route(line, k)) for k in range(1, line)]


def exchange_line(x, place):
    line = x.shape[0]
    parts = exchange_line_parts([pick(x, 0, (place + k) % line) for k in range(line)])
    for k in range(1, line):
        x = put(x, parts[k], (place + line - k) % line)
    return x


def scatter_line(x):
    return lax.psum_scatter(x, "seq", scatter_dimension=0, axis_index_groups=line_groups())


def scatter_line_steps(x, place):
    line = x.shape[0]
    right = left = None
    for step in range(1, line):
        going = pick(x, 0, jnp.clip(line - step + place, 0, line - 1))
        coming = pick(x, 0, jnp.clip(step - line + place, 0, line - 1))
        right = going if right is None else going + right
        left = coming if left is None else coming + left
        right_route = [(2 * i + c, 2 * i + 2 + c) for i in range(step) for c in (0, 1)]
        left_route = [
            (2 * (line - 1 - i) + c, 2 * (line - 2 - i) + c) for i in range(step) for c in (0, 1)
        ]
        right = lax.ppermute(right, "seq", right_route)
        left = lax.ppermute(left, "seq", left_route)
    f32 = jnp.float32
    return pick(x, 0, place).astype(f32) + right.astype(f32) + left.astype(f32)


def gather_quad_near(x):
    return across(x, 1), across(x, 2)


def gather_quad_far_parts(one, two):
    half = one.shape[0] // 2
    return across(two[:half], 1), across(one[half:], 2)


def gather_quad_far(one, two):
    return jnp.concatenate(gather_quad_far_parts(one, two), axis=0)


def gather_quad(x):
    one, two = gather_quad_near(x)
    return [x, one, two, gather_quad_far(one, two)]


def scatter_quad_near(sent):
    return across(sent[0], 1), across(sent[1], 2)


def scatter_quad_far(kept, near):
    return across(kept[1] + near[0][1], 2), across(kept[2] + near[1][1], 1)


def scatter_quad_end(kept, near, far):
    half = kept[0].shape[0] // 2
    f32 = jnp.float32
    low = kept[0][:half].astype(f32) + near[0][0].astype(f32) + far[0].astype(f32)
    high = kept[0][half:].astype(f32) + near[1][0].astype(f32) + far[1].astype(f32)
    return jnp.concatenate([low, high], axis=0)


def flip_order(x, bits):
    pairs = x.reshape((2, 2) + x.shape[1:])
    pairs = jnp.where(bits % 2 == 1, pairs[:, ::-1], pairs)
    pairs = jnp.where(bits // 2 == 1, pairs[::-1], pairs)
    return pairs.reshape(x.shape)


def exchange_quad(x, place):
    parts = flip_order(x, place)
    return exchange_quad_end([parts[0]] + [across(parts[k], k) for k in (1, 2, 3)], place)


def exchange_quad_end(parts, place):
    return flip_order(jnp.stack(parts), place)


def pick(x, axis, index):
    return lax.dynamic_index_in_dim(x, index, axis, keepdims=False)


def put(x, part, *index):
    for _ in index:
        part = part[None]
    return lax.dynamic_update_slice(x, part, index + (0,) * (x.ndim - len(index)))


def after(x, *others):
    def kernel(x_ref, *rest):
        rest[-1][...] = x_ref[...]

    return pl.pallas_call(
        kernel,
        in_specs=[pl.BlockSpec(memory_space=pltpu.VMEM)] + [ANYWHERE] * len(others),
        out_specs=pl.BlockSpec(memory_space=pltpu.VMEM),
        out_shape=jax.ShapeDtypeStruct(x.shape, x.dtype),
    )(x, *others)


def empty(shape, dtype):
    return pl.pallas_call(
        lambda out_ref: None, out_specs=ANYWHERE, out_shape=jax.ShapeDtypeStruct(shape, dtype)
    )()


class Order:
    def __init__(self):
        self.token = jnp.zeros((8, 128), jnp.float32)

    def __call__(self, *trees):
        leaves, tree = jax.tree.flatten(trees)
        held = pl.pallas_call(
            lambda *refs: None,
            in_specs=[ANYWHERE] * (1 + len(leaves)),
            out_specs=[ANYWHERE] * (1 + len(leaves)),
            out_shape=[jax.ShapeDtypeStruct(x.shape, x.dtype) for x in [self.token, *leaves]],
            input_output_aliases={i: i for i in range(1 + len(leaves))},
        )(self.token, *leaves)
        self.token = held[0]
        out = jax.tree.unflatten(tree, held[1:])
        return out[0] if len(trees) == 1 else out


FREE = pl.CostEstimate(flops=0, bytes_accessed=0, transcendentals=0)


def cost(us):
    return pl.CostEstimate(flops=0, bytes_accessed=int(us * 3.5e6), transcendentals=0)


def deposit(place, targets, sources, moves):
    count = len(targets)

    def kernel(place_ref, *refs):
        source_refs = refs[count : count + len(sources)]
        target_refs, sems = refs[count + len(sources) : -1], refs[-1]
        copies = []
        for n, (source, source_at, target, target_at) in enumerate(moves):
            source_ref, target_ref = source_refs[source], target_refs[target]
            if source_at is not None:
                source_ref = source_ref.at[source_at(place_ref)]
            copies.append(
                pltpu.make_async_copy(source_ref, target_ref.at[target_at(place_ref)], sems.at[n])
            )
            copies[-1].start()
        for copy in copies:
            copy.wait()

    return pl.pallas_call(
        kernel,
        in_specs=[pl.BlockSpec(memory_space=pltpu.SMEM)]
        + [ANYWHERE] * count
        + [pl.BlockSpec(memory_space=pltpu.VMEM)] * len(sources),
        out_specs=[ANYWHERE] * count,
        out_shape=[jax.ShapeDtypeStruct(x.shape, x.dtype) for x in targets],
        scratch_shapes=[pltpu.SemaphoreType.DMA((len(moves),))],
        input_output_aliases={1 + i: i for i in range(count)},
        compiler_params=pltpu.CompilerParams(vmem_limit_bytes=VMEM_LIMIT),
        cost_estimate=FREE,
    )(place, *targets, *sources)


LINE_AT, CORE_AT, HALF_AT, HEAD_AT = range(4)


def pack_heads(place, query, key, value):
    rows, width = query.shape[0], GROUP * HEAD_DIM

    def kernel(place_ref, query_ref, key_ref, value_ref, *out_refs):
        for k, out_ref in enumerate(out_refs):
            head = place_ref[HEAD_AT] ^ k
            first = pl.multiple_of(head * width, width)
            out_ref[:, :width] = query_ref[:, pl.ds(first, width)]
            first = pl.multiple_of(head * HEAD_DIM, HEAD_DIM)
            out_ref[:, width : width + HEAD_DIM] = key_ref[:, pl.ds(first, HEAD_DIM)]
            out_ref[:, width + HEAD_DIM :] = value_ref[:, pl.ds(first, HEAD_DIM)]

    return pl.pallas_call(
        kernel,
        in_specs=[pl.BlockSpec(memory_space=pltpu.SMEM)]
        + [pl.BlockSpec(memory_space=pltpu.VMEM)] * 3,
        out_shape=[jax.ShapeDtypeStruct((rows, 2 * width), query.dtype)] * KEY_VALUE_HEADS,
        compiler_params=pltpu.CompilerParams(vmem_limit_bytes=VMEM_LIMIT),
        cost_estimate=FREE,
    )(place, query, key, value)


def order_heads(place, parts):
    def kernel(place_ref, *refs):
        for k in range(KEY_VALUE_HEADS):
            refs[-1][place_ref[HEAD_AT] ^ k] = refs[k][...]

    return pl.pallas_call(
        kernel,
        in_specs=[pl.BlockSpec(memory_space=pltpu.SMEM)]
        + [pl.BlockSpec(memory_space=pltpu.VMEM)] * KEY_VALUE_HEADS,
        out_shape=jax.ShapeDtypeStruct((KEY_VALUE_HEADS,) + parts[0].shape, parts[0].dtype),
        compiler_params=pltpu.CompilerParams(vmem_limit_bytes=VMEM_LIMIT),
        cost_estimate=FREE,
    )(place, *parts)


def weight_halves(place, lefts, rights, inner):
    rows, model = lefts[0].shape
    columns = rights[0].shape[1]
    block, strip = math.gcd(model, 1152), math.gcd(columns, 256)
    groups = block // (2 * inner)

    def kernel(place_ref, left_a, left_b, right_a, right_b, own_ref, other_ref, turned):
        turned[:, :rows] = left_a[...].T
        turned[:, rows:] = left_b[...].T
        core_here = place_ref[CORE_AT]

        def body(n, carry):
            at = pl.ds(pl.multiple_of(n * strip, strip), strip)
            term = matmul(turned[:, :rows], right_a[:, at])
            term = (term + matmul(turned[:, rows:], right_b[:, at])).astype(jnp.bfloat16)
            term = term.reshape(groups, 2, inner, strip)
            own_ref[:, :, at] = jnp.where(core_here == 0, term[:, 0], term[:, 1])
            other_ref[:, :, at] = jnp.where(core_here == 0, term[:, 1], term[:, 0])
            return carry

        lax.fori_loop(0, columns // strip, body, 0)

    half = pl.BlockSpec((groups, inner, columns), lambda i: (i, 0, 0))
    shape = jax.ShapeDtypeStruct((model // (2 * inner), inner, columns), jnp.bfloat16)
    left_spec = pl.BlockSpec((rows, block), lambda i: (0, i))
    right_spec = pl.BlockSpec((rows, columns), lambda i: (0, 0))
    return pl.pallas_call(
        kernel,
        grid=(model // block,),
        in_specs=[pl.BlockSpec(memory_space=pltpu.SMEM)] + [left_spec] * 2 + [right_spec] * 2,
        out_specs=[half, half],
        out_shape=[shape, shape],
        scratch_shapes=[pltpu.VMEM((block, 2 * rows), jnp.bfloat16)],
        compiler_params=pltpu.CompilerParams(vmem_limit_bytes=VMEM_LIMIT),
        cost_estimate=FREE,
    )(place, *lefts, *rights)


def quad_terms(lefts, weight, part, turned, sent):
    first, count = part.start, part.stop - part.start
    half = count // 2
    model = weight.shape[0] if turned else weight.shape[1]
    if sent:
        plan = [(1, 0, half, 0, 0), (3, 0, half, 0, 1), (2, half, half, 1, 0), (3, half, half, 1, 1)]
        shapes = [(2, half, model), (2, half, model)]
    else:
        plan = [(0, 0, count, 0, None), (2, 0, half, 1, None), (1, half, half, 2, None)]
        shapes = [(count, model), (half, model), (half, model)]
    widths = [pair[0].shape[2] for pair in lefts]

    def kernel(*refs):
        weight_ref, scratch = refs[2 * len(lefts)], refs[-1]
        out_refs = refs[2 * len(lefts) + 1 : -1]
        row = 0
        for k, start, size, _, _ in plan:
            column = 0
            for n, width in enumerate(widths):
                ref = refs[2 * n + k // 2]
                scratch[row : row + size, column : column + width] = ref[
                    k % 2, first + start : first + start + size, :
                ]
                column += width
            row += size
        product = matmul_t if turned else matmul
        term = product(scratch[...], weight_ref[...]).astype(jnp.bfloat16)
        row = 0
        for _, _, size, out, at in plan:
            if at is None:
                out_refs[out][...] = term[row : row + size]
            else:
                out_refs[out][at] = term[row : row + size]
            row += size

    return pl.pallas_call(
        kernel,
        out_shape=[jax.ShapeDtypeStruct(shape, jnp.bfloat16) for shape in shapes],
        scratch_shapes=[pltpu.VMEM((2 * count, sum(widths)), jnp.bfloat16)],
        compiler_params=pltpu.CompilerParams(vmem_limit_bytes=VMEM_LIMIT),
        cost_estimate=cost(1),
    )(*[x for pair in lefts for x in pair], weight)


def split_columns(place, gate, up, dp, line):
    rows, ff = gate.shape
    rest = ff // (dp * line)

    def kernel(place_ref, gate_ref, up_ref, *out_refs):
        def fill(j, k):
            for which, ref in enumerate((gate_ref, up_ref)):
                for i in range(dp):
                    first = (i * line + j) * rest
                    out_refs[k][which, :, i * rest : (i + 1) * rest] = ref[:, first : first + rest]

        for j in range(line):
            for k in range(line):
                there = lax.rem(place_ref[LINE_AT] + k, line) == j
                pl.when(there)(functools.partial(fill, j, k))

    return pl.pallas_call(
        kernel,
        in_specs=[pl.BlockSpec(memory_space=pltpu.SMEM)]
        + [pl.BlockSpec(memory_space=pltpu.VMEM)] * 2,
        out_shape=[jax.ShapeDtypeStruct((2, rows, dp * rest), gate.dtype)] * line,
        compiler_params=pltpu.CompilerParams(vmem_limit_bytes=VMEM_LIMIT),
        cost_estimate=FREE,
    )(place, gate, up)


def join_columns(place, parts, which, dp):
    line = len(parts)
    _, rows, part = parts[0].shape
    rest = part // dp

    def kernel(place_ref, *refs):
        def fill(j, k):
            for i in range(dp):
                first = (i * line + j) * rest
                refs[line][:, first : first + rest] = refs[k][
                    0, :, i * rest : (i + 1) * rest
                ].astype(jnp.float32)

        for j in range(line):
            for k in range(line):
                there = lax.rem(place_ref[LINE_AT] + line - k, line) == j
                pl.when(there)(functools.partial(fill, j, k))

    return pl.pallas_call(
        kernel,
        grid_spec=pltpu.PrefetchScalarGridSpec(
            num_scalar_prefetch=1,
            grid=(1,),
            in_specs=[pl.BlockSpec((1, rows, part), lambda i, place: (which, 0, 0))] * line,
            out_specs=pl.BlockSpec((rows, line * part), lambda i, place: (0, 0)),
        ),
        out_shape=jax.ShapeDtypeStruct((rows, line * part), jnp.float32),
        compiler_params=pltpu.CompilerParams(vmem_limit_bytes=VMEM_LIMIT),
        cost_estimate=FREE,
    )(place, *parts)


def add_second(term, pair):
    rows, columns = term.shape

    def kernel(term_ref, pair_ref, out_ref):
        total = term_ref[...].astype(jnp.float32) + pair_ref[0].astype(jnp.float32)
        out_ref[...] = total.astype(jnp.bfloat16)

    return pl.pallas_call(
        kernel,
        grid=(1,),
        in_specs=[
            pl.BlockSpec((rows, columns), lambda i: (0, 0)),
            pl.BlockSpec((1, rows, columns), lambda i: (1, 0, 0)),
        ],
        out_specs=pl.BlockSpec((rows, columns), lambda i: (0, 0)),
        out_shape=jax.ShapeDtypeStruct((rows, columns), jnp.bfloat16),
        compiler_params=pltpu.CompilerParams(vmem_limit_bytes=VMEM_LIMIT),
        cost_estimate=FREE,
    )(term, pair)


def combine_quad(place, own, other, shapes, plan):
    _, inner, columns = own.shape
    spec = pl.BlockSpec((1, inner, columns), lambda k, place: (place[HEAD_AT] ^ k, 0, 0))

    def kernel(place_ref, own_ref, other_ref, *out_refs):
        total = own_ref[0].astype(jnp.float32) + other_ref[0].astype(jnp.float32)
        total = total.astype(jnp.bfloat16)

        def write(k):
            for out, at, taken in plan[k]:
                if at is None:
                    out_refs[out][...] = total[taken]
                else:
                    out_refs[out][at] = total[taken]

        for k in range(4):
            pl.when(pl.program_id(0) == k)(functools.partial(write, k))

    return pl.pallas_call(
        kernel,
        grid_spec=pltpu.PrefetchScalarGridSpec(
            num_scalar_prefetch=1,
            grid=(4,),
            in_specs=[spec, spec],
            out_specs=[
                pl.BlockSpec(shape, lambda k, place, rank=len(shape): (0,) * rank)
                for shape in shapes
            ],
        ),
        out_shape=[jax.ShapeDtypeStruct(shape, jnp.bfloat16) for shape in shapes],
        compiler_params=pltpu.CompilerParams(vmem_limit_bytes=VMEM_LIMIT),
        cost_estimate=FREE,
    )(place, own, other)


def to_line(place, terms, line):
    count, columns = terms[0][0].shape
    rows, half = count // line, count // 2
    alone = pl.BlockSpec((count, columns), lambda i, place: (0, 0))
    first = pl.BlockSpec((1, half, columns), lambda i, place: (0, 0, 0))
    last = pl.BlockSpec((half, columns), lambda i, place: (0, 0))
    part = pl.BlockSpec((len(terms), rows, columns), lambda i, place: (0, 0, 0))

    def kernel(place_ref, *refs):
        def fill(j, k):
            start, high = j * rows % half, j * rows // half
            for which in range(len(terms)):
                kept_ref, *near_refs = refs[5 * which : 5 * which + 3]
                far_ref = refs[5 * which + 3 + high]
                total = kept_ref[j * rows : (j + 1) * rows].astype(jnp.float32)
                total = total + near_refs[high][0, start : start + rows].astype(jnp.float32)
                total = total + far_ref[start : start + rows].astype(jnp.float32)
                refs[5 * len(terms) + k][which] = total.astype(jnp.bfloat16)

        for j in range(line):
            for k in range(line):
                there = lax.rem(place_ref[LINE_AT] + k, line) == j
                pl.when(there)(functools.partial(fill, j, k))

    return pl.pallas_call(
        kernel,
        grid_spec=pltpu.PrefetchScalarGridSpec(
            num_scalar_prefetch=1,
            grid=(1,),
            in_specs=[alone, first, first, last, last] * len(terms),
            out_specs=[part] * line,
        ),
        out_shape=[jax.ShapeDtypeStruct((len(terms), rows, columns), jnp.bfloat16)] * line,
        compiler_params=pltpu.CompilerParams(vmem_limit_bytes=VMEM_LIMIT),
        cost_estimate=FREE,
    )(place, *[x for kept, near, far in terms for x in (kept, *near, *far)])


def input_terms(lefts, rights, dp, seq):
    count, model = lefts[0].shape
    widths = [pair[0].shape[1] for pair in rights]
    rest = model // (dp * seq)
    block, strip = model // 2, math.gcd(*widths, 256)
    halves = dp // 2

    def kernel(left_a, left_b, *refs):
        out_ref, turned = refs[-2:]
        turned[:, :count] = left_a[...].T
        turned[:, count:] = left_b[...].T
        column = 0
        for n, width in enumerate(widths):

            def body(m, carry, right_a=refs[2 * n], right_b=refs[2 * n + 1], column=column):
                at = pl.ds(pl.multiple_of(m * strip, strip), strip)
                to = pl.ds(pl.multiple_of(column + m * strip, strip), strip)
                term = matmul(turned[:, :count], right_a[:, at])
                term = (term + matmul(turned[:, count:], right_b[:, at])).astype(jnp.bfloat16)
                term = term.reshape(halves, seq, rest, strip)
                for i in range(halves):
                    out_ref[:, i, :, to] = term[i]
                return carry

            lax.fori_loop(0, width // strip, body, 0)
            column += width

    left_spec = pl.BlockSpec((count, block), lambda i: (0, i))
    columns = sum(widths)
    return pl.pallas_call(
        kernel,
        grid=(2,),
        in_specs=[left_spec] * 2
        + [pl.BlockSpec((count, width), lambda i: (0, 0)) for width in widths for _ in (0, 1)],
        out_specs=pl.BlockSpec((seq, halves, rest, columns), lambda i: (0, i, 0, 0)),
        out_shape=jax.ShapeDtypeStruct((seq, dp, rest, columns), jnp.bfloat16),
        scratch_shapes=[pltpu.VMEM((block, 2 * count), jnp.bfloat16)],
        compiler_params=pltpu.CompilerParams(vmem_limit_bytes=VMEM_LIMIT),
        cost_estimate=cost(6),
    )(*lefts, *[x for pair in rights for x in pair])


def tile_facts(place, span, tile):
    line = pl.num_programs(0) // 2
    row_tokens = line * 2 * span
    half = tile // line
    key_first = half * row_tokens + (tile % line) * 2 * span
    query_first = [(place[2] ^ j) * row_tokens + (2 * place[0] + place[1]) * span for j in (0, 1)]
    return key_first, query_first


def reach(key_first, keys, query_first, queries):
    key_last, query_last = key_first + keys - 1, query_first + queries - 1
    live = (key_first <= query_last) & (query_first - key_last < WINDOW)
    plain = (key_last < query_first) & (query_last - key_first < WINDOW)
    return live & plain, live & jnp.logical_not(plain)


def row_of(columns, scale):
    ones = jnp.full((8, columns.shape[1]), scale, jnp.float32)
    return lax.dot_general(
        ones,
        columns,
        (((1,), (1,)), ((), ())),
        precision=lax.Precision.HIGHEST,
        preferred_element_type=jnp.float32,
    )


def forward_kernel(
    place, query_ref, own_ref, other_ref, code_ref, segment_ref, out_ref, log_ref, acc, total
):
    tile = pl.program_id(0)
    span = query_ref.shape[1]
    key_first, query_first = tile_facts(place, span, tile)

    @pl.when(tile == 0)
    def _():
        acc[...] = jnp.zeros_like(acc)
        total[...] = jnp.zeros_like(total)

    def step(j, masked):
        keys = jnp.concatenate([own_ref[0, 0, :, :HEAD_DIM], other_ref[0, 0, :, :HEAD_DIM]], axis=0)
        values = jnp.concatenate(
            [own_ref[0, 0, :, HEAD_DIM:], other_ref[0, 0, :, HEAD_DIM:]], axis=0
        )
        allowed = code_ref[0, 0] == segment_ref[j]
        if masked:
            lane = lax.broadcasted_iota(jnp.int32, (1, 2 * span), 1)
            key_pos = key_first + lane + jnp.where(lane < span, place[1], -place[1]) * span
            query_pos = query_first[j] + lax.broadcasted_iota(jnp.int32, (span, 1), 0)
            back = query_pos - key_pos
            allowed = (allowed & (back > 0) & (back < WINDOW)) | (back == 0)
        for h in range(GROUP):
            query = query_ref[j, :, h * HEAD_DIM : (h + 1) * HEAD_DIM]
            scores = matmul_t(query, keys)
            weights = jnp.exp2(log2_scale * jnp.tanh(scores * score_scale))
            weights = jnp.where(allowed, weights, 0.0)
            total[j, h] += jnp.sum(weights, axis=-1, keepdims=True)
            acc[j, h] += matmul(weights.astype(jnp.bfloat16), values)

    for j in (0, 1):
        plain, masked = reach(key_first, 2 * span, query_first[j], span)
        pl.when(plain)(functools.partial(step, j, False))
        pl.when(masked)(functools.partial(step, j, True))

    @pl.when(tile == pl.num_programs(0) - 1)
    def _():
        for j in (0, 1):
            for h in range(GROUP):
                out_ref[j, :, h * HEAD_DIM : (h + 1) * HEAD_DIM] = (
                    acc[j, h] / total[j, h]
                ).astype(jnp.bfloat16)
                column = jnp.broadcast_to(jnp.log2(total[j, h]), (span, 128))
                log_ref[j, :, h * span : (h + 1) * span] = row_of(column, 1.0 / 128)


def backward_kernel(
    place, query_ref, grad_ref, attended_ref, own_ref, other_ref, code_ref, log_ref, segment_ref,
    query_grad_ref, own_grad_ref, other_grad_ref,
    queries, grads, query_acc, key_acc, value_acc, delta,
):
    tile = pl.program_id(0)
    span = query_ref.shape[1]
    key_first, query_first = tile_facts(place, span, tile)

    @pl.when(tile == 0)
    def _():
        query_acc[...] = jnp.zeros_like(query_acc)
        for j in (0, 1):
            for h in range(GROUP):
                rows, columns = pl.ds(h * span, span), slice(h * HEAD_DIM, (h + 1) * HEAD_DIM)
                queries[j, rows, :] = query_ref[j, :, columns]
                grads[j, rows, :] = grad_ref[j, :, columns]
                products = grad_ref[j, :, columns].astype(jnp.float32) * attended_ref[
                    j, :, columns
                ].astype(jnp.float32)
                delta[j, :, h * span : (h + 1) * span] = row_of(products, 1.0)

    def step(j, side, side_first, keys, values, masked):
        allowed = code_ref[0, 0, pl.ds(side * span, span), :] == segment_ref[j, 0:1, :]
        if masked:
            lane = lax.broadcasted_iota(jnp.int32, (1, GROUP * span), 1)
            query_pos = query_first[j] + jnp.where(lane < span, lane, lane - span)
            key_pos = side_first + lax.broadcasted_iota(jnp.int32, (span, 1), 0)
            back = query_pos - key_pos
            allowed = (allowed & (back > 0) & (back < WINDOW)) | (back == 0)
        squashed = jnp.tanh(matmul_t(keys, queries[j]) * score_scale)
        weights = jnp.exp2(log2_scale * squashed - log_ref[j, 0:1, :])
        weights = jnp.where(allowed, weights, 0.0)
        grad_weights = matmul_t(values, grads[j])
        value_acc[side] += matmul(weights.astype(jnp.bfloat16), grads[j])
        grad_scores = weights * (grad_weights - delta[j, 0:1, :]) * (1.0 - squashed * squashed)
        grad_scores = grad_scores.astype(jnp.bfloat16)
        key_acc[side] += matmul(grad_scores, queries[j])
        query_acc[j] += inner_t(grad_scores, keys)

    key_acc[...] = jnp.zeros_like(key_acc)
    value_acc[...] = jnp.zeros_like(value_acc)
    scale = HEAD_DIM ** (-0.5)
    for side, key_ref, grad_out in ((0, own_ref, own_grad_ref), (1, other_ref, other_grad_ref)):
        side_first = key_first + (place[1] if side == 0 else 1 - place[1]) * span

        def on_side(j, masked, side=side, side_first=side_first, key_ref=key_ref):
            keys, values = key_ref[0, 0, :, :HEAD_DIM], key_ref[0, 0, :, HEAD_DIM:]
            step(j, side, side_first, keys, values, masked)

        for j in (0, 1):
            plain, masked = reach(side_first, span, query_first[j], span)
            pl.when(plain)(functools.partial(on_side, j, False))
            pl.when(masked)(functools.partial(on_side, j, True))
        grad_out[0, 0, :, :HEAD_DIM] = (key_acc[side] * scale).astype(jnp.bfloat16)
        grad_out[0, 0, :, HEAD_DIM:] = value_acc[side].astype(jnp.bfloat16)

    @pl.when(tile == pl.num_programs(0) - 1)
    def _():
        for j in (0, 1):
            for h in range(GROUP):
                query_grad_ref[j, :, h * HEAD_DIM : (h + 1) * HEAD_DIM] = (
                    query_acc[j, h * span : (h + 1) * span, :] * scale
                ).astype(jnp.bfloat16)


def whole(*shape):
    return pl.BlockSpec(shape, lambda tile, place: (0,) * len(shape))


def tile_specs(line, span):
    def key_place(tile, place):
        return (tile % line, (tile // line) ^ place[2], 0, 0)

    def code_place(tile, place):
        return ((tile // line) ^ place[2], tile % line, 0, 0)

    return pl.BlockSpec((1, 1, span, 2 * HEAD_DIM), key_place), code_place


def attention_forward(place, queries, own, other, codes, segments):
    line, _, span, width = own.shape
    tile_spec, code_place = tile_specs(line, span)
    return pl.pallas_call(
        forward_kernel,
        grid_spec=pltpu.PrefetchScalarGridSpec(
            num_scalar_prefetch=1,
            grid=(2 * line,),
            in_specs=[
                whole(2, span, width),
                tile_spec,
                tile_spec,
                pl.BlockSpec((1, 1, 1, 2 * span), code_place),
                whole(2, span, 1),
            ],
            out_specs=[whole(2, span, width), whole(2, 8, GROUP * span)],
            scratch_shapes=[
                pltpu.VMEM((2, GROUP, span, HEAD_DIM), jnp.float32),
                pltpu.VMEM((2, GROUP, span, 1), jnp.float32),
            ],
        ),
        out_shape=[
            jax.ShapeDtypeStruct((2, span, width), jnp.bfloat16),
            jax.ShapeDtypeStruct((2, 8, GROUP * span), jnp.float32),
        ],
        compiler_params=pltpu.CompilerParams(vmem_limit_bytes=VMEM_LIMIT),
        cost_estimate=cost(6),
    )(place, queries, own, other, codes, segments)


def attention_backward(place, queries, grads, attended, own, other, codes, logs, segments):
    line, _, span, width = own.shape
    tile_spec, code_place = tile_specs(line, span)
    return pl.pallas_call(
        backward_kernel,
        grid_spec=pltpu.PrefetchScalarGridSpec(
            num_scalar_prefetch=1,
            grid=(2 * line,),
            in_specs=[
                whole(2, span, width),
                whole(2, span, width),
                whole(2, span, width),
                tile_spec,
                tile_spec,
                pl.BlockSpec((1, 1, 2 * span, 1), code_place),
                whole(2, 8, GROUP * span),
                whole(2, 8, GROUP * span),
            ],
            out_specs=[whole(2, span, width), tile_spec, tile_spec],
            scratch_shapes=[
                pltpu.VMEM((2, GROUP * span, HEAD_DIM), jnp.bfloat16),
                pltpu.VMEM((2, GROUP * span, HEAD_DIM), jnp.bfloat16),
                pltpu.VMEM((2, GROUP * span, HEAD_DIM), jnp.float32),
                pltpu.VMEM((2, span, HEAD_DIM), jnp.float32),
                pltpu.VMEM((2, span, HEAD_DIM), jnp.float32),
                pltpu.VMEM((2, 8, GROUP * span), jnp.float32),
            ],
        ),
        out_shape=[
            jax.ShapeDtypeStruct((2, span, width), jnp.bfloat16),
            jax.ShapeDtypeStruct(own.shape, jnp.bfloat16),
            jax.ShapeDtypeStruct(own.shape, jnp.bfloat16),
        ],
        compiler_params=pltpu.CompilerParams(vmem_limit_bytes=VMEM_LIMIT),
        cost_estimate=FREE,
    )(place, queries, grads, attended, own, other, codes, logs, segments)


def body(
    tokens, pre_attention, post_attention, pre_feedforward, post_feedforward, w_query, key_weight,
    value_weight, w_output, w_gate, w_up, w_down, document_index, token_padding_mask, cotangent,
):
    bf16, f32 = jnp.bfloat16, jnp.float32
    dp, seq = lax.axis_size("dp"), lax.axis_size("seq")
    line, groups = seq // 2, dp // KEY_VALUE_HEADS
    dp_at, seq_at = lax.axis_index("dp"), lax.axis_index("seq")
    line_at, core = seq_at // 2, seq_at % 2
    head = dp_at % KEY_VALUE_HEADS
    half_bit = dp_at % 2
    _, span, model = tokens.shape
    rows = w_query.shape[0]
    ff = w_gate.shape[1]
    ff_rows = w_down.shape[0]
    ff_part = ff // line
    width = GROUP * HEAD_DIM

    order = Order()

    def attention_codes():
        sequence = dp_at // 2

        def by_pair(table):
            both = jnp.stack([pick(table, 0, sequence), pick(table, 0, sequence ^ 1)])
            both = both.reshape(2, 2, line, 2, span)
            both = jnp.where(half_bit == 1, both[:, ::-1], both)
            return jnp.where(core == 1, both[:, :, :, ::-1], both)

        segments = by_pair(document_index)
        codes = jnp.where(by_pair(token_padding_mask) == 1, segments, -1)
        return codes.reshape(2, 2, line, 2 * span), pick(segments[:, :, :, 0], 2, line_at)

    quad = groups == 1
    place = jnp.stack([line_at, core, half_bit, head]).astype(jnp.int32)
    inputs = tokens[0].astype(f32)
    flipped = pack_heads(place, w_query, key_weight, value_weight)
    split = split_columns(place, w_gate, w_up, dp, line)
    if quad:
        flipped = order(flipped)
        mixed = [flipped[0]] + [across(flipped[k], k) for k in (1, 2, 3)]
        normed_in = normed(inputs, pre_attention).astype(bf16)
        mixed, normed_in, split, place = order(order_heads(place, mixed), normed_in, split, place)
        near_normed = gather_quad_near(normed_in)
        in_weight = lax.all_gather(mixed, "seq", axis=1).reshape(model, 2 * width)
    else:
        normed_in = normed(inputs, pre_attention).astype(bf16)
        near_normed = gather_quad_near(normed_in)
        blocks = lax.all_gather(order_heads(place, flipped), ("dp", "seq"), axis=1, tiled=True)
        in_weight = pick(blocks, 0, head)

    per_device = line * rows
    split = exchange_line_parts(split)

    def ordered_split(split):
        (whole,) = deposit(
            place,
            [empty((2, line, rows, ff_part), bf16)],
            split,
            [
                (k, lambda at, w=w: (w,), 0, lambda at, w=w, k=k: (w, (at[LINE_AT] + line - k) % line))
                for k in range(line)
                for w in (0, 1)
            ],
        )
        return whole.reshape(2 * per_device, ff_part)

    def near_blocks(own):
        return gather_quad_near(own) if quad else (lax.all_gather(own, "dp", axis=0),)

    def far_blocks(near):
        return (gather_quad_far(*near),) if quad else ()

    def far_halves(near):
        return gather_quad_far_parts(*near) if quad else ()

    def swap_all(blocks):
        return [swap_core(block) for block in blocks]

    down_weight = empty((dp, 2, ff_rows, model), bf16)
    gate_weight = empty((dp, line, 2, rows, ff_part), bf16)
    up_weight = empty((dp, line, 2, rows, ff_part), bf16)

    def sides(numbers, mine, swapped):
        for k, *blocks in zip(numbers, mine, swapped):
            for other, block in enumerate(blocks):
                yield k, other, block

    def at_dp(at, k):
        return at[HEAD_AT] ^ k if quad else pl.ds(0, dp)

    def fill_down(weight, numbers, mine, swapped):
        sources, moves = [], []
        for k, other, block in sides(numbers, mine, swapped):
            target = lambda at, k=k, other=other: (at_dp(at, k), at[CORE_AT] ^ other)
            moves.append((len(sources), None, 0, target))
            sources.append(block)
        return deposit(place, [weight], sources, moves)[0] if sources else weight

    def fill_in(gate, up, numbers, mine, swapped, halves=()):
        sources, moves = [], []
        for which, pair in enumerate(halves):
            for other, block in enumerate(pair):
                target = lambda at, other=other: (at_dp(at, 3), slice(None), at[CORE_AT] ^ other)
                moves.append((len(sources), None, which, target))
                sources.append(block.reshape(line, rows, ff_part))
        for k, other, block in sides(numbers, mine, swapped):
            for which in (0, 1):
                source = lambda at, which=which: (slice(None),) * (not quad) + (which,)
                target = lambda at, k=k, other=other: (
                    at_dp(at, k), slice(None), at[CORE_AT] ^ other
                )
                moves.append((len(sources), source, which, target))
            lead = () if quad else (dp,)
            sources.append(block.reshape(lead + (2, line, rows, ff_part)))
        return deposit(place, [gate, up], sources, moves) if sources else (gate, up)

    def project(pair_rows):
        projected = matmul(pair_rows, in_weight).astype(bf16).reshape(2, span, 2 * width)
        return projected[..., :width], projected[..., width:]

    codes, own_segments = attention_codes()
    row_codes = codes[:, :, :, None, :]
    column_segments = own_segments[..., None]
    first_rows = jnp.concatenate([normed_in, near_normed[0]], axis=0)
    halfway = span // 2
    far_normed = near_normed[1][:halfway], near_normed[0][halfway:]
    near_two, far_normed, first_rows, in_weight, split, row_codes, column_segments = order(
        near_normed[1], far_normed, first_rows, in_weight, split, row_codes, column_segments
    )
    far_normed = across(far_normed[0], 1), across(far_normed[1], 2)
    first_queries, first_keys = project(first_rows)
    first_queries, first_keys, first_rows = order(first_queries, first_keys, first_rows)
    first_own = gather_line(first_keys)
    gate_up = ordered_split(split)
    far_normed, gate_up = order(far_normed, gate_up)
    second_rows = jnp.concatenate([near_two, *far_normed], axis=0)
    second_queries, second_keys = project(second_rows)
    second_queries, second_keys, second_rows, gate_up = order(
        second_queries, second_keys, second_rows, gate_up
    )
    second_own = gather_line(second_keys)
    normed_rows = [first_rows, second_rows]
    near_in = near_blocks(gate_up)
    swapped = swap_all([gate_up] if quad else [])
    swapped, first_own = order(swapped, first_own)
    first_other = order(swap_core(first_own))
    attended, log_total = [None, None], [None, None]
    attended[0], log_total[0] = attention_forward(
        place, first_queries, first_own, first_other, row_codes[0], column_segments[0]
    )
    if quad:
        gate_weight, up_weight = fill_in(gate_weight, up_weight, (0,), [gate_up], swapped)
    attended[0], log_total[0], gate_weight, up_weight, near_in = order(
        attended[0], log_total[0], gate_weight, up_weight, near_in
    )
    far_in = far_halves(near_in)
    swapped = swap_all(near_in)
    second_own, swapped, far_in = order(second_own, swapped, far_in)
    second_other = swap_core(second_own)
    if quad:
        out_weight = lax.all_gather(after(w_output, attended[0]), "seq", axis=0, tiled=True)
    else:
        out_weight = lax.dynamic_slice_in_dim(
            lax.all_gather(w_output, ("dp", "seq"), axis=0, tiled=True), head * width, width
        )
    numbers = (1, 2, 3) if quad else (0,)
    near_swapped = swapped
    second_other = order(second_other)
    swapped = swap_all(far_in)
    attended[1], log_total[1] = attention_forward(
        place, second_queries, second_own, second_other, row_codes[1], column_segments[1]
    )
    attended, log_total, out_weight, swapped = order(attended, log_total, out_weight, swapped)
    in_halves = list(zip(far_in, swapped))
    queries = [first_queries, second_queries]
    own_keys, other_keys = [first_own, second_own], [first_other, second_other]

    def activation(gate_in, up_in):
        return jax.nn.gelu(gate_in, approximate=True) * up_in

    step = span // 2
    chunks = [slice(0, step), slice(step, 2 * step)]
    grad_output = cotangent[0].astype(f32)

    def into_feedforward(part, kept, near, far):
        attn_out = scatter_quad_end(kept, near, far)
        residual = inputs[part] + normed(attn_out, post_attention)
        return attn_out, residual, normed(residual, pre_feedforward).astype(bf16)

    sent_a = order(quad_terms([attended], out_weight, chunks[0], False, True))
    near_a = scatter_quad_near(sent_a)
    kept_a = quad_terms([attended], out_weight, chunks[0], False, False)
    near_a, kept_a = order(near_a, kept_a)
    far_a = scatter_quad_far(kept_a, near_a)
    sent_b = quad_terms([attended], out_weight, chunks[1], False, True)
    far_a, sent_b = order(far_a, sent_b)
    near_b = scatter_quad_near(sent_b)
    attn_out_a, residual_a, mid_a = order(into_feedforward(chunks[0], kept_a, near_a, far_a))
    mid_rows_a = gather_line(mid_a).reshape(line * step, model)
    kept_b = quad_terms([attended], out_weight, chunks[1], False, False)
    near_b, kept_b = order(near_b, kept_b)
    far_b = order(scatter_quad_far(kept_b, near_b))
    attn_out_b, residual_b, mid_b = order(into_feedforward(chunks[1], kept_b, near_b, far_b))
    mid_rows_b = gather_line(mid_b).reshape(line * step, model)
    own_down = after(w_down, far_b[0])
    near_down = near_blocks(own_down)
    gate_weight, up_weight = fill_in(
        gate_weight, up_weight, numbers, near_in, near_swapped, in_halves
    )
    mid_rows_a, gate_weight, up_weight = order(mid_rows_a, gate_weight, up_weight)
    gate_weight = gate_weight.reshape(model, ff_part)
    up_weight = up_weight.reshape(model, ff_part)
    gate_a = matmul(mid_rows_a, gate_weight)
    gate_a, mid_rows_a, near_down = order(gate_a, mid_rows_a, near_down)
    far_down = far_blocks(near_down)
    down_blocks = ([own_down] if quad else []) + list(near_down)
    swapped = swap_all(down_blocks)
    up_a = matmul(mid_rows_a, up_weight)
    hidden_a, far_down, swapped = order(activation(gate_a, up_a).astype(bf16), far_down, swapped)
    down_weight = fill_down(down_weight, range(3), down_blocks, swapped)
    swapped = swap_all(far_down)
    down_weight, swapped = order(down_weight, swapped)
    down_weight = fill_down(down_weight, (3,), far_down, swapped)
    down_weight = down_weight.reshape(ff_part, model)

    def feedforward_end(hidden):
        return matmul(hidden, down_weight).astype(bf16).reshape(line, step, model)

    def output_of(part, residual, down_out):
        down_out = down_out.astype(f32)
        normed_down, down_back = jax.vjp(normed, down_out, post_feedforward)
        grad_down, gain_part = down_back(grad_output[part])
        return residual + normed_down, grad_down.astype(bf16), gain_part

    def feedforward_back(down_rows, gate_value, up_value):
        grad_hidden = matmul_t(down_rows, down_weight)
        _, act_back = jax.vjp(activation, gate_value, up_value)
        grad_gate, grad_up = act_back(grad_hidden)
        grad_gate, grad_up = grad_gate.astype(bf16), grad_up.astype(bf16)
        mid_part = matmul_t(grad_gate, gate_weight) + matmul_t(grad_up, up_weight)
        return grad_gate, grad_up, mid_part.astype(bf16).reshape(line, step, model)

    def attention_grad(part, residual, attn_out, grad_mid):
        _, mid_back = jax.vjp(normed, residual, pre_feedforward)
        grad_residual, grad_pre = mid_back(grad_mid.astype(f32))
        grad_residual = grad_output[part] + grad_residual
        _, attn_back = jax.vjp(normed, attn_out, post_attention)
        grad_attn, grad_post = attn_back(grad_residual)
        return grad_residual, grad_attn.astype(bf16), grad_pre, grad_post

    down_a = scatter_line(order(feedforward_end(hidden_a)))
    mid_rows_b = order(mid_rows_b)
    gate_b, up_b = matmul(mid_rows_b, gate_weight), matmul(mid_rows_b, up_weight)
    hidden_b = activation(gate_b, up_b).astype(bf16)
    down_b = order(feedforward_end(hidden_b))
    down_b = scatter_line(down_b)
    down_a = order(down_a)
    result_a, grad_down_a, post_ff_a = order(output_of(chunks[0], residual_a, down_a))
    down_rows_a = gather_line(grad_down_a).reshape(line * step, model)
    column_codes = [codes[pair][..., None] for pair in (0, 1)]
    lane_segments = jnp.broadcast_to(
        own_segments[:, :, None, None, :], (2, 2, 8, GROUP, span)
    ).reshape(2, 2, 8, GROUP * span)
    lane_segments = [lane_segments[0], lane_segments[1]]
    down_b, column_codes, lane_segments = order(down_b, column_codes, lane_segments)
    result_b, grad_down_b, post_ff_b = order(output_of(chunks[1], residual_b, down_b))
    down_rows_b = gather_line(grad_down_b).reshape(line * step, model)
    down_rows_a = order(down_rows_a)
    grad_gate_a, grad_up_a, mid_part = order(feedforward_back(down_rows_a, gate_a, up_a))
    grad_mid_a = scatter_line(mid_part)
    down_rows_b = order(down_rows_b)
    grad_gate_b, grad_up_b, mid_part = order(feedforward_back(down_rows_b, gate_b, up_b))
    grad_mid_b = scatter_line(mid_part)
    result = jnp.concatenate([result_a, result_b], axis=0)

    def halves(lefts, rights, inner):
        if inner % 8 == 0:
            return weight_halves(place, lefts, rights, inner)
        term = sum(inner_t(left, right) for left, right in zip(lefts, rights))
        term = term.astype(bf16).reshape(-1, 2, inner, rights[0].shape[1])
        return pick(term, 1, core), pick(term, 1, 1 - core)

    def from_cores(own, moved, inner, plan, *shapes):
        own, moved = own.reshape(dp, inner, -1), moved.reshape(dp, inner, -1)
        if not quad:
            return own + moved
        shapes = [tuple(shape) + (own.shape[-1],) for shape in shapes]
        return combine_quad(place, own, moved, shapes, plan)

    def quad_plan(inner):
        low, high = slice(0, inner // 2), slice(inner // 2, inner)
        plan = [
            [(2, None, slice(0, inner))],
            [(0, 0, low), (4, None, high)],
            [(1, 0, high), (3, None, low)],
            [(0, 1, low), (1, 1, high)],
        ]
        half = inner // 2
        return plan, (2, half), (2, half), (inner,), (half,), (half,)

    def combine(own, moved, inner):
        parts = from_cores(own, moved, inner, *quad_plan(inner))
        return (parts[:2], parts[2:]) if quad else (parts, ())

    def near_sums(sent):
        return scatter_quad_near(sent) if quad else ()

    def far_terms(kept, near):
        return (add_second(kept[1], near[0]), add_second(kept[2], near[1])) if quad else ()

    def far_sums(terms):
        return (across(terms[0], 2), across(terms[1], 1)) if quad else ()

    def line_parts(*terms):
        if quad:
            return to_line(place, [(kept[0], near, far) for _, kept, near, far in terms], line)
        totals = [
            lax.psum_scatter(sent, "dp", scatter_dimension=0).reshape(line, rows, ff_part)
            for sent, _, _, _ in terms
        ]
        totals = jnp.stack(totals, axis=1)
        return [pick(totals, 0, (line_at + k) % line) for k in range(line)]

    mid_rows, hiddens, down_rows = (mid_rows_a, mid_rows_b), (hidden_a, hidden_b), (
        down_rows_a, down_rows_b
    )
    grad_gates, grad_ups = (grad_gate_a, grad_gate_b), (grad_up_a, grad_up_b)
    gate_own, gate_other = halves(mid_rows, grad_gates, rows)
    grad_mid_a, gate_own, gate_other = order(grad_mid_a, gate_own, gate_other)
    gate_other = swap_core(gate_other)
    grad_residual_a, grad_attn, pre_ff_a, post_attn_a = attention_grad(
        chunks[0], residual_a, attn_out_a, grad_mid_a
    )
    grad_residual_a, grad_attn, pre_ff_a, post_attn_a, gate_other = order(
        grad_residual_a, grad_attn, pre_ff_a, post_attn_a, gate_other
    )
    near_a = gather_quad_near(grad_attn)
    gate_sent, gate_kept, near_a, mid_rows, grad_ups = order(
        *combine(gate_own, gate_other, per_device), near_a, mid_rows, grad_ups
    )
    gate_near = near_sums(gate_sent)
    up_own, up_other = halves(mid_rows, grad_ups, rows)
    up_own, up_other, gate_near, grad_mid_b = order(up_own, up_other, gate_near, grad_mid_b)
    up_other = swap_core(up_other)
    gate_far = far_terms(gate_kept, gate_near)
    attn_grads, gate_far, up_other, up_own = order(
        attention_grad(chunks[1], residual_b, attn_out_b, grad_mid_b), gate_far, up_other, up_own
    )
    quad_a = [grad_attn, *near_a]
    grad_residual_b, grad_attn, pre_ff_b, post_attn_b = attn_grads
    near_b = gather_quad_near(grad_attn)
    gate_far = far_sums(gate_far)
    up_sent, up_kept = combine(up_own, up_other, per_device)
    near_b, up_sent, up_kept, near_a = order(near_b, up_sent, up_kept, near_a)
    far_b = gather_quad_far_parts(*near_b)
    far_a = gather_quad_far_parts(*near_a)
    grad_residual = jnp.concatenate([grad_residual_a, grad_residual_b], axis=0)

    def attention_rows(blocks_a, blocks_b):
        return jnp.concatenate(
            [block for pair in zip(blocks_a, blocks_b) for block in pair], axis=0
        )

    def attended_grad(attn_rows):
        return matmul_t(attn_rows, out_weight).astype(bf16).reshape(2, span, width)

    def attend_back(pair, grad_attended):
        return attention_backward(
            place, queries[pair], grad_attended, attended[pair], own_keys[pair], other_keys[pair],
            column_codes[pair], log_total[pair], lane_segments[pair],
        )

    def gains_over_dp(terms):
        terms = jnp.stack(terms, axis=1)
        if not quad:
            return lax.psum_scatter(terms, ("dp", "seq"), scatter_dimension=0, tiled=True)
        terms = terms.reshape(dp, line, 2, -1)
        return [pick(terms, 0, head)] + [across(pick(terms, 0, head ^ k), k) for k in (1, 2, 3)]

    def gains_over_seq(terms):
        if not quad:
            return terms
        terms = sum(terms)
        terms = pick(terms, 1, core) + swap_core(pick(terms, 1, 1 - core))
        return jnp.sum(exchange_line(terms, line_at), axis=0).reshape(rows, -1)

    first_attn = attention_rows(quad_a[:2], [grad_attn, near_b[0]])
    grad_attended, gate_far, far_a = order(attended_grad(first_attn), gate_far, far_a)
    gate_line = order(line_parts((gate_sent, gate_kept, gate_near, gate_far)))
    gate_line = exchange_line_parts(gate_line)
    first_grads, own_grad, other_grad, far_b, gate_line, up_sent = order(
        *attend_back(0, grad_attended), far_b, gate_line, up_sent
    )
    up_near = near_sums(up_sent)
    swapped = swap_core(other_grad)
    swapped, far_b, far_a = order(swapped, far_b, far_a)
    first_key_grads, far_b, far_a = order(own_grad + swapped, far_b, far_a)
    first_key_grads = scatter_line(first_key_grads)
    second_attn = attention_rows(
        [quad_a[2], jnp.concatenate(far_a, axis=0)], [near_b[1], jnp.concatenate(far_b, axis=0)]
    )
    grad_attended = attended_grad(second_attn)
    second_grads, own_grad, other_grad, up_near = order(*attend_back(1, grad_attended), up_near)
    swapped = swap_core(other_grad)
    up_far = far_terms(up_kept, up_near)
    swapped, up_far = order(swapped, up_far)
    second_key_grads, first_key_grads, hiddens, down_rows = order(
        own_grad + swapped, first_key_grads, hiddens, down_rows
    )
    second_key_grads = scatter_line(second_key_grads)

    up_far = far_sums(up_far)
    down_own, down_other = halves(hiddens, down_rows, ff_rows)
    output_term = inner_t(attended[0].reshape(2 * span, width), first_attn)
    output_term += inner_t(attended[1].reshape(2 * span, width), second_attn)
    output_term = output_term.astype(bf16)
    up_line = line_parts((up_sent, up_kept, up_near, up_far))
    second_key_grads, down_own, down_other, output_term, up_line = order(
        second_key_grads, down_own, down_other, output_term, up_line
    )

    grads = [(first_grads, second_grads), (first_key_grads, second_key_grads)]
    sent, grads = order(quad_terms(grads, in_weight, slice(0, span), True, True), grads)
    near = scatter_quad_near(sent)
    kept = quad_terms(grads, in_weight, slice(0, span), True, False)
    if quad:
        output_shard = lax.psum_scatter(output_term, "seq", scatter_dimension=0, tiled=True)
    else:
        spread = jnp.zeros((KEY_VALUE_HEADS, width, model), bf16).at[head].set(output_term)
        output_shard = lax.psum_scatter(
            spread.reshape(KEY_VALUE_HEADS * width, model),
            ("dp", "seq"),
            scatter_dimension=0,
            tiled=True,
        )
    up_line = exchange_line_parts(up_line)
    down_other = swap_core(down_other)
    if quad:
        flat = [[x.reshape(2 * span, width) for x in pair] for pair in grads]
        in_term = input_terms(normed_rows, flat, dp, seq)
        down_sent, down_kept = combine(down_own, down_other, ff_rows)
        near, kept, in_term, down_sent, down_kept = order(
            near, kept, in_term, down_sent, down_kept
        )
        far = scatter_quad_far(kept, near)
        in_part = lax.psum_scatter(
            in_term.reshape(model, 2 * width), "seq", scatter_dimension=0, tiled=True
        )
        far, down_sent = order(far, down_sent)
        down_near = scatter_quad_near(down_sent)
    else:
        in_term = sum(
            inner_t(left, jnp.concatenate(right, axis=2).reshape(2 * span, 2 * width))
            for left, right in zip(normed_rows, zip(*grads))
        )
        near, in_term = order(near, in_term.astype(bf16))
        far = order(scatter_quad_far(kept, near))
        down_mine, _ = combine(down_own, down_other, ff_rows)
        down_shard = lax.psum_scatter(down_mine, "dp", scatter_dimension=0).astype(f32)
    grad_in = scatter_quad_end(kept, near, far)
    _, in_back = jax.vjp(normed, inputs, pre_attention)
    grad_inputs, grad_pre_attn = in_back(grad_in)
    grad_pre_attn, grad_inputs = order(grad_pre_attn, grad_inputs)
    gains = gains_over_dp(
        [grad_pre_attn, post_attn_a + post_attn_b, pre_ff_a + pre_ff_b, post_ff_a + post_ff_b]
    )
    tokens_grad = grad_residual + grad_inputs
    if quad:
        gains, down_near = order(gains, down_near)
        down_far = scatter_quad_far(down_kept, down_near)
        in_part, up_line = order(in_part, up_line)
        part_shard = exchange_quad(in_part.reshape(dp, rows, 2 * width), head)
        part_shard, down_far = order(part_shard, down_far)
        down_shard = scatter_quad_end(down_kept, down_near, down_far)
    gains = gains_over_seq(gains)
    gate_shard, up_shard = (join_columns(place, x, 0, dp) for x in (gate_line, up_line))
    if not quad:
        spread = jnp.zeros((KEY_VALUE_HEADS, model, 2 * width), bf16).at[head].set(in_term)
        part_shard = lax.psum_scatter(spread, ("dp", "seq"), scatter_dimension=1, tiled=True)
    part_shard = part_shard.astype(f32).transpose(1, 0, 2)
    query_shard = part_shard[..., :width].reshape(rows, KEY_VALUE_HEADS * width)
    key_shard = part_shard[..., width : width + HEAD_DIM].reshape(rows, KEY_VALUE_HEADS * HEAD_DIM)
    value_shard = part_shard[..., width + HEAD_DIM :].reshape(rows, KEY_VALUE_HEADS * HEAD_DIM)
    return (
        result[None],
        tokens_grad[None],
        query_shard,
        key_shard,
        value_shard,
        output_shard.astype(f32),
        gate_shard,
        up_shard,
        down_shard,
        gains[:, 0],
        gains[:, 1],
        gains[:, 2],
        gains[:, 3],
    )


def solution(mesh):
    tokens, weights, whole_copy = P("dp", "seq", None), P(("dp", "seq"), None), P()
    gains = P(("dp", "seq"))
    return jax.shard_map(
        body,
        mesh=mesh,
        in_specs=(tokens,) + (whole_copy,) * 4 + (weights,) * 7 + (whole_copy,) * 2 + (tokens,),
        out_specs=(tokens,) * 2 + (weights,) * 7 + (gains,) * 4,
        check_vma=False,
    )
```
